128 devices in a mesh: seq: 8 (over y, core), tp: 16 (over x, z).
Axes of the slice: x: 4, y: 4, z: 4, core: 2. Of those that a mesh axis runs over, the one named last changes fastest.
Arguments:
- tokens: bfloat16 [8192, 5376], P('seq'), may hold values from -6 to 6
- pre_gain: float32 [5376], replicated, may hold values from 0.5 to 2
- w_query: bfloat16 [5376, 4096], P(None, 'tp'), may hold values from -0.078125 to 0.078125
- key_weight_matrix: bfloat16 [5376, 2048], P(None, 'tp'), may hold values from -0.078125 to 0.078125
- value_weight_matrix: bfloat16 [5376, 2048], P(None, 'tp'), may hold values from -0.078125 to 0.078125
- query_gain: float32 [128], replicated, may hold values from 0.5 to 9
- key_norm_gain: float32 [128], replicated, may hold values from 0.5 to 9
- prior_key_cache: bfloat16 [1024, 2048], P(None, 'tp'), may hold values from -6 to 6
- prior_value_cache: bfloat16 [1024, 2048], P(None, 'tp'), may hold values from -6 to 6
- w_out: bfloat16 [4096, 5376], P('tp'), may hold values from -0.09375 to 0.09375
- post_gain: float32 [5376], replicated, may hold values from 0.5 to 2
Outputs:
- updated: bfloat16 [8192, 5376], P(('seq', 'tp'))
The draws below stay inside these ranges and needn't reach their ends.
All inputs are finite; a program needn't handle non-finite values.
Results may differ from the reference program's by a relative error of at most 0.015.
The reference program's roundings to bfloat16 on the way count: a program that leaves them out, or rounds other values in their place, can miss the bound.
Values may be sent and summed in bfloat16 or wider, within the bound.
No kernel may reach another device: no remote copies, remote signals or barrier semaphores. Data moves between devices by JAX's collectives and lax.ppermute only.
A program may use at most 128 MiB of HBM per device.

```python
import math
import jax
import jax.numpy as jnp
from jax import lax

MODEL_WIDTH = 5376
HQ = 32
KEY_VALUE_HEADS = 16
HEAD_DIM = 128
WINDOW_SPAN = 1024
BLOCK_TOKENS = 8192
N_TP = 16


def gain_helper(key):
    low, high = (0.5, 2.0)
    logs = jax.random.uniform(key, (HEAD_DIM,), jnp.float32, math.log(low), math.log(high))
    return jnp.exp(logs).astype(jnp.float32)


def draw_query_gain(key, part):
    return gain_helper(jax.random.fold_in(key, 11))


def draw_key_norm_gain(key, part):
    return gain_helper(jax.random.fold_in(key, 12))


def block_scale(own_key, dims, shards, least, high):
    def one(axis_at, parts):
        steps = jax.random.uniform(jax.random.fold_in(jax.random.fold_in(own_key, 6), axis_at), (parts,), jnp.float32, least / len(shards), high / len(shards))
        return jnp.repeat(jnp.exp(steps), dims[axis_at] // parts).reshape((-1,) + (1,) * (len(dims) - axis_at - 1))

    level = one(*shards[0])
    for cut in shards[1:]:
        level = level * one(*cut)
    return level


def centred(own_key, dims, width, bound, shards=(), held_as=jnp.bfloat16):
    level = block_scale(own_key, dims, shards, -0.22, 0.18) if shards else 1.0
    entries = jax.random.normal(own_key, dims, jnp.float32) * width * level
    return jnp.minimum(jnp.maximum(entries, -bound), bound).astype(held_as)


def setup_inputs(seed: int = 0) -> dict:
    seeds = jax.random.split(jax.random.key(seed), 12)
    tokens = centred(seeds[0], (BLOCK_TOKENS, MODEL_WIDTH), 1.0, 6.0, ((0, 8),))
    pre_gain = jnp.clip(jnp.exp(jax.random.uniform(seeds[1], (MODEL_WIDTH,), jnp.float32, math.log(0.5), math.log(2.0))), 0.5, 2.0)
    w_query = centred(seeds[2], (MODEL_WIDTH, HQ * HEAD_DIM), MODEL_WIDTH ** -0.5, 0.078125, ((1, 16),))
    key_weight_matrix = centred(seeds[3], (MODEL_WIDTH, KEY_VALUE_HEADS * HEAD_DIM), MODEL_WIDTH ** -0.5, 0.078125, ((1, 16),))
    value_weight_matrix = centred(seeds[4], (MODEL_WIDTH, KEY_VALUE_HEADS * HEAD_DIM), MODEL_WIDTH ** -0.5, 0.078125, ((1, 16),))
    query_gain = draw_query_gain(jax.random.fold_in(seeds[11], 71), 0)
    key_norm_gain = draw_key_norm_gain(jax.random.fold_in(seeds[11], 71), 0)
    prior_key_cache = centred(seeds[7], (WINDOW_SPAN, KEY_VALUE_HEADS * HEAD_DIM), 1.0, 6.0, ((1, 16),))
    prior_value_cache = centred(seeds[8], (WINDOW_SPAN, KEY_VALUE_HEADS * HEAD_DIM), 1.0, 6.0, ((1, 16),))
    w_out = centred(seeds[9], (HQ * HEAD_DIM, MODEL_WIDTH), (HQ * HEAD_DIM) ** -0.5, 0.09375, ((0, 16),))
    post_gain = jnp.clip(jnp.exp(jax.random.uniform(seeds[10], (MODEL_WIDTH,), jnp.float32, math.log(0.5), math.log(2.0))), 0.5, 2.0)
    return dict(tokens=tokens, pre_gain=pre_gain, w_query=w_query, key_weight_matrix=key_weight_matrix, value_weight_matrix=value_weight_matrix, query_gain=query_gain, key_norm_gain=key_norm_gain, prior_key_cache=prior_key_cache, prior_value_cache=prior_value_cache, w_out=w_out, post_gain=post_gain)


EPSILON = 1e-06

def root_mean_norm(values, gain):
    mean_square = lax.optimization_barrier(jnp.mean(values * values, axis=-1, keepdims=True))
    return values * lax.rsqrt(mean_square + EPSILON) * gain

def rotary_embed_pairs(values, token_positions):
    half = values.shape[-1] // 2
    exponent = jnp.arange(half, dtype=jnp.float32) * (-2.0 / values.shape[-1])
    frequency = jnp.power(jnp.float32(10000.0), exponent)
    angles = token_positions.astype(jnp.float32)[:, None] * frequency[None, :]
    cosine = jnp.cos(angles)[:, None, :]
    sine = jnp.sin(angles)[:, None, :]
    first = values[..., :half]
    second = values[..., half:]
    return jnp.concatenate([first * cosine - second * sine, second * cosine + first * sine], axis=-1)

def attend_block(query_rows, key_rows, value_rows, scale):
    count = query_rows.shape[0]
    heads = query_rows.shape[1]
    kv_heads = key_rows.shape[1]
    grouped = query_rows.reshape(count, kv_heads, heads // kv_heads, -1).astype(jnp.float32)
    scores = jnp.einsum('bkgd,mkd->kgbm', grouped, key_rows.astype(jnp.float32)) * scale
    row_ids = lax.broadcasted_iota(jnp.int32, (count, key_rows.shape[0]), 0)
    col_ids = lax.broadcasted_iota(jnp.int32, (count, key_rows.shape[0]), 1)
    allowed = (col_ids > row_ids) & (col_ids <= row_ids + WINDOW_SPAN)
    scores = jnp.where(allowed, scores, -jnp.inf)
    highest = lax.optimization_barrier(jnp.max(scores, axis=-1, keepdims=True))
    weights = jnp.exp(scores - highest)
    weights = (weights / lax.optimization_barrier(jnp.sum(weights, axis=-1, keepdims=True))).astype(jnp.bfloat16)
    mixed = jnp.einsum('kgbm,mkd->bkgd', weights.astype(jnp.float32), value_rows.astype(jnp.float32))
    return mixed.astype(jnp.bfloat16).reshape(count, heads, -1)

def reference(tokens, pre_gain, w_query, key_weight_matrix, value_weight_matrix, query_gain, key_norm_gain, prior_key_cache, prior_value_cache, w_out, post_gain):
    inputs = tokens.astype(jnp.float32)
    normed = root_mean_norm(inputs, pre_gain).astype(jnp.bfloat16)
    query_raw = jnp.dot(normed, w_query, preferred_element_type=jnp.float32)
    unnormed_keys = jnp.dot(normed, key_weight_matrix, preferred_element_type=jnp.float32)
    projected_values = jnp.dot(normed, value_weight_matrix, preferred_element_type=jnp.float32)
    token_positions = WINDOW_SPAN + jnp.arange(BLOCK_TOKENS, dtype=jnp.int32)
    queries = rotary_embed_pairs(root_mean_norm(query_raw.reshape(BLOCK_TOKENS, HQ, HEAD_DIM), query_gain), token_positions).astype(jnp.bfloat16)
    block_keys = rotary_embed_pairs(root_mean_norm(unnormed_keys.reshape(BLOCK_TOKENS, KEY_VALUE_HEADS, HEAD_DIM), key_norm_gain), token_positions).astype(jnp.bfloat16)
    block_values = projected_values.astype(jnp.bfloat16).reshape(BLOCK_TOKENS, KEY_VALUE_HEADS, HEAD_DIM)
    joined_keys = jnp.concatenate([prior_key_cache.reshape(WINDOW_SPAN, KEY_VALUE_HEADS, HEAD_DIM), block_keys], axis=0)
    joined_values = jnp.concatenate([prior_value_cache.reshape(WINDOW_SPAN, KEY_VALUE_HEADS, HEAD_DIM), block_values], axis=0)
    size = min(512, BLOCK_TOKENS)
    scale = float(MODEL_WIDTH // HQ) ** (-0.5)

    def one_block(number):
        start = (number * size).astype(jnp.int32)
        query_rows = lax.dynamic_slice_in_dim(queries, start, size, 0)
        key_rows = lax.dynamic_slice_in_dim(joined_keys, start, size + WINDOW_SPAN, 0)
        value_rows = lax.dynamic_slice_in_dim(joined_values, start, size + WINDOW_SPAN, 0)
        return attend_block(query_rows, key_rows, value_rows, scale)
    blocks = lax.map(one_block, jnp.arange(BLOCK_TOKENS // size, dtype=jnp.int32))
    attended = blocks.reshape(BLOCK_TOKENS, HQ * HEAD_DIM)
    group_cols = HQ * HEAD_DIM // N_TP

    def add_group(total, group):
        begin = (group * group_cols).astype(jnp.int32)
        columns = lax.dynamic_slice_in_dim(attended, begin, group_cols, 1)
        rows = lax.dynamic_slice_in_dim(w_out, begin, group_cols, 0)
        term = jnp.dot(columns, rows, preferred_element_type=jnp.float32).astype(jnp.bfloat16)
        term = lax.optimization_barrier(term)
        return (total + term.astype(jnp.float32), None)
    summed, _ = lax.scan(add_group, jnp.zeros((BLOCK_TOKENS, MODEL_WIDTH), jnp.float32), jnp.arange(N_TP, dtype=jnp.int32))
    return (inputs + root_mean_norm(summed, post_gain)).astype(jnp.bfloat16)
```

```python
import functools

import jax
import jax.numpy as jnp
import numpy as np
from jax import lax
from jax.experimental import pallas as pl
from jax.experimental.pallas import tpu as pltpu
from jax.sharding import Mesh
from jax.sharding import PartitionSpec as P

MODEL_WIDTH = 5376
HQ = 32
HEAD = 128
WINDOW_SPAN = 1024
BLOCK_TOKENS = 8192
SHARD = 1024
EPSILON = 1e-06
LOG2E = 1.4426950408889634
SCORE_SCALE = float(MODEL_WIDTH // HQ) ** (-0.5)

F32 = jnp.float32
BF16 = jnp.bfloat16

ROWS = 256
GROUP = 16
HALF = 128


def rotary_table():
    half = HEAD // 2
    exponent = np.arange(half, dtype=np.float32) * np.float32(-2.0 / HEAD)
    frequency = np.power(np.float64(10000.0), exponent.astype(np.float64)).astype(np.float32)
    position = (WINDOW_SPAN + np.arange(BLOCK_TOKENS)).astype(np.float32)
    angle = (position[:, None] * frequency[None, :]).astype(np.float64)
    return np.concatenate([np.cos(angle), np.sin(angle)], axis=1).astype(np.float32)


def project_kernel(
    seq_ref, tok_ref, g_ref, wq_ref, wk_ref, wv_ref, qg_ref, kg_ref, tab_ref,
    q_ref, kv_ref, w_all, g_all, normed,
):
    @pl.when(pl.program_id(0) == 0)
    def _():
        w_all[:, 0:256] = wq_ref[...]
        w_all[:, 256:384] = wk_ref[...]
        w_all[:, 384:512] = wv_ref[...]
        g_all[...] = jnp.broadcast_to(g_ref[...], g_all.shape)

    blocks = MODEL_WIDTH // 128

    def norm_group(i, carry):
        rows = pl.ds(pl.multiple_of(i * GROUP, GROUP), GROUP)
        parts = [jnp.zeros((GROUP, 128), F32) for _ in range(2)]
        for b in range(blocks):
            v = tok_ref[rows, b * 128 : (b + 1) * 128].astype(F32)
            parts[b % 2] = parts[b % 2] + v * v
        mean = jnp.sum(parts[0] + parts[1], axis=-1, keepdims=True) * (1.0 / MODEL_WIDTH)
        r = lax.rsqrt(mean + EPSILON)
        for b in range(blocks):
            cols = slice(b * 128, (b + 1) * 128)
            v = tok_ref[rows, cols].astype(F32)
            normed[rows, cols] = (v * r * g_all[:, cols]).astype(BF16)
        return carry

    lax.fori_loop(0, ROWS // GROUP, norm_group, 0)
    raw = jnp.dot(normed[...], w_all[...], preferred_element_type=F32)

    table = tab_ref[...]
    swapped = pltpu.roll(table, 64, 1)
    low = lax.broadcasted_iota(jnp.int32, table.shape, 1) < 64
    cosine = jnp.where(low, table, swapped)
    sine = jnp.where(low, -swapped, table)

    def rotate(u, gain):
        mean = jnp.sum(u * u, axis=-1, keepdims=True) * (1.0 / HEAD)
        u = u * lax.rsqrt(mean + EPSILON) * gain
        return (u * cosine + pltpu.roll(u, 64, 1) * sine).astype(BF16)

    q_ref[:, 0:128] = rotate(raw[:, 0:128], qg_ref[...])
    q_ref[:, 128:256] = rotate(raw[:, 128:256], qg_ref[...])
    kv_ref[:, 0:128] = rotate(raw[:, 256:384], kg_ref[...])
    kv_ref[:, 128:256] = raw[:, 384:512].astype(BF16)


def project(seq, tokens, pre_gain, wq, wk, wv, q_gain, k_gain, table):
    whole = lambda shape: pl.BlockSpec(shape, lambda i, s: (0, 0))
    return pl.pallas_call(
        project_kernel,
        grid_spec=pltpu.PrefetchScalarGridSpec(
            num_scalar_prefetch=1,
            grid=(SHARD // ROWS,),
            in_specs=[
                pl.BlockSpec((ROWS, MODEL_WIDTH), lambda i, s: (i, 0)),
                whole((1, MODEL_WIDTH)),
                whole((MODEL_WIDTH, 256)),
                whole((MODEL_WIDTH, 128)),
                whole((MODEL_WIDTH, 128)),
                whole((1, 128)),
                whole((1, 128)),
                pl.BlockSpec((ROWS, 128), lambda i, s: (s[0] * (SHARD // ROWS) + i, 0)),
            ],
            out_specs=[
                pl.BlockSpec((ROWS, 256), lambda i, s: (i, 0)),
                pl.BlockSpec((ROWS, 256), lambda i, s: (i, 0)),
            ],
            scratch_shapes=[
                pltpu.VMEM((MODEL_WIDTH, 512), BF16),
                pltpu.VMEM((GROUP, MODEL_WIDTH), F32),
                pltpu.VMEM((ROWS, MODEL_WIDTH), BF16),
            ],
        ),
        out_shape=[
            jax.ShapeDtypeStruct((SHARD, 256), BF16),
            jax.ShapeDtypeStruct((SHARD, 256), BF16),
        ],
        compiler_params=pltpu.CompilerParams(vmem_limit_bytes=48 << 20),
        cost_estimate=pl.CostEstimate(
            flops=2 * SHARD * MODEL_WIDTH * 512, bytes_accessed=18 << 20, transcendentals=0
        ),
        name="project",
    )(
        seq, tokens, pre_gain.reshape(1, -1), wq, wk, wv,
        q_gain.reshape(1, -1), k_gain.reshape(1, -1), table,
    )


def attend_kernel(pos_ref, q_ref, kv_ref, got_ref, pk_ref, pv_ref, out_ref, keys, values):
    @pl.when(pos_ref[0] == 0)
    def _():
        keys[0:SHARD] = pk_ref[...]
        values[0:SHARD, 0:128] = pv_ref[...]

    @pl.when(pos_ref[0] != 0)
    def _():
        keys[0:SHARD] = got_ref[:, 0:128]
        values[0:SHARD, 0:128] = got_ref[:, 128:256]

    keys[SHARD:] = kv_ref[:, 0:128]
    values[SHARD:, 0:128] = kv_ref[:, 128:256]
    values[:, 128:256] = jnp.ones((2 * SHARD, 128), BF16)

    span = HALF + WINDOW_SPAN
    row = lax.broadcasted_iota(jnp.int32, (2 * HALF, HALF), 0) % HALF
    col = lax.broadcasted_iota(jnp.int32, (2 * HALF, HALF), 1)
    lowest = jnp.float32(-jnp.inf)
    for part in range(out_ref.shape[0] // HALF):
        first = pl.multiple_of(pos_ref[1 + part], HALF)
        q = q_ref[pl.ds(first, HALF), :]
        q = jnp.concatenate([q[:, 0:128], q[:, 128:256]], axis=0)
        k = keys[pl.ds(first, span), :]
        scores = lax.dot_general(q, k, (((1,), (1,)), ((), ())), preferred_element_type=F32)
        scores = jnp.concatenate(
            [
                jnp.where(col > row, scores[:, 0:HALF], lowest),
                scores[:, HALF:WINDOW_SPAN],
                jnp.where(col <= row, scores[:, WINDOW_SPAN:], lowest),
            ],
            axis=1,
        )
        top = jnp.max(scores, axis=-1, keepdims=True)
        weights = jnp.exp2((scores - top) * (SCORE_SCALE * LOG2E)).astype(BF16)
        mixed = jnp.dot(weights, values[pl.ds(first, span), :], preferred_element_type=F32)
        mixed = (mixed[:, 0:128] / mixed[:, 128:256]).astype(BF16)
        out_ref[part * HALF : (part + 1) * HALF, 0:128] = mixed[0:HALF]
        out_ref[part * HALF : (part + 1) * HALF, 128:256] = mixed[HALF:]


def attend(pos, q, kv, got, prior_k, prior_v, parts):
    vmem = pl.BlockSpec(memory_space=pltpu.VMEM)
    return pl.pallas_call(
        attend_kernel,
        in_specs=[pl.BlockSpec(memory_space=pltpu.SMEM)] + [vmem] * 5,
        out_specs=vmem,
        out_shape=jax.ShapeDtypeStruct((parts * HALF, 256), BF16),
        scratch_shapes=[
            pltpu.VMEM((2 * SHARD, 128), BF16),
            pltpu.VMEM((2 * SHARD, 256), BF16),
        ],
        compiler_params=pltpu.CompilerParams(vmem_limit_bytes=32 << 20),
        cost_estimate=pl.CostEstimate(
            flops=8 * parts * HALF * 1152 * 256, bytes_accessed=2 << 20,
            transcendentals=parts * 2 * HALF * 1152,
        ),
        name="attend",
    )(pos, q, kv, got, prior_k, prior_v)


def per_device(
    tokens, pre_gain, w_query, key_weight, value_weight, query_gain, key_gain,
    prior_key, prior_value, w_out, post_gain, table,
):
    seq = lax.axis_index("y") * 2 + lax.axis_index("c")
    tp = lax.axis_index("x") * 4 + lax.axis_index("z")
    q, kv = project(
        seq.reshape(1), tokens, pre_gain, w_query, key_weight, value_weight,
        query_gain, key_gain, table,
    )
    got = lax.ppermute(kv, ("y", "c"), [(i, i + 1) for i in range(7)])
    steps = []
    for step in range(4):
        pos = jnp.stack([seq, jnp.int32(step * 256), jnp.int32(step * 256 + 128)])
        steps.append(attend(pos, q, kv, got, prior_key, prior_value, 2))
    attended = jnp.concatenate(steps, axis=0)
    partial = jnp.dot(attended, w_out, preferred_element_type=F32)
    summed = lax.psum_scatter(
        partial.astype(BF16), ("x", "z"), scatter_dimension=0, tiled=True
    ).astype(F32)
    own = lax.dynamic_slice_in_dim(tokens, tp * 64, 64, 0).astype(F32)
    mean = jnp.mean(summed * summed, axis=-1, keepdims=True)
    return (own + summed * lax.rsqrt(mean + EPSILON) * post_gain).astype(BF16)


def solution(mesh):
    fine = Mesh(mesh.devices.reshape(4, 2, 4, 4), ("y", "c", "x", "z"))
    seq, tp = ("y", "c"), ("x", "z")
    inner = jax.shard_map(
        per_device,
        mesh=fine,
        in_specs=(
            P(seq, None), P(), P(None, tp), P(None, tp), P(None, tp), P(), P(),
            P(None, tp), P(None, tp), P(tp, None), P(), P(),
        ),
        out_specs=P(seq + tp, None),
        check_vma=False,
    )

    def run(*args):
        return inner(*args, jnp.asarray(rotary_table()))

    return run
```

```python
import functools

import jax
import jax.numpy as jnp
import numpy as np
from jax import lax
from jax.experimental import pallas as pl
from jax.experimental.pallas import tpu as pltpu
from jax.sharding import Mesh
from jax.sharding import PartitionSpec as P

MODEL_WIDTH = 5376
HQ = 32
HEAD = 128
WINDOW_SPAN = 1024
BLOCK_TOKENS = 8192
SHARD = 1024
EPSILON = 1e-06
LOG2E = 1.4426950408889634
SCORE_SCALE = float(MODEL_WIDTH // HQ) ** (-0.5)

F32 = jnp.float32
BF16 = jnp.bfloat16

ROWS = 256
GROUP = 16
HALF = 128
QUARTER = 1408
ROW_AT = 3


def rotary_table():
    half = HEAD // 2
    exponent = np.arange(half, dtype=np.float32) * np.float32(-2.0 / HEAD)
    frequency = np.power(np.float64(10000.0), exponent.astype(np.float64)).astype(np.float32)
    position = (WINDOW_SPAN + np.arange(BLOCK_TOKENS)).astype(np.float32)
    angle = (position[:, None] * frequency[None, :]).astype(np.float64)
    return np.concatenate([np.cos(angle), np.sin(angle)], axis=1).astype(np.float32)


def places():
    rows = []
    for device in range(128):
        seq, x, z = device // 16, device // 4 % 4, device % 4
        far, up, down = ((x + by) % 4 * 256 for by in (2, 1, 3))
        rows.append(
            [seq, z, seq % 2, far, far + 128, up + 128, down, up, down + 128, x * 256,
             x * 256 + 128, x * 256 + z * 64]
        )
    return np.array(rows, np.int32)


def project_kernel(
    seq_ref, tok_ref, g_ref, wq_ref, wk_ref, wv_ref, qg_ref, kg_ref, tab_ref,
    q_ref, kv_ref, w_all, g_all, normed,
):
    @pl.when(pl.program_id(0) == 0)
    def _():
        w_all[:, 0:256] = wq_ref[...]
        w_all[:, 256:384] = wk_ref[...]
        w_all[:, 384:512] = wv_ref[...]
        g_all[...] = jnp.broadcast_to(g_ref[...], g_all.shape)

    blocks = MODEL_WIDTH // 128

    def norm_group(i, carry):
        rows = pl.ds(pl.multiple_of(i * GROUP, GROUP), GROUP)
        parts = [jnp.zeros((GROUP, 128), F32) for _ in range(2)]
        for b in range(blocks):
            v = tok_ref[rows, b * 128 : (b + 1) * 128].astype(F32)
            parts[b % 2] = parts[b % 2] + v * v
        mean = jnp.sum(parts[0] + parts[1], axis=-1, keepdims=True) * (1.0 / MODEL_WIDTH)
        r = lax.rsqrt(mean + EPSILON)
        for b in range(blocks):
            cols = slice(b * 128, (b + 1) * 128)
            v = tok_ref[rows, cols].astype(F32)
            normed[rows, cols] = (v * r * g_all[:, cols]).astype(BF16)
        return carry

    lax.fori_loop(0, ROWS // GROUP, norm_group, 0)
    raw = jnp.dot(normed[...], w_all[...], preferred_element_type=F32)

    table = tab_ref[...]
    swapped = pltpu.roll(table, 64, 1)
    low = lax.broadcasted_iota(jnp.int32, table.shape, 1) < 64
    cosine = jnp.where(low, table, swapped)
    sine = jnp.where(low, -swapped, table)

    def rotate(u, gain):
        mean = jnp.sum(u * u, axis=-1, keepdims=True) * (1.0 / HEAD)
        u = u * lax.rsqrt(mean + EPSILON) * gain
        return (u * cosine + pltpu.roll(u, 64, 1) * sine).astype(BF16)

    q_ref[:, 0:128] = rotate(raw[:, 0:128], qg_ref[...])
    q_ref[:, 128:256] = rotate(raw[:, 128:256], qg_ref[...])
    kv_ref[:, 0:128] = rotate(raw[:, 256:384], kg_ref[...])
    kv_ref[:, 128:256] = raw[:, 384:512].astype(BF16)


def project(seq, tokens, pre_gain, wq, wk, wv, q_gain, k_gain, table):
    whole = lambda shape: pl.BlockSpec(shape, lambda i, s: (0, 0))
    return pl.pallas_call(
        project_kernel,
        grid_spec=pltpu.PrefetchScalarGridSpec(
            num_scalar_prefetch=1,
            grid=(SHARD // ROWS,),
            in_specs=[
                pl.BlockSpec((ROWS, MODEL_WIDTH), lambda i, s: (i, 0)),
                whole((1, MODEL_WIDTH)),
                whole((MODEL_WIDTH, 256)),
                whole((MODEL_WIDTH, 128)),
                whole((MODEL_WIDTH, 128)),
                whole((1, 128)),
                whole((1, 128)),
                pl.BlockSpec((ROWS, 128), lambda i, s: (s[0] * (SHARD // ROWS) + i, 0)),
            ],
            out_specs=[
                pl.BlockSpec((ROWS, 256), lambda i, s: (i, 0)),
                pl.BlockSpec((ROWS, 256), lambda i, s: (i, 0)),
            ],
            scratch_shapes=[
                pltpu.VMEM((MODEL_WIDTH, 512), BF16),
                pltpu.VMEM((GROUP, MODEL_WIDTH), F32),
                pltpu.VMEM((ROWS, MODEL_WIDTH), BF16),
            ],
        ),
        out_shape=[
            jax.ShapeDtypeStruct((SHARD, 256), BF16),
            jax.ShapeDtypeStruct((SHARD, 256), BF16),
        ],
        compiler_params=pltpu.CompilerParams(vmem_limit_bytes=48 << 20),
        cost_estimate=pl.CostEstimate(
            flops=2 * SHARD * MODEL_WIDTH * 512, bytes_accessed=18 << 20, transcendentals=0
        ),
        name="project",
    )(
        seq, tokens, pre_gain.reshape(1, -1), wq, wk, wv,
        q_gain.reshape(1, -1), k_gain.reshape(1, -1), table,
    )


def attend_kernel(step, pos_ref, q_ref, kv_ref, got_ref, pk_ref, pv_ref, out_ref, keys, values):
    @pl.when(pos_ref[0] == 0)
    def _():
        keys[0:SHARD] = pk_ref[...]
        values[0:SHARD, 0:128] = pv_ref[...]

    @pl.when(pos_ref[0] != 0)
    def _():
        keys[0:SHARD] = got_ref[:, 0:128]
        values[0:SHARD, 0:128] = got_ref[:, 128:256]

    keys[SHARD:] = kv_ref[:, 0:128]
    values[SHARD:, 0:128] = kv_ref[:, 128:256]
    values[:, 128:256] = jnp.ones((2 * SHARD, 128), BF16)

    span = HALF + WINDOW_SPAN
    row = lax.broadcasted_iota(jnp.int32, (2 * HALF, HALF), 0) % HALF
    col = lax.broadcasted_iota(jnp.int32, (2 * HALF, HALF), 1)
    lowest = jnp.float32(-jnp.inf)
    for part in range(2):
        first = pl.multiple_of(pos_ref[ROW_AT + 2 * step + part], HALF)
        q = q_ref[pl.ds(first, HALF), :]
        q = jnp.concatenate([q[:, 0:128], q[:, 128:256]], axis=0)
        k = keys[pl.ds(first, span), :]
        scores = lax.dot_general(q, k, (((1,), (1,)), ((), ())), preferred_element_type=F32)
        scores = jnp.concatenate(
            [
                jnp.where(col > row, scores[:, 0:HALF], lowest),
                scores[:, HALF:WINDOW_SPAN],
                jnp.where(col <= row, scores[:, WINDOW_SPAN:], lowest),
            ],
            axis=1,
        )
        top = jnp.max(scores, axis=-1, keepdims=True)
        weights = jnp.exp2((scores - top) * (SCORE_SCALE * LOG2E)).astype(BF16)
        mixed = jnp.dot(weights, values[pl.ds(first, span), :], preferred_element_type=F32)
        mixed = (mixed[:, 0:128] / mixed[:, 128:256]).astype(BF16)
        out_ref[part * HALF : (part + 1) * HALF, 0:128] = mixed[0:HALF]
        out_ref[part * HALF : (part + 1) * HALF, 128:256] = mixed[HALF:]


def attend(step, pos, q, kv, got, prior_k, prior_v):
    parts = 2
    vmem = pl.BlockSpec(memory_space=pltpu.VMEM)
    return pl.pallas_call(
        functools.partial(attend_kernel, step),
        in_specs=[pl.BlockSpec(memory_space=pltpu.SMEM)] + [vmem] * 5,
        out_specs=vmem,
        out_shape=jax.ShapeDtypeStruct((parts * HALF, 256), BF16),
        scratch_shapes=[
            pltpu.VMEM((2 * SHARD, 128), BF16),
            pltpu.VMEM((2 * SHARD, 256), BF16),
        ],
        compiler_params=pltpu.CompilerParams(vmem_limit_bytes=32 << 20),
        cost_estimate=pl.CostEstimate(
            flops=8 * parts * HALF * 1152 * 256, bytes_accessed=2 << 20,
            transcendentals=parts * 2 * HALF * 1152,
        ),
        name="attend",
    )(pos, q, kv, got, prior_k, prior_v)


ANY = pl.BlockSpec(memory_space=pl.ANY)
VMEM = pl.BlockSpec(memory_space=pltpu.VMEM)
SMEM = pl.BlockSpec(memory_space=pltpu.SMEM)


def quarter_start(number):
    return pl.multiple_of((number * 21 // 2) * 128, 128)


def pick_kernel(pos_ref, w_ref, own_ref, next_ref, last_ref, far_ref, sems):
    z, c = pos_ref[1], pos_ref[2]
    rows = pl.ds(pl.multiple_of(c * 128, 128), 128)
    copies = [
        pltpu.make_async_copy(
            w_ref.at[:, pl.ds(quarter_start(z), QUARTER)], own_ref, sems.at[3]
        )
    ]
    for i, (shift, ref) in enumerate(((1, next_ref), (3, last_ref), (2, far_ref))):
        cols = pl.ds(quarter_start((z + shift) % 4), QUARTER)
        copies.append(pltpu.make_async_copy(w_ref.at[rows, cols], ref, sems.at[i]))
    for copy in copies:
        copy.start()
    for copy in copies:
        copy.wait()


def pick(pos, w_out):
    part = jax.ShapeDtypeStruct((128, QUARTER), BF16)
    return pl.pallas_call(
        pick_kernel,
        in_specs=[SMEM, ANY],
        out_specs=[ANY] * 4,
        out_shape=[jax.ShapeDtypeStruct((256, QUARTER), BF16), part, part, part],
        scratch_shapes=[pltpu.SemaphoreType.DMA((4,))],
        cost_estimate=pl.CostEstimate(flops=0, bytes_accessed=4 << 20, transcendentals=0),
        name="pick",
    )(pos, w_out)


def product(pos_ref, a_refs, w_refs, a_all, w_all, sems):
    c = pos_ref[2]
    copies = [pltpu.make_async_copy(w_refs[0], w_all.at[0:256], sems.at[0])]
    for i in range(3):
        for j, side in enumerate((c, 1 - c)):
            at = pl.multiple_of(256 * (i + 1) + side * 128, 128)
            copies.append(
                pltpu.make_async_copy(
                    w_refs[1 + i + 3 * j], w_all.at[pl.ds(at, 128)], sems.at[1 + 2 * i + j]
                )
            )
    for copy in copies:
        copy.start()
    for i in range(4):
        a_all[:, 256 * i : 256 * (i + 1)] = a_refs[i][...]
    for copy in copies:
        copy.wait()
    return jnp.dot(a_all[...], w_all[...], preferred_element_type=F32)


def send_kernel(has_relay, *refs):
    pos_ref, a_refs, w_refs = refs[0], refs[1:5], refs[5:12]
    relay_refs = refs[12:14] if has_relay else ()
    up_ref, down_ref, a_all, w_all, sems = refs[-5:]
    out = product(pos_ref, a_refs, w_refs, a_all, w_all, sems)
    up, down = out[0:HALF], out[HALF:]
    if has_relay:
        up = up + relay_refs[0][...].astype(F32)
        down = down + relay_refs[1][...].astype(F32)
    up_ref[...] = up.astype(BF16)
    down_ref[...] = down.astype(BF16)


def keep_kernel(*refs):
    pos_ref, a_refs, w_refs = refs[0], refs[1:5], refs[5:12]
    first_ref, second_ref, out_ref, a_all, w_all, sems = refs[12:]
    out = product(pos_ref, a_refs, w_refs, a_all, w_all, sems)
    out_ref[0:HALF] = out[0:HALF] + first_ref[...].astype(F32)
    out_ref[HALF:] = out[HALF:] + second_ref[...].astype(F32)


PRODUCT_SCRATCH = [
    pltpu.VMEM((256, 1024), BF16),
    pltpu.VMEM((1024, QUARTER), BF16),
    pltpu.SemaphoreType.DMA((7,)),
]
PRODUCT_COST = pl.CostEstimate(
    flops=2 * 256 * 1024 * QUARTER, bytes_accessed=5 << 20, transcendentals=0
)


def send_step(pos, pieces, weights, relays):
    half = jax.ShapeDtypeStruct((HALF, QUARTER), BF16)
    return pl.pallas_call(
        functools.partial(send_kernel, bool(relays)),
        in_specs=[SMEM] + [VMEM] * 4 + [ANY] * 7 + [VMEM] * len(relays),
        out_specs=[VMEM] * 2,
        out_shape=[half, half],
        scratch_shapes=PRODUCT_SCRATCH,
        compiler_params=pltpu.CompilerParams(vmem_limit_bytes=32 << 20),
        cost_estimate=PRODUCT_COST,
        name="send_step",
    )(pos, *pieces, *weights, *relays)


def keep_step(pos, pieces, weights, first, second):
    return pl.pallas_call(
        keep_kernel,
        in_specs=[SMEM] + [VMEM] * 4 + [ANY] * 7 + [VMEM] * 2,
        out_specs=VMEM,
        out_shape=jax.ShapeDtypeStruct((256, QUARTER), F32),
        scratch_shapes=PRODUCT_SCRATCH,
        compiler_params=pltpu.CompilerParams(vmem_limit_bytes=32 << 20),
        cost_estimate=PRODUCT_COST,
        name="keep_step",
    )(pos, *pieces, *weights, first, second)


def total_kernel(pos_ref, kept_ref, up_ref, down_ref, own_ref, next_ref, last_ref, far_ref, total):
    z = pos_ref[1]
    total[0:HALF] = kept_ref[0:HALF] + up_ref[...].astype(F32)
    total[HALF:] = kept_ref[HALF:] + down_ref[...].astype(F32)

    def rows(shift):
        return total[pl.ds(pl.multiple_of(((z + shift) % 4) * 64, 64), 64), :]

    own_ref[...] = rows(0)
    next_ref[...] = rows(1).astype(BF16)
    last_ref[...] = rows(3).astype(BF16)
    far_ref[...] = rows(2).astype(BF16)


def total_step(pos, kept, up, down):
    part = jax.ShapeDtypeStruct((64, QUARTER), BF16)
    return pl.pallas_call(
        total_kernel,
        in_specs=[SMEM] + [VMEM] * 3,
        out_specs=[VMEM] * 4,
        out_shape=[jax.ShapeDtypeStruct((64, QUARTER), F32), part, part, part],
        scratch_shapes=[pltpu.VMEM((256, QUARTER), F32)],
        compiler_params=pltpu.CompilerParams(vmem_limit_bytes=32 << 20),
        cost_estimate=pl.CostEstimate(flops=1 << 20, bytes_accessed=4 << 20, transcendentals=0),
        name="total_step",
    )(pos, kept, up, down)


def finish_kernel(pos_ref, own_ref, next_ref, last_ref, far_ref, tok_ref, g_ref, out_ref, line, tok, sem):
    z = pos_ref[1]
    at = pl.multiple_of(pos_ref[ROW_AT + 8], 64)
    copy = pltpu.make_async_copy(tok_ref.at[pl.ds(at, 64)], tok, sem)
    copy.start()
    for shift, ref in ((0, own_ref), (3, next_ref), (1, last_ref), (2, far_ref)):
        line[:, pl.ds(quarter_start((z + shift) % 4), QUARTER)] = ref[...].astype(F32)
    copy.wait()

    def group(i, carry):
        rows = pl.ds(pl.multiple_of(i * 16, 16), 16)
        summed = line[rows, :]
        mean = jnp.sum(summed * summed, axis=-1, keepdims=True) * (1.0 / MODEL_WIDTH)
        normed = summed * lax.rsqrt(mean + EPSILON) * g_ref[...]
        out_ref[rows, :] = (tok[rows, :].astype(F32) + normed).astype(BF16)
        return carry

    lax.fori_loop(0, 4, group, 0)


def finish(pos, own, nxt, last, far, tokens, gain):
    return pl.pallas_call(
        finish_kernel,
        in_specs=[SMEM] + [VMEM] * 4 + [ANY, VMEM],
        out_specs=VMEM,
        out_shape=jax.ShapeDtypeStruct((64, MODEL_WIDTH), BF16),
        scratch_shapes=[
            pltpu.VMEM((64, MODEL_WIDTH), F32),
            pltpu.VMEM((64, MODEL_WIDTH), BF16),
            pltpu.SemaphoreType.DMA(()),
        ],
        compiler_params=pltpu.CompilerParams(vmem_limit_bytes=32 << 20),
        cost_estimate=pl.CostEstimate(flops=1 << 21, bytes_accessed=3 << 20, transcendentals=0),
        name="finish",
    )(pos, own, nxt, last, far, tokens, gain.reshape(1, -1))


def shift_by(array, axis, steps):
    return lax.ppermute(array, axis, [(i, (i + steps) % 4) for i in range(4)])


def from_line(pieces):
    return [shift_by(piece, "z", by) for piece, by in zip(pieces, (1, 3, 2), strict=True)]


def per_device(
    tokens, pre_gain, w_query, key_weight, value_weight, query_gain, key_gain,
    prior_key, prior_value, w_out, post_gain, table,
):
    device = lax.axis_index(("y", "c", "x", "z"))
    pos = lax.dynamic_slice_in_dim(jnp.asarray(places()), device, 1, 0).reshape(-1)
    own_w, *parts = pick(pos, w_out)
    pos, own_w, *parts = lax.optimization_barrier((pos, own_w, *parts))
    lines = from_line(parts)
    swapped = [lax.ppermute(part, "c", [(0, 1), (1, 0)]) for part in lines]
    weights = [own_w, *lines, *swapped]
    q, kv = project(
        pos, tokens, pre_gain, w_query, key_weight, value_weight,
        query_gain, key_gain, table,
    )
    got = lax.ppermute(kv, ("y", "c"), [(i, i + 1) for i in range(7)])

    def heads(step):
        mixed = attend(step, pos, q, kv, got, prior_key, prior_value)
        return [mixed, *from_line([mixed] * 3)]

    def send(step, relays):
        ahead, behind = send_step(pos, heads(step), weights, relays)
        return shift_by(ahead, "x", 1), shift_by(behind, "x", 3)

    relays = send(0, ())
    from_below, from_above = send(1, ())
    late_below, late_above = send(2, relays)
    kept = keep_step(pos, heads(3), weights, from_above, from_below)
    own, *others = total_step(pos, kept, late_below, late_above)
    return finish(pos, own, *from_line(others), tokens, post_gain)


def solution(mesh):
    fine = Mesh(mesh.devices.reshape(4, 2, 4, 4), ("y", "c", "x", "z"))
    seq, tp = ("y", "c"), ("x", "z")
    inner = jax.shard_map(
        per_device,
        mesh=fine,
        in_specs=(
            P(seq, None), P(), P(None, tp), P(None, tp), P(None, tp), P(), P(),
            P(None, tp), P(None, tp), P(tp, None), P(), P(),
        ),
        out_specs=P(seq + tp, None),
        check_vma=False,
    )

    def run(*args):
        return inner(*args, jnp.asarray(rotary_table()))

    return run
```

```python
import functools

import jax
import jax.numpy as jnp
import numpy as np
from jax import lax
from jax.experimental import pallas as pl
from jax.experimental.pallas import tpu as pltpu
from jax.sharding import Mesh
from jax.sharding import PartitionSpec as P

MODEL_WIDTH = 5376
HQ = 32
HEAD = 128
WINDOW_SPAN = 1024
BLOCK_TOKENS = 8192
SHARD = 1024
EPSILON = 1e-06
LOG2E = 1.4426950408889634
SCORE_SCALE = float(MODEL_WIDTH // HQ) ** (-0.5)

F32 = jnp.float32
BF16 = jnp.bfloat16

ROWS = 256
GROUP = 16
HALF = 128
QUARTER = 1408
ROW_AT = 3


ANY = pl.BlockSpec(memory_space=pl.ANY)
VMEM = pl.BlockSpec(memory_space=pltpu.VMEM)
SMEM = pl.BlockSpec(memory_space=pltpu.SMEM)
SMALL = pl.CostEstimate(flops=0, bytes_accessed=0, transcendentals=0)


def rotary_table():
    half = HEAD // 2
    exponent = np.arange(half, dtype=np.float32) * np.float32(-2.0 / HEAD)
    frequency = np.power(np.float64(10000.0), exponent.astype(np.float64)).astype(np.float32)
    position = (WINDOW_SPAN + np.arange(BLOCK_TOKENS)).astype(np.float32)
    angle = (position[:, None] * frequency[None, :]).astype(np.float64)
    return np.concatenate([np.cos(angle), np.sin(angle)], axis=1).astype(np.float32)


def places():
    rows = []
    for device in range(128):
        seq, x, z = device // 16, device // 4 % 4, device % 4
        far, up, down = ((x + by) % 4 * 256 for by in (2, 1, 3))
        rows.append(
            [seq, z, seq % 2, far, far + 128, up, up + 128, down, down + 128, x * 256,
             x * 256 + 128, x]
        )
    return np.array(rows, np.int32)


def rotate(u, gain, table):
    swapped = pltpu.roll(table, 64, 1)
    low = lax.broadcasted_iota(jnp.int32, table.shape, 1) < 64
    cosine = jnp.where(low, table, swapped)
    sine = jnp.where(low, -swapped, table)
    mean = jnp.sum(u * u, axis=-1, keepdims=True) * (1.0 / HEAD)
    u = u * lax.rsqrt(mean + EPSILON) * gain
    return (u * cosine + pltpu.roll(u, 64, 1) * sine).astype(BF16)


def project_kernel(
    pos_ref, tok_ref, g_ref, wq_ref, wk_ref, wv_ref, qg_ref, kg_ref, tab_ref,
    q_ref, kv_ref, own_ref, w_all, g_all, normed, sems,
):
    step = pl.program_id(0)
    copies = [
        pltpu.make_async_copy(wq_ref, w_all.at[:, 0:256], sems.at[0]),
        pltpu.make_async_copy(wk_ref, w_all.at[:, 256:384], sems.at[1]),
        pltpu.make_async_copy(wv_ref, w_all.at[:, 384:512], sems.at[2]),
    ]
    blocks = MODEL_WIDTH // 128

    def norm_group(i, carry):
        at = i * GROUP if isinstance(i, int) else pl.multiple_of(i * GROUP, GROUP)
        rows = pl.ds(at, GROUP)
        parts = [jnp.zeros((GROUP, 128), F32) for _ in range(2)]
        for b in range(blocks):
            v = tok_ref[rows, b * 128 : (b + 1) * 128].astype(F32)
            parts[b % 2] = parts[b % 2] + v * v
        mean = jnp.sum(parts[0] + parts[1], axis=-1, keepdims=True) * (1.0 / MODEL_WIDTH)
        r = jnp.broadcast_to(lax.rsqrt(mean + EPSILON), (GROUP, 128))
        for b in range(blocks):
            cols = slice(b * 128, (b + 1) * 128)
            v = tok_ref[rows, cols].astype(F32)
            normed[rows, cols] = (v * r * g_all[:, cols]).astype(BF16)
        return carry

    def multiply_and_rotate():
        raw = jnp.dot(normed[...], w_all[...], preferred_element_type=F32)
        table = tab_ref[...]
        q_ref[:, 0:128] = rotate(raw[:, 0:128], qg_ref[...], table)
        q_ref[:, 128:256] = rotate(raw[:, 128:256], qg_ref[...], table)
        kv_ref[:, 0:128] = rotate(raw[:, 256:384], kg_ref[...], table)
        kv_ref[:, 128:256] = raw[:, 384:512].astype(BF16)

    @pl.when(step == 0)
    def _():
        for copy in copies:
            copy.start()
        g_all[...] = jnp.broadcast_to(g_ref[...], g_all.shape)
        lax.fori_loop(0, ROWS // GROUP, norm_group, 0, unroll=4)
        for copy in copies:
            copy.wait()
        multiply_and_rotate()

    @pl.when(step != 0)
    def _():
        for i in range(ROWS // GROUP):
            norm_group(i, 0)
        multiply_and_rotate()

    @pl.when(step == pos_ref[ROW_AT + 8])
    def _():
        own_ref[...] = tok_ref[pl.ds(pl.multiple_of(pos_ref[1] * 64, 64), 64), :]


def project(pos, tokens, pre_gain, wq, wk, wv, q_gain, k_gain, table):
    whole = lambda shape: pl.BlockSpec(shape, lambda i, s: (0, 0))
    tile = lambda width: pl.BlockSpec((ROWS, width), lambda i, s: (i, 0))
    return pl.pallas_call(
        project_kernel,
        grid_spec=pltpu.PrefetchScalarGridSpec(
            num_scalar_prefetch=1,
            grid=(SHARD // ROWS,),
            in_specs=[
                tile(MODEL_WIDTH), whole((1, MODEL_WIDTH)), ANY, ANY, ANY,
                whole((1, 128)), whole((1, 128)),
                pl.BlockSpec((ROWS, 128), lambda i, s: (s[0] * (SHARD // ROWS) + i, 0)),
            ],
            out_specs=[tile(256), tile(256), whole((64, MODEL_WIDTH))],
            scratch_shapes=[
                pltpu.VMEM((MODEL_WIDTH, 512), BF16),
                pltpu.VMEM((GROUP, MODEL_WIDTH), F32),
                pltpu.VMEM((ROWS, MODEL_WIDTH), BF16),
                pltpu.SemaphoreType.DMA((3,)),
            ],
        ),
        out_shape=[
            jax.ShapeDtypeStruct((SHARD, 256), BF16),
            jax.ShapeDtypeStruct((SHARD, 256), BF16),
            jax.ShapeDtypeStruct((64, MODEL_WIDTH), BF16),
        ],
        compiler_params=pltpu.CompilerParams(vmem_limit_bytes=58 << 20),
        cost_estimate=pl.CostEstimate(
            flops=4 * SHARD * MODEL_WIDTH * 512, bytes_accessed=18 << 20, transcendentals=0
        ),
        name="project",
    )(
        pos, tokens, pre_gain.reshape(1, -1), wq, wk, wv,
        q_gain.reshape(1, -1), k_gain.reshape(1, -1), table,
    )


def attend_kernel(first_part, pos_ref, q_ref, kv_ref, got_ref, pk_ref, pv_ref, out_ref, keys, values):
    @pl.when(pos_ref[0] == 0)
    def _():
        keys[0:SHARD] = pk_ref[...]
        values[0:SHARD, 0:128] = pv_ref[...]

    @pl.when(pos_ref[0] != 0)
    def _():
        keys[0:SHARD] = got_ref[:, 0:128]
        values[0:SHARD, 0:128] = got_ref[:, 128:256]

    keys[SHARD:] = kv_ref[:, 0:128]
    values[SHARD:, 0:128] = kv_ref[:, 128:256]
    values[:, 128:256] = jnp.ones((2 * SHARD, 128), BF16)

    span = HALF + WINDOW_SPAN
    row = lax.broadcasted_iota(jnp.int32, (2 * HALF, HALF), 0) % HALF
    col = lax.broadcasted_iota(jnp.int32, (2 * HALF, HALF), 1)
    lowest = jnp.float32(-jnp.inf)
    for part in range(out_ref.shape[0] // HALF):
        first = pl.multiple_of(pos_ref[ROW_AT + first_part + part], HALF)
        q = q_ref[pl.ds(first, HALF), :]
        q = jnp.concatenate([q[:, 0:128], q[:, 128:256]], axis=0)
        k = keys[pl.ds(first, span), :]
        scores = lax.dot_general(q, k, (((1,), (1,)), ((), ())), preferred_element_type=F32)
        scores = jnp.concatenate(
            [
                jnp.where(col > row, scores[:, 0:HALF], lowest),
                scores[:, HALF:WINDOW_SPAN],
                jnp.where(col <= row, scores[:, WINDOW_SPAN:], lowest),
            ],
            axis=1,
        )
        top = jnp.max(scores, axis=-1, keepdims=True)
        weights = jnp.exp2((scores - top) * (SCORE_SCALE * LOG2E)).astype(BF16)
        mixed = jnp.dot(weights, values[pl.ds(first, span), :], preferred_element_type=F32)
        mixed = (mixed[:, 0:128] / mixed[:, 128:256]).astype(BF16)
        out_ref[part * HALF : (part + 1) * HALF, 0:128] = mixed[0:HALF]
        out_ref[part * HALF : (part + 1) * HALF, 128:256] = mixed[HALF:]


def attend(first_part, parts, pos, q, kv, got, prior_k, prior_v):
    vmem = pl.BlockSpec(memory_space=pltpu.VMEM)
    return pl.pallas_call(
        functools.partial(attend_kernel, first_part),
        in_specs=[pl.BlockSpec(memory_space=pltpu.SMEM)] + [vmem] * 5,
        out_specs=vmem,
        out_shape=jax.ShapeDtypeStruct((parts * HALF, 256), BF16),
        scratch_shapes=[
            pltpu.VMEM((2 * SHARD, 128), BF16),
            pltpu.VMEM((2 * SHARD, 256), BF16),
        ],
        compiler_params=pltpu.CompilerParams(vmem_limit_bytes=32 << 20),
        cost_estimate=SMALL,
        name="attend",
    )(pos, q, kv, got, prior_k, prior_v)


def quarter_start(number):
    return pl.multiple_of((number * 21 // 2) * 128, 128)


def pick_kernel(pos_ref, w_ref, own_ref, next_ref, last_ref, far_ref):
    z = pos_ref[1]
    for shift, ref in ((1, next_ref), (3, last_ref), (2, far_ref), (0, own_ref)):
        ref[...] = w_ref[:, pl.ds(quarter_start((z + shift) % 4), QUARTER)]


def pick(pos, w_out):
    return pl.pallas_call(
        pick_kernel,
        in_specs=[SMEM, VMEM],
        out_specs=[VMEM] * 4,
        out_shape=[jax.ShapeDtypeStruct((256, QUARTER), BF16)] * 4,
        compiler_params=pltpu.CompilerParams(vmem_limit_bytes=16 << 20),
        cost_estimate=SMALL,
        name="pick",
    )(pos, w_out)


def product(a_refs, w_refs, rows=slice(None)):
    out = None
    for a_ref, w_ref in zip(a_refs, w_refs, strict=True):
        term = jnp.dot(a_ref[rows, :], w_ref[...], preferred_element_type=F32)
        out = term if out is None else out + term
    return out


def far_kernel(*refs):
    out = product(refs[0:4], refs[4:8])
    refs[8][...] = out[0:HALF].astype(BF16)
    refs[9][...] = out[HALF:].astype(BF16)


def near_kernel(*refs):
    relay_up, relay_down, up_ref, down_ref = refs[8:]
    up = product(refs[0:4], refs[4:8], slice(0, 256))
    up_ref[0:HALF] = (up[0:HALF] + relay_up[...].astype(F32)).astype(BF16)
    up_ref[HALF:] = up[HALF:].astype(BF16)
    down = product(refs[0:4], refs[4:8], slice(256, 512))
    down_ref[0:HALF] = down[0:HALF].astype(BF16)
    down_ref[HALF:] = (down[HALF:] + relay_down[...].astype(F32)).astype(BF16)


def keep_kernel(*refs):
    refs[8][...] = product(refs[0:4], refs[4:8])


def multiply(kernel, pieces, weights, relays, out_shape, name):
    return pl.pallas_call(
        kernel,
        in_specs=[VMEM] * (8 + len(relays)),
        out_specs=jax.tree.map(lambda _: VMEM, out_shape),
        out_shape=out_shape,
        compiler_params=pltpu.CompilerParams(vmem_limit_bytes=24 << 20),
        cost_estimate=SMALL,
        name=name,
    )(*pieces, *weights, *relays)


def total_kernel(pos_ref, kept_ref, up_ref, down_ref, own_ref, next_ref, last_ref, far_ref, total):
    z = pos_ref[1]
    total[...] = kept_ref[...] + up_ref[...].astype(F32) + down_ref[...].astype(F32)

    def rows(shift):
        return total[pl.ds(pl.multiple_of(((z + shift) % 4) * 64, 64), 64), :]

    next_ref[...] = rows(1).astype(BF16)
    last_ref[...] = rows(3).astype(BF16)
    far_ref[...] = rows(2).astype(BF16)
    own_ref[...] = rows(0)


def total_step(pos, kept, up, down):
    part = jax.ShapeDtypeStruct((64, QUARTER), BF16)
    return pl.pallas_call(
        total_kernel,
        in_specs=[SMEM] + [VMEM] * 3,
        out_specs=[VMEM] * 4,
        out_shape=[jax.ShapeDtypeStruct((64, QUARTER), F32), part, part, part],
        scratch_shapes=[pltpu.VMEM((256, QUARTER), F32)],
        compiler_params=pltpu.CompilerParams(vmem_limit_bytes=32 << 20),
        cost_estimate=SMALL,
        name="total_step",
    )(pos, kept, up, down)


def finish_kernel(pos_ref, own_ref, next_ref, last_ref, far_ref, tok_ref, g_ref, out_ref, line):
    z = pos_ref[1]
    for shift, ref in ((0, own_ref), (3, next_ref), (1, last_ref), (2, far_ref)):
        line[:, pl.ds(quarter_start((z + shift) % 4), QUARTER)] = ref[...].astype(F32)
    for i in range(4):
        rows = slice(i * 16, (i + 1) * 16)
        total = jnp.zeros((16, 128), F32)
        for b in range(MODEL_WIDTH // 128):
            part = line[rows, b * 128 : (b + 1) * 128]
            total = total + part * part
        mean = jnp.sum(total, axis=-1, keepdims=True) * (1.0 / MODEL_WIDTH)
        r = jnp.broadcast_to(lax.rsqrt(mean + EPSILON), (16, 128))
        for b in range(MODEL_WIDTH // 128):
            cols = slice(b * 128, (b + 1) * 128)
            normed = line[rows, cols] * r * g_ref[:, cols]
            out_ref[rows, cols] = (tok_ref[rows, cols].astype(F32) + normed).astype(BF16)


def finish(pos, own, nxt, last, far, own_tokens, gain):
    return pl.pallas_call(
        finish_kernel,
        in_specs=[SMEM] + [VMEM] * 6,
        out_specs=VMEM,
        out_shape=jax.ShapeDtypeStruct((64, MODEL_WIDTH), BF16),
        scratch_shapes=[pltpu.VMEM((64, MODEL_WIDTH), F32)],
        compiler_params=pltpu.CompilerParams(vmem_limit_bytes=16 << 20),
        cost_estimate=SMALL,
        name="finish",
    )(pos, own, nxt, last, far, own_tokens, gain.reshape(1, -1))


def shift_by(array, axis, steps):
    return lax.ppermute(array, axis, [(i, (i + steps) % 4) for i in range(4)])


def from_line(pieces):
    return [shift_by(piece, "z", by) for piece, by in zip(pieces, (1, 3, 2), strict=True)]


def per_device(
    tokens, pre_gain, w_query, key_weight, value_weight, query_gain, key_gain,
    prior_key, prior_value, w_out, post_gain, table,
):
    device = lax.axis_index(("y", "c", "x", "z"))
    pos = lax.dynamic_slice_in_dim(jnp.asarray(places()), device, 1, 0).reshape(-1)
    own_w, *parts = pick(pos, w_out)
    pos, *parts = lax.optimization_barrier((pos, *parts))
    weights = [own_w, *from_line(parts)]
    q, kv, own_tokens = project(
        pos, tokens, pre_gain, w_query, key_weight, value_weight, query_gain, key_gain, table
    )
    got = lax.ppermute(kv, ("y", "c"), [(i, i + 1) for i in range(7)])

    pos, *weights[1:3] = lax.optimization_barrier((pos, *weights[1:3]))
    far = attend(0, 2, pos, q, kv, got, prior_key, prior_value)
    far_heads = [far, *from_line([far] * 3)]
    pos, _ = lax.optimization_barrier((pos, far))
    near = attend(2, 4, pos, q, kv, got, prior_key, prior_value)
    near_heads = [near, *from_line([near] * 3)]
    *far_heads, _ = lax.optimization_barrier((*far_heads, near))

    half = jax.ShapeDtypeStruct((HALF, QUARTER), BF16)
    full = jax.ShapeDtypeStruct((256, QUARTER), BF16)
    kept_shape = jax.ShapeDtypeStruct((256, QUARTER), F32)
    up, down = multiply(far_kernel, far_heads, weights, (), [half, half], "far")
    relays = (shift_by(up, "x", 1), shift_by(down, "x", 3))
    pos, _ = lax.optimization_barrier((pos, near))
    kept = attend(6, 2, pos, q, kv, got, prior_key, prior_value)
    kept_heads = [kept, *from_line([kept] * 3)]
    kept, *relays = lax.optimization_barrier((kept, *relays))
    up, down = multiply(near_kernel, near_heads, weights, relays, [full, full], "near")
    up, down = shift_by(up, "x", 1), shift_by(down, "x", 3)
    kept = multiply(keep_kernel, kept_heads, weights, (), kept_shape, "keep")
    own, *others = total_step(pos, kept, up, down)
    return finish(pos, own, *from_line(others), own_tokens, post_gain)


def solution(mesh):
    fine = Mesh(mesh.devices.reshape(4, 2, 4, 4), ("y", "c", "x", "z"))
    seq, tp = ("y", "c"), ("x", "z")
    inner = jax.shard_map(
        per_device,
        mesh=fine,
        in_specs=(
            P(seq, None), P(), P(None, tp), P(None, tp), P(None, tp), P(), P(),
            P(None, tp), P(None, tp), P(tp, None), P(), P(),
        ),
        out_specs=P(seq + tp, None),
        check_vma=False,
    )

    def run(*args):
        return inner(*args, jnp.asarray(rotary_table()))

    return run
```

```python
import functools

import jax
import jax.numpy as jnp
import numpy as np
from jax import lax
from jax.experimental import pallas as pl
from jax.experimental.pallas import tpu as pltpu
from jax.sharding import Mesh
from jax.sharding import PartitionSpec as P

MODEL_WIDTH = 5376
HQ = 32
HEAD = 128
WINDOW_SPAN = 1024
BLOCK_TOKENS = 8192
SHARD = 1024
EPSILON = 1e-06
LOG2E = 1.4426950408889634
SCORE_SCALE = float(MODEL_WIDTH // HQ) ** (-0.5)

F32 = jnp.float32
BF16 = jnp.bfloat16

ROWS = 256
GROUP = 16
HALF = 128
QUARTER = 1408
ROW_AT = 3


ANY = pl.BlockSpec(memory_space=pl.ANY)
VMEM = pl.BlockSpec(memory_space=pltpu.VMEM)
SMEM = pl.BlockSpec(memory_space=pltpu.SMEM)
SMALL = pl.CostEstimate(flops=0, bytes_accessed=0, transcendentals=0)


def rotary_table():
    half = HEAD // 2
    exponent = np.arange(half, dtype=np.float32) * np.float32(-2.0 / HEAD)
    frequency = np.power(np.float64(10000.0), exponent.astype(np.float64)).astype(np.float32)
    position = (WINDOW_SPAN + np.arange(BLOCK_TOKENS)).astype(np.float32)
    angle = (position[:, None] * frequency[None, :]).astype(np.float64)
    return np.concatenate([np.cos(angle), np.sin(angle)], axis=1).astype(np.float32)


def places():
    rows = []
    for device in range(128):
        seq, x, z = device // 16, device // 4 % 4, device % 4
        far, up, down = ((x + by) % 4 * 256 for by in (2, 1, 3))
        rows.append(
            [seq, z, seq % 2, far, far + 128, up, up + 128, down, down + 128, x * 256,
             x * 256 + 128, x]
        )
    return np.array(rows, np.int32)


def rotate(u, gain, table):
    swapped = pltpu.roll(table, 64, 1)
    low = lax.broadcasted_iota(jnp.int32, table.shape, 1) < 64
    cosine = jnp.where(low, table, swapped)
    sine = jnp.where(low, -swapped, table)
    mean = jnp.sum(u * u, axis=-1, keepdims=True) * (1.0 / HEAD)
    u = u * lax.rsqrt(mean + EPSILON) * gain
    return (u * cosine + pltpu.roll(u, 64, 1) * sine).astype(BF16)


def key_value_kernel(
    pos_ref, tok_ref, g_ref, wk_ref, wv_ref, gain_ref, tab_ref,
    normed, kv_ref, own_ref, w_all, g_all, sems,
):
    step = pl.program_id(0)
    copies = [
        pltpu.make_async_copy(wk_ref, w_all.at[:, 0:128], sems.at[0]),
        pltpu.make_async_copy(wv_ref, w_all.at[:, 128:256], sems.at[1]),
    ]
    blocks = MODEL_WIDTH // 128

    def norm_group(i, carry):
        at = i * GROUP if isinstance(i, int) else pl.multiple_of(i * GROUP, GROUP)
        rows = pl.ds(at, GROUP)
        parts = [jnp.zeros((GROUP, 128), F32) for _ in range(2)]
        for b in range(blocks):
            v = tok_ref[rows, b * 128 : (b + 1) * 128].astype(F32)
            parts[b % 2] = parts[b % 2] + v * v
        mean = jnp.sum(parts[0] + parts[1], axis=-1, keepdims=True) * (1.0 / MODEL_WIDTH)
        r = jnp.broadcast_to(lax.rsqrt(mean + EPSILON), (GROUP, 128))
        for b in range(blocks):
            cols = slice(b * 128, (b + 1) * 128)
            v = tok_ref[rows, cols].astype(F32)
            normed[rows, cols] = (v * r * g_all[:, cols]).astype(BF16)
        return carry

    def multiply_and_rotate():
        raw = jnp.dot(normed[...], w_all[...], preferred_element_type=F32)
        kv_ref[:, 0:128] = rotate(raw[:, 0:128], gain_ref[...], tab_ref[...])
        kv_ref[:, 128:256] = raw[:, 128:256].astype(BF16)

    @pl.when(step == 0)
    def _():
        for copy in copies:
            copy.start()
        g_all[...] = jnp.broadcast_to(g_ref[...], g_all.shape)
        lax.fori_loop(0, ROWS // GROUP, norm_group, 0, unroll=4)
        for copy in copies:
            copy.wait()
        multiply_and_rotate()

    @pl.when(step != 0)
    def _():
        for i in range(ROWS // GROUP):
            norm_group(i, 0)
        multiply_and_rotate()

    @pl.when(step == pos_ref[ROW_AT + 8])
    def _():
        own_ref[...] = tok_ref[pl.ds(pl.multiple_of(pos_ref[1] * 64, 64), 64), :]


def in_hbm(*arrays):
    return [pltpu.with_memory_space_constraint(array, pltpu.HBM) for array in arrays]


def whole(shape):
    return pl.BlockSpec(shape, lambda i, s: (0, 0))


def row_tile(width):
    return pl.BlockSpec((ROWS, width), lambda i, s: (i, 0))


TABLE_TILE = pl.BlockSpec((ROWS, 128), lambda i, s: (s[0] * (SHARD // ROWS) + i, 0))


def key_value(pos, tokens, pre_gain, wk, wv, gain, table):
    tokens, wk, wv, table = in_hbm(tokens, wk, wv, table)
    return pl.pallas_call(
        key_value_kernel,
        grid_spec=pltpu.PrefetchScalarGridSpec(
            num_scalar_prefetch=1,
            grid=(SHARD // ROWS,),
            in_specs=[
                row_tile(MODEL_WIDTH), whole((1, MODEL_WIDTH)), ANY, ANY,
                whole((1, 128)), TABLE_TILE,
            ],
            out_specs=[row_tile(MODEL_WIDTH), row_tile(256), whole((64, MODEL_WIDTH))],
            scratch_shapes=[
                pltpu.VMEM((MODEL_WIDTH, 256), BF16),
                pltpu.VMEM((GROUP, MODEL_WIDTH), F32),
                pltpu.SemaphoreType.DMA((2,)),
            ],
        ),
        out_shape=[
            jax.ShapeDtypeStruct((SHARD, MODEL_WIDTH), BF16),
            jax.ShapeDtypeStruct((SHARD, 256), BF16),
            jax.ShapeDtypeStruct((64, MODEL_WIDTH), BF16),
        ],
        compiler_params=pltpu.CompilerParams(vmem_limit_bytes=28 << 20),
        cost_estimate=pl.CostEstimate(
            flops=8 * SHARD * MODEL_WIDTH * 256, bytes_accessed=26 << 20, transcendentals=0
        ),
        name="key_value",
    )(pos, tokens, pre_gain.reshape(1, -1), wk, wv, gain.reshape(1, -1), table)


def query_kernel(pos_ref, normed_ref, w_ref, gain_ref, tab_ref, q_ref):
    raw = jnp.dot(normed_ref[...], w_ref[...], preferred_element_type=F32)
    q_ref[:, 0:128] = rotate(raw[:, 0:128], gain_ref[...], tab_ref[...])
    q_ref[:, 128:256] = rotate(raw[:, 128:256], gain_ref[...], tab_ref[...])


def query(pos, normed, wq, gain, table):
    wq, table = in_hbm(wq, table)
    return pl.pallas_call(
        query_kernel,
        grid_spec=pltpu.PrefetchScalarGridSpec(
            num_scalar_prefetch=1,
            grid=(SHARD // ROWS,),
            in_specs=[
                row_tile(MODEL_WIDTH), whole((MODEL_WIDTH, 256)), whole((1, 128)), TABLE_TILE
            ],
            out_specs=row_tile(256),
        ),
        out_shape=jax.ShapeDtypeStruct((SHARD, 256), BF16),
        compiler_params=pltpu.CompilerParams(vmem_limit_bytes=24 << 20),
        cost_estimate=SMALL,
        name="query",
    )(pos, normed, wq, gain.reshape(1, -1), table)


def attend_kernel(first_part, pos_ref, q_ref, kv_ref, got_ref, pk_ref, pv_ref, out_ref, keys, values):
    @pl.when(pos_ref[0] == 0)
    def _():
        keys[0:SHARD] = pk_ref[...]
        values[0:SHARD, 0:128] = pv_ref[...]

    @pl.when(pos_ref[0] != 0)
    def _():
        keys[0:SHARD] = got_ref[:, 0:128]
        values[0:SHARD, 0:128] = got_ref[:, 128:256]

    keys[SHARD:] = kv_ref[:, 0:128]
    values[SHARD:, 0:128] = kv_ref[:, 128:256]
    values[:, 128:256] = jnp.ones((2 * SHARD, 128), BF16)

    span = HALF + WINDOW_SPAN
    row = lax.broadcasted_iota(jnp.int32, (2 * HALF, HALF), 0) % HALF
    col = lax.broadcasted_iota(jnp.int32, (2 * HALF, HALF), 1)
    lowest = jnp.float32(-jnp.inf)
    for part in range(out_ref.shape[0] // HALF):
        first = pl.multiple_of(pos_ref[ROW_AT + first_part + part], HALF)
        q = q_ref[pl.ds(first, HALF), :]
        q = jnp.concatenate([q[:, 0:128], q[:, 128:256]], axis=0)
        k = keys[pl.ds(first, span), :]
        scores = lax.dot_general(q, k, (((1,), (1,)), ((), ())), preferred_element_type=F32)
        scores = jnp.concatenate(
            [
                jnp.where(col > row, scores[:, 0:HALF], lowest),
                scores[:, HALF:WINDOW_SPAN],
                jnp.where(col <= row, scores[:, WINDOW_SPAN:], lowest),
            ],
            axis=1,
        )
        top = jnp.max(scores, axis=-1, keepdims=True)
        weights = jnp.exp2((scores - top) * (SCORE_SCALE * LOG2E)).astype(BF16)
        mixed = jnp.dot(weights, values[pl.ds(first, span), :], preferred_element_type=F32)
        mixed = (mixed[:, 0:128] / mixed[:, 128:256]).astype(BF16)
        out_ref[part * HALF : (part + 1) * HALF, 0:128] = mixed[0:HALF]
        out_ref[part * HALF : (part + 1) * HALF, 128:256] = mixed[HALF:]


def attend(first_part, parts, pos, q, kv, got, prior_k, prior_v):
    vmem = pl.BlockSpec(memory_space=pltpu.VMEM)
    return pl.pallas_call(
        functools.partial(attend_kernel, first_part),
        in_specs=[pl.BlockSpec(memory_space=pltpu.SMEM)] + [vmem] * 5,
        out_specs=vmem,
        out_shape=jax.ShapeDtypeStruct((parts * HALF, 256), BF16),
        scratch_shapes=[
            pltpu.VMEM((2 * SHARD, 128), BF16),
            pltpu.VMEM((2 * SHARD, 256), BF16),
        ],
        compiler_params=pltpu.CompilerParams(vmem_limit_bytes=32 << 20),
        cost_estimate=SMALL,
        name="attend",
    )(pos, q, kv, got, prior_k, prior_v)


def quarter_start(number):
    return pl.multiple_of((number * 21 // 2) * 128, 128)


def pick_kernel(pos_ref, w_ref, own_ref, next_ref, last_ref, far_ref):
    z = pos_ref[1]
    rows = pl.ds(pl.multiple_of(pos_ref[2] * 128, 128), 128)
    for shift, ref in ((1, next_ref), (3, last_ref), (2, far_ref)):
        ref[...] = w_ref[rows, pl.ds(quarter_start((z + shift) % 4), QUARTER)]
    own_ref[...] = w_ref[:, pl.ds(quarter_start(z), QUARTER)]


def pick(pos, w_out):
    part = jax.ShapeDtypeStruct((128, QUARTER), BF16)
    return pl.pallas_call(
        pick_kernel,
        in_specs=[SMEM, VMEM],
        out_specs=[VMEM] * 4,
        out_shape=[jax.ShapeDtypeStruct((256, QUARTER), BF16), part, part, part],
        compiler_params=pltpu.CompilerParams(vmem_limit_bytes=16 << 20),
        cost_estimate=SMALL,
        name="pick",
    )(pos, w_out)


def join_kernel(pos_ref, *refs):
    c, out_ref = pos_ref[2], refs[6]
    for i in range(3):
        out_ref[i, pl.ds(pl.multiple_of(c * 128, 128), 128)] = refs[i][...]
        out_ref[i, pl.ds(pl.multiple_of((1 - c) * 128, 128), 128)] = refs[3 + i][...]


def join(pos, lines, swapped):
    return pl.pallas_call(
        join_kernel,
        in_specs=[SMEM] + [VMEM] * 6,
        out_specs=VMEM,
        out_shape=jax.ShapeDtypeStruct((3, 256, QUARTER), BF16),
        compiler_params=pltpu.CompilerParams(vmem_limit_bytes=16 << 20),
        cost_estimate=SMALL,
        name="join",
    )(pos, *lines, *swapped)


def product(a_refs, w_refs, rows=slice(None)):
    out = jnp.dot(a_refs[0][rows, :], w_refs[0][...], preferred_element_type=F32)
    for i in range(3):
        out = out + jnp.dot(a_refs[1 + i][rows, :], w_refs[1][i], preferred_element_type=F32)
    return out


def far_kernel(*refs):
    out = product(refs[0:4], refs[4:6])
    refs[6][...] = out[0:HALF].astype(BF16)
    refs[7][...] = out[HALF:].astype(BF16)


def near_kernel(*refs):
    relay_up, relay_down, up_ref, down_ref = refs[6:]
    up = product(refs[0:4], refs[4:6], slice(0, 256))
    up_ref[0:HALF] = (up[0:HALF] + relay_up[...].astype(F32)).astype(BF16)
    up_ref[HALF:] = up[HALF:].astype(BF16)
    down = product(refs[0:4], refs[4:6], slice(256, 512))
    down_ref[0:HALF] = down[0:HALF].astype(BF16)
    down_ref[HALF:] = (down[HALF:] + relay_down[...].astype(F32)).astype(BF16)


def keep_kernel(*refs):
    refs[6][...] = product(refs[0:4], refs[4:6])


def multiply(kernel, pieces, weights, relays, out_shape, name):
    return pl.pallas_call(
        kernel,
        in_specs=[VMEM] * (6 + len(relays)),
        out_specs=jax.tree.map(lambda _: VMEM, out_shape),
        out_shape=out_shape,
        compiler_params=pltpu.CompilerParams(vmem_limit_bytes=24 << 20),
        cost_estimate=SMALL,
        name=name,
    )(*pieces, *weights, *relays)


def total_kernel(pos_ref, kept_ref, up_ref, down_ref, own_ref, next_ref, last_ref, far_ref, total):
    z = pos_ref[1]
    total[...] = kept_ref[...] + up_ref[...].astype(F32) + down_ref[...].astype(F32)

    def rows(shift):
        return total[pl.ds(pl.multiple_of(((z + shift) % 4) * 64, 64), 64), :]

    next_ref[...] = rows(1).astype(BF16)
    last_ref[...] = rows(3).astype(BF16)
    far_ref[...] = rows(2).astype(BF16)
    own_ref[...] = rows(0)


def total_step(pos, kept, up, down):
    part = jax.ShapeDtypeStruct((64, QUARTER), BF16)
    return pl.pallas_call(
        total_kernel,
        in_specs=[SMEM] + [VMEM] * 3,
        out_specs=[VMEM] * 4,
        out_shape=[jax.ShapeDtypeStruct((64, QUARTER), F32), part, part, part],
        scratch_shapes=[pltpu.VMEM((256, QUARTER), F32)],
        compiler_params=pltpu.CompilerParams(vmem_limit_bytes=32 << 20),
        cost_estimate=SMALL,
        name="total_step",
    )(pos, kept, up, down)


def finish_kernel(pos_ref, own_ref, next_ref, last_ref, far_ref, tok_ref, g_ref, out_ref, line):
    z = pos_ref[1]
    for shift, ref in ((0, own_ref), (3, next_ref), (1, last_ref), (2, far_ref)):
        line[:, pl.ds(quarter_start((z + shift) % 4), QUARTER)] = ref[...].astype(F32)
    for i in range(4):
        rows = slice(i * 16, (i + 1) * 16)
        total = jnp.zeros((16, 128), F32)
        for b in range(MODEL_WIDTH // 128):
            part = line[rows, b * 128 : (b + 1) * 128]
            total = total + part * part
        mean = jnp.sum(total, axis=-1, keepdims=True) * (1.0 / MODEL_WIDTH)
        r = jnp.broadcast_to(lax.rsqrt(mean + EPSILON), (16, 128))
        for b in range(MODEL_WIDTH // 128):
            cols = slice(b * 128, (b + 1) * 128)
            normed = line[rows, cols] * r * g_ref[:, cols]
            out_ref[rows, cols] = (tok_ref[rows, cols].astype(F32) + normed).astype(BF16)


def finish(pos, own, nxt, last, far, own_tokens, gain):
    return pl.pallas_call(
        finish_kernel,
        in_specs=[SMEM] + [VMEM] * 6,
        out_specs=VMEM,
        out_shape=jax.ShapeDtypeStruct((64, MODEL_WIDTH), BF16),
        scratch_shapes=[pltpu.VMEM((64, MODEL_WIDTH), F32)],
        compiler_params=pltpu.CompilerParams(vmem_limit_bytes=16 << 20),
        cost_estimate=SMALL,
        name="finish",
    )(pos, own, nxt, last, far, own_tokens, gain.reshape(1, -1))


def shift_by(array, axis, steps):
    return lax.ppermute(array, axis, [(i, (i + steps) % 4) for i in range(4)])


def from_line(pieces):
    return [shift_by(piece, "z", by) for piece, by in zip(pieces, (1, 3, 2), strict=True)]


def per_device(
    tokens, pre_gain, w_query, key_weight, value_weight, query_gain, key_gain,
    prior_key, prior_value, w_out, post_gain, table,
):
    device = lax.axis_index(("y", "c", "x", "z"))
    pos = lax.dynamic_slice_in_dim(jnp.asarray(places()), device, 1, 0).reshape(-1)
    own_w, *parts = pick(pos, w_out)
    pos, *parts = lax.optimization_barrier((pos, *parts))
    lines = from_line(parts)
    normed, kv, own_tokens = key_value(
        pos, tokens, pre_gain, key_weight, value_weight, key_gain, table
    )
    got = lax.ppermute(kv, ("y", "c"), [(i, i + 1) for i in range(7)])
    q = query(pos, normed, w_query, query_gain, table)
    *lines, q = lax.optimization_barrier((*lines, q))
    swapped = [lax.ppermute(part, "c", [(0, 1), (1, 0)]) for part in lines]
    weights = [own_w, join(pos, lines, swapped)]

    pos, weights[1] = lax.optimization_barrier((pos, weights[1]))
    far = attend(0, 2, pos, q, kv, got, prior_key, prior_value)
    far_heads = [far, *from_line([far] * 3)]
    pos, _ = lax.optimization_barrier((pos, far))
    near = attend(2, 4, pos, q, kv, got, prior_key, prior_value)
    near_heads = [near, *from_line([near] * 3)]
    *far_heads, _ = lax.optimization_barrier((*far_heads, near))

    half = jax.ShapeDtypeStruct((HALF, QUARTER), BF16)
    full = jax.ShapeDtypeStruct((256, QUARTER), BF16)
    kept_shape = jax.ShapeDtypeStruct((256, QUARTER), F32)
    up, down = multiply(far_kernel, far_heads, weights, (), [half, half], "far")
    relays = (shift_by(up, "x", 1), shift_by(down, "x", 3))
    pos, _ = lax.optimization_barrier((pos, near))
    kept = attend(6, 2, pos, q, kv, got, prior_key, prior_value)
    kept_heads = [kept, *from_line([kept] * 3)]
    kept, *relays = lax.optimization_barrier((kept, *relays))
    up, down = multiply(near_kernel, near_heads, weights, relays, [full, full], "near")
    up, down = shift_by(up, "x", 1), shift_by(down, "x", 3)
    kept = multiply(keep_kernel, kept_heads, weights, (), kept_shape, "keep")
    own, *others = total_step(pos, kept, up, down)
    return finish(pos, own, *from_line(others), own_tokens, post_gain)


def solution(mesh):
    fine = Mesh(mesh.devices.reshape(4, 2, 4, 4), ("y", "c", "x", "z"))
    seq, tp = ("y", "c"), ("x", "z")
    inner = jax.shard_map(
        per_device,
        mesh=fine,
        in_specs=(
            P(seq, None), P(), P(None, tp), P(None, tp), P(None, tp), P(), P(),
            P(None, tp), P(None, tp), P(tp, None), P(), P(),
        ),
        out_specs=P(seq + tp, None),
        check_vma=False,
    )

    def run(*args):
        return inner(*args, jnp.asarray(rotary_table()))

    return run
```

```python
import functools

import jax
import jax.numpy as jnp
import numpy as np
from jax import lax
from jax.experimental import pallas as pl
from jax.experimental.pallas import tpu as pltpu
from jax.sharding import Mesh
from jax.sharding import PartitionSpec as P

MODEL_WIDTH = 5376
HQ = 32
HEAD = 128
WINDOW_SPAN = 1024
BLOCK_TOKENS = 8192
SHARD = 1024
EPSILON = 1e-06
LOG2E = 1.4426950408889634
SCORE_SCALE = float(MODEL_WIDTH // HQ) ** (-0.5)

F32 = jnp.float32
BF16 = jnp.bfloat16

ROWS = 256
GROUP = 16
HALF = 128
QUARTER = 1408
ROW_AT = 3


ANY = pl.BlockSpec(memory_space=pl.ANY)
VMEM = pl.BlockSpec(memory_space=pltpu.VMEM)
SMEM = pl.BlockSpec(memory_space=pltpu.SMEM)
SMALL = pl.CostEstimate(flops=0, bytes_accessed=0, transcendentals=0)


def rotary_table():
    half = HEAD // 2
    exponent = np.arange(half, dtype=np.float32) * np.float32(-2.0 / HEAD)
    frequency = np.power(np.float64(10000.0), exponent.astype(np.float64)).astype(np.float32)
    position = (WINDOW_SPAN + np.arange(BLOCK_TOKENS)).astype(np.float32)
    angle = (position[:, None] * frequency[None, :]).astype(np.float64)
    return np.concatenate([np.cos(angle), np.sin(angle)], axis=1).astype(np.float32)


def places():
    rows = []
    for device in range(128):
        seq, x, z = device // 16, device // 4 % 4, device % 4
        far, up, down = ((x + by) % 4 * 256 for by in (2, 1, 3))
        rows.append(
            [seq, z, seq % 2, far, far + 128, up, up + 128, down, down + 128, x * 256,
             x * 256 + 128, x]
        )
    return np.array(rows, np.int32)


def rotate(u, gain, table):
    swapped = pltpu.roll(table, 64, 1)
    low = lax.broadcasted_iota(jnp.int32, table.shape, 1) < 64
    cosine = jnp.where(low, table, swapped)
    sine = jnp.where(low, -swapped, table)
    mean = jnp.sum(u * u, axis=-1, keepdims=True) * (1.0 / HEAD)
    u = u * lax.rsqrt(mean + EPSILON) * gain
    return (u * cosine + pltpu.roll(u, 64, 1) * sine).astype(BF16)


def key_value_kernel(
    pos_ref, tok_ref, g_ref, wk_ref, wv_ref, gain_ref, tab_ref,
    normed, kv_ref, own_ref, w_all, g_all, sems,
):
    step = pl.program_id(0)
    copies = [
        pltpu.make_async_copy(wk_ref, w_all.at[:, 0:128], sems.at[0]),
        pltpu.make_async_copy(wv_ref, w_all.at[:, 128:256], sems.at[1]),
    ]
    blocks = MODEL_WIDTH // 128

    def norm_group(i, carry):
        at = i * GROUP if isinstance(i, int) else pl.multiple_of(i * GROUP, GROUP)
        rows = pl.ds(at, GROUP)
        parts = [jnp.zeros((GROUP, 128), F32) for _ in range(2)]
        for b in range(blocks):
            v = tok_ref[rows, b * 128 : (b + 1) * 128].astype(F32)
            parts[b % 2] = parts[b % 2] + v * v
        mean = jnp.sum(parts[0] + parts[1], axis=-1, keepdims=True) * (1.0 / MODEL_WIDTH)
        r = jnp.broadcast_to(lax.rsqrt(mean + EPSILON), (GROUP, 128))
        for b in range(blocks):
            cols = slice(b * 128, (b + 1) * 128)
            v = tok_ref[rows, cols].astype(F32)
            normed[rows, cols] = (v * r * g_all[:, cols]).astype(BF16)
        return carry

    def multiply_and_rotate():
        raw = jnp.dot(normed[...], w_all[...], preferred_element_type=F32)
        kv_ref[:, 0:128] = rotate(raw[:, 0:128], gain_ref[...], tab_ref[...])
        kv_ref[:, 128:256] = raw[:, 128:256].astype(BF16)

    @pl.when(step == 0)
    def _():
        for copy in copies:
            copy.start()
        g_all[...] = jnp.broadcast_to(g_ref[...], g_all.shape)
        lax.fori_loop(0, ROWS // GROUP, norm_group, 0, unroll=4)
        for copy in copies:
            copy.wait()
        multiply_and_rotate()

    @pl.when(step != 0)
    def _():
        for i in range(ROWS // GROUP):
            norm_group(i, 0)
        multiply_and_rotate()

    @pl.when(step == pos_ref[ROW_AT + 8])
    def _():
        own_ref[...] = tok_ref[pl.ds(pl.multiple_of(pos_ref[1] * 64, 64), 64), :]


def in_hbm(*arrays):
    return [pltpu.with_memory_space_constraint(array, pltpu.HBM) for array in arrays]


def whole(shape):
    return pl.BlockSpec(shape, lambda i, s: (0, 0))


def row_tile(width):
    return pl.BlockSpec((ROWS, width), lambda i, s: (i, 0))


TABLE_TILE = pl.BlockSpec((ROWS, 128), lambda i, s: (s[0] * (SHARD // ROWS) + i, 0))


def key_value(pos, tokens, pre_gain, wk, wv, gain, table):
    tokens, wk, wv, table = in_hbm(tokens, wk, wv, table)
    return pl.pallas_call(
        key_value_kernel,
        grid_spec=pltpu.PrefetchScalarGridSpec(
            num_scalar_prefetch=1,
            grid=(SHARD // ROWS,),
            in_specs=[
                row_tile(MODEL_WIDTH), whole((1, MODEL_WIDTH)), ANY, ANY,
                whole((1, 128)), TABLE_TILE,
            ],
            out_specs=[row_tile(MODEL_WIDTH), row_tile(256), whole((64, MODEL_WIDTH))],
            scratch_shapes=[
                pltpu.VMEM((MODEL_WIDTH, 256), BF16),
                pltpu.VMEM((GROUP, MODEL_WIDTH), F32),
                pltpu.SemaphoreType.DMA((2,)),
            ],
        ),
        out_shape=[
            jax.ShapeDtypeStruct((SHARD, MODEL_WIDTH), BF16),
            jax.ShapeDtypeStruct((SHARD, 256), BF16),
            jax.ShapeDtypeStruct((64, MODEL_WIDTH), BF16),
        ],
        compiler_params=pltpu.CompilerParams(vmem_limit_bytes=28 << 20),
        cost_estimate=pl.CostEstimate(
            flops=8 * SHARD * MODEL_WIDTH * 256, bytes_accessed=26 << 20, transcendentals=0
        ),
        name="key_value",
    )(pos, tokens, pre_gain.reshape(1, -1), wk, wv, gain.reshape(1, -1), table)


def query_kernel(pos_ref, normed_ref, w_ref, gain_ref, tab_ref, q_ref):
    raw = jnp.dot(normed_ref[...], w_ref[...], preferred_element_type=F32)
    q_ref[:, 0:128] = rotate(raw[:, 0:128], gain_ref[...], tab_ref[...])
    q_ref[:, 128:256] = rotate(raw[:, 128:256], gain_ref[...], tab_ref[...])


def query(pos, normed, wq, gain, table):
    (table,) = in_hbm(table)
    return pl.pallas_call(
        query_kernel,
        grid_spec=pltpu.PrefetchScalarGridSpec(
            num_scalar_prefetch=1,
            grid=(SHARD // ROWS,),
            in_specs=[
                row_tile(MODEL_WIDTH), whole((MODEL_WIDTH, 256)), whole((1, 128)), TABLE_TILE
            ],
            out_specs=row_tile(256),
        ),
        out_shape=jax.ShapeDtypeStruct((SHARD, 256), BF16),
        compiler_params=pltpu.CompilerParams(vmem_limit_bytes=24 << 20),
        cost_estimate=SMALL,
        name="query",
    )(pos, normed, wq, gain.reshape(1, -1), table)


def attend_kernel(first_part, pos_ref, q_ref, kv_ref, got_ref, pk_ref, pv_ref, out_ref, keys, values):
    @pl.when(pos_ref[0] == 0)
    def _():
        keys[0:SHARD] = pk_ref[...]
        values[0:SHARD, 0:128] = pv_ref[...]

    @pl.when(pos_ref[0] != 0)
    def _():
        keys[0:SHARD] = got_ref[:, 0:128]
        values[0:SHARD, 0:128] = got_ref[:, 128:256]

    keys[SHARD:] = kv_ref[:, 0:128]
    values[SHARD:, 0:128] = kv_ref[:, 128:256]
    values[:, 128:256] = jnp.ones((2 * SHARD, 128), BF16)

    span = HALF + WINDOW_SPAN
    row = lax.broadcasted_iota(jnp.int32, (2 * HALF, HALF), 0) % HALF
    col = lax.broadcasted_iota(jnp.int32, (2 * HALF, HALF), 1)
    lowest = jnp.float32(-jnp.inf)
    for part in range(out_ref.shape[0] // HALF):
        first = pl.multiple_of(pos_ref[ROW_AT + first_part + part], HALF)
        q = q_ref[pl.ds(first, HALF), :]
        q = jnp.concatenate([q[:, 0:128], q[:, 128:256]], axis=0)
        k = keys[pl.ds(first, span), :]
        scores = lax.dot_general(q, k, (((1,), (1,)), ((), ())), preferred_element_type=F32)
        scores = jnp.concatenate(
            [
                jnp.where(col > row, scores[:, 0:HALF], lowest),
                scores[:, HALF:WINDOW_SPAN],
                jnp.where(col <= row, scores[:, WINDOW_SPAN:], lowest),
            ],
            axis=1,
        )
        top = jnp.max(scores, axis=-1, keepdims=True)
        weights = jnp.exp2((scores - top) * (SCORE_SCALE * LOG2E)).astype(BF16)
        mixed = jnp.dot(weights, values[pl.ds(first, span), :], preferred_element_type=F32)
        mixed = (mixed[:, 0:128] / mixed[:, 128:256]).astype(BF16)
        out_ref[part * HALF : (part + 1) * HALF, 0:128] = mixed[0:HALF]
        out_ref[part * HALF : (part + 1) * HALF, 128:256] = mixed[HALF:]


def attend(first_part, parts, pos, q, kv, got, prior_k, prior_v):
    vmem = pl.BlockSpec(memory_space=pltpu.VMEM)
    return pl.pallas_call(
        functools.partial(attend_kernel, first_part),
        in_specs=[pl.BlockSpec(memory_space=pltpu.SMEM)] + [vmem] * 5,
        out_specs=vmem,
        out_shape=jax.ShapeDtypeStruct((parts * HALF, 256), BF16),
        scratch_shapes=[
            pltpu.VMEM((2 * SHARD, 128), BF16),
            pltpu.VMEM((2 * SHARD, 256), BF16),
        ],
        compiler_params=pltpu.CompilerParams(vmem_limit_bytes=32 << 20),
        cost_estimate=SMALL,
        name="attend",
    )(pos, q, kv, got, prior_k, prior_v)


def quarter_start(number):
    return pl.multiple_of((number * 21 // 2) * 128, 128)


def pick_kernel(pos_ref, w_ref, own_ref, next_ref, last_ref, far_ref, sems):
    z = pos_ref[1]
    rows = pl.ds(pl.multiple_of(pos_ref[2] * 128, 128), 128)
    copies = []
    for i, (shift, ref) in enumerate(((1, next_ref), (3, last_ref), (2, far_ref))):
        cols = pl.ds(quarter_start((z + shift) % 4), QUARTER)
        copies.append(pltpu.make_async_copy(w_ref.at[rows, cols], ref, sems.at[i]))
    cols = pl.ds(quarter_start(z), QUARTER)
    copies.append(pltpu.make_async_copy(w_ref.at[:, cols], own_ref, sems.at[3]))
    for copy in copies:
        copy.start()
    for copy in copies:
        copy.wait()


def pick(pos, w_out):
    part = jax.ShapeDtypeStruct((128, QUARTER), BF16)
    return pl.pallas_call(
        pick_kernel,
        in_specs=[SMEM, ANY],
        out_specs=[VMEM] * 4,
        out_shape=[jax.ShapeDtypeStruct((256, QUARTER), BF16), part, part, part],
        scratch_shapes=[pltpu.SemaphoreType.DMA((4,))],
        compiler_params=pltpu.CompilerParams(vmem_limit_bytes=16 << 20),
        cost_estimate=SMALL,
        name="pick",
    )(pos, *in_hbm(w_out))


def join_kernel(pos_ref, *refs):
    c, out_ref = pos_ref[2], refs[6]
    for i in range(3):
        out_ref[i, pl.ds(pl.multiple_of(c * 128, 128), 128)] = refs[i][...]
        out_ref[i, pl.ds(pl.multiple_of((1 - c) * 128, 128), 128)] = refs[3 + i][...]


def join(pos, lines, swapped):
    return pl.pallas_call(
        join_kernel,
        in_specs=[SMEM] + [VMEM] * 6,
        out_specs=VMEM,
        out_shape=jax.ShapeDtypeStruct((3, 256, QUARTER), BF16),
        compiler_params=pltpu.CompilerParams(vmem_limit_bytes=16 << 20),
        cost_estimate=SMALL,
        name="join",
    )(pos, *lines, *swapped)


def product(a_refs, w_refs, rows=slice(None)):
    out = jnp.dot(a_refs[0][rows, :], w_refs[0][...], preferred_element_type=F32)
    for i in range(3):
        out = out + jnp.dot(a_refs[1 + i][rows, :], w_refs[1][i], preferred_element_type=F32)
    return out


def far_kernel(*refs):
    out = product(refs[0:4], refs[4:6])
    refs[6][...] = out[0:HALF].astype(BF16)
    refs[7][...] = out[HALF:].astype(BF16)


def near_kernel(*refs):
    relay_up, relay_down, up_ref, down_ref = refs[6:]
    up = product(refs[0:4], refs[4:6], slice(0, 256))
    up_ref[0:HALF] = (up[0:HALF] + relay_up[...].astype(F32)).astype(BF16)
    up_ref[HALF:] = up[HALF:].astype(BF16)
    down = product(refs[0:4], refs[4:6], slice(256, 512))
    down_ref[0:HALF] = down[0:HALF].astype(BF16)
    down_ref[HALF:] = (down[HALF:] + relay_down[...].astype(F32)).astype(BF16)


def keep_kernel(*refs):
    refs[6][...] = product(refs[0:4], refs[4:6])


def multiply(kernel, pieces, weights, relays, out_shape, name):
    return pl.pallas_call(
        kernel,
        in_specs=[VMEM] * (6 + len(relays)),
        out_specs=jax.tree.map(lambda _: VMEM, out_shape),
        out_shape=out_shape,
        compiler_params=pltpu.CompilerParams(vmem_limit_bytes=24 << 20),
        cost_estimate=SMALL,
        name=name,
    )(*pieces, *weights, *relays)


def total_kernel(pos_ref, kept_ref, up_ref, down_ref, own_ref, next_ref, last_ref, far_ref, total):
    z = pos_ref[1]
    total[...] = kept_ref[...] + up_ref[...].astype(F32) + down_ref[...].astype(F32)

    def rows(shift):
        return total[pl.ds(pl.multiple_of(((z + shift) % 4) * 64, 64), 64), :]

    next_ref[...] = rows(1).astype(BF16)
    last_ref[...] = rows(3).astype(BF16)
    far_ref[...] = rows(2).astype(BF16)
    own_ref[...] = rows(0)


def total_step(pos, kept, up, down):
    part = jax.ShapeDtypeStruct((64, QUARTER), BF16)
    return pl.pallas_call(
        total_kernel,
        in_specs=[SMEM] + [VMEM] * 3,
        out_specs=[VMEM] * 4,
        out_shape=[jax.ShapeDtypeStruct((64, QUARTER), F32), part, part, part],
        scratch_shapes=[pltpu.VMEM((256, QUARTER), F32)],
        compiler_params=pltpu.CompilerParams(vmem_limit_bytes=32 << 20),
        cost_estimate=SMALL,
        name="total_step",
    )(pos, kept, up, down)


def finish_kernel(pos_ref, own_ref, next_ref, last_ref, far_ref, tok_ref, g_ref, out_ref, line):
    z = pos_ref[1]
    for shift, ref in ((0, own_ref), (3, next_ref), (1, last_ref), (2, far_ref)):
        line[:, pl.ds(quarter_start((z + shift) % 4), QUARTER)] = ref[...].astype(F32)
    for i in range(4):
        rows = slice(i * 16, (i + 1) * 16)
        total = jnp.zeros((16, 128), F32)
        for b in range(MODEL_WIDTH // 128):
            part = line[rows, b * 128 : (b + 1) * 128]
            total = total + part * part
        mean = jnp.sum(total, axis=-1, keepdims=True) * (1.0 / MODEL_WIDTH)
        r = jnp.broadcast_to(lax.rsqrt(mean + EPSILON), (16, 128))
        for b in range(MODEL_WIDTH // 128):
            cols = slice(b * 128, (b + 1) * 128)
            normed = line[rows, cols] * r * g_ref[:, cols]
            out_ref[rows, cols] = (tok_ref[rows, cols].astype(F32) + normed).astype(BF16)


def finish(pos, own, nxt, last, far, own_tokens, gain):
    return pl.pallas_call(
        finish_kernel,
        in_specs=[SMEM] + [VMEM] * 6,
        out_specs=VMEM,
        out_shape=jax.ShapeDtypeStruct((64, MODEL_WIDTH), BF16),
        scratch_shapes=[pltpu.VMEM((64, MODEL_WIDTH), F32)],
        compiler_params=pltpu.CompilerParams(vmem_limit_bytes=16 << 20),
        cost_estimate=SMALL,
        name="finish",
    )(pos, own, nxt, last, far, own_tokens, gain.reshape(1, -1))


def shift_by(array, axis, steps):
    return lax.ppermute(array, axis, [(i, (i + steps) % 4) for i in range(4)])


def from_line(pieces):
    return [shift_by(piece, "z", by) for piece, by in zip(pieces, (1, 3, 2), strict=True)]


def per_device(
    tokens, pre_gain, w_query, key_weight, value_weight, query_gain, key_gain,
    prior_key, prior_value, w_out, post_gain, table,
):
    device = lax.axis_index(("y", "c", "x", "z"))
    pos = lax.dynamic_slice_in_dim(jnp.asarray(places()), device, 1, 0).reshape(-1)
    own_w, *parts = pick(pos, w_out)
    pos, *parts = lax.optimization_barrier((pos, *parts))
    lines = from_line(parts)
    normed, kv, own_tokens = key_value(
        pos, tokens, pre_gain, key_weight, value_weight, key_gain, table
    )
    got = lax.ppermute(kv, ("y", "c"), [(i, i + 1) for i in range(7)])
    q = query(pos, normed, w_query, query_gain, table)
    q, *lines = lax.optimization_barrier((q, *lines))
    swapped = [lax.ppermute(part, "c", [(0, 1), (1, 0)]) for part in lines]
    pos, *swapped = lax.optimization_barrier((pos, *swapped))

    far = attend(0, 2, pos, q, kv, got, prior_key, prior_value)
    far_heads = [far, *from_line([far] * 3)]
    pos, _ = lax.optimization_barrier((pos, far))
    near = attend(2, 4, pos, q, kv, got, prior_key, prior_value)
    near_heads = [near, *from_line([near] * 3)]
    *far_heads, _ = lax.optimization_barrier((*far_heads, near))
    last_pos, _ = lax.optimization_barrier((pos, near))
    weights = [own_w, join(last_pos, lines, swapped)]

    half = jax.ShapeDtypeStruct((HALF, QUARTER), BF16)
    full = jax.ShapeDtypeStruct((256, QUARTER), BF16)
    kept_shape = jax.ShapeDtypeStruct((256, QUARTER), F32)
    up, down = multiply(far_kernel, far_heads, weights, (), [half, half], "far")
    relays = (shift_by(up, "x", 1), shift_by(down, "x", 3))
    pos, _ = lax.optimization_barrier((pos, near))
    kept = attend(6, 2, pos, q, kv, got, prior_key, prior_value)
    kept_heads = [kept, *from_line([kept] * 3)]
    kept, *relays = lax.optimization_barrier((kept, *relays))
    up, down = multiply(near_kernel, near_heads, weights, relays, [full, full], "near")
    up, down = shift_by(up, "x", 1), shift_by(down, "x", 3)
    kept = multiply(keep_kernel, kept_heads, weights, (), kept_shape, "keep")
    own, *others = total_step(pos, kept, up, down)
    return finish(pos, own, *from_line(others), own_tokens, post_gain)


def solution(mesh):
    fine = Mesh(mesh.devices.reshape(4, 2, 4, 4), ("y", "c", "x", "z"))
    seq, tp = ("y", "c"), ("x", "z")
    inner = jax.shard_map(
        per_device,
        mesh=fine,
        in_specs=(
            P(seq, None), P(), P(None, tp), P(None, tp), P(None, tp), P(), P(),
            P(None, tp), P(None, tp), P(tp, None), P(), P(),
        ),
        out_specs=P(seq + tp, None),
        check_vma=False,
    )

    def run(*args):
        return inner(*args, jnp.asarray(rotary_table()))

    return run
```

```python
import functools

import jax
import jax.numpy as jnp
import numpy as np
from jax import lax
from jax.experimental import pallas as pl
from jax.experimental.pallas import tpu as pltpu
from jax.sharding import Mesh
from jax.sharding import PartitionSpec as P

MODEL_WIDTH = 5376
HQ = 32
HEAD = 128
WINDOW_SPAN = 1024
BLOCK_TOKENS = 8192
SHARD = 1024
EPSILON = 1e-06
LOG2E = 1.4426950408889634
SCORE_SCALE = float(MODEL_WIDTH // HQ) ** (-0.5)

F32 = jnp.float32
BF16 = jnp.bfloat16

ROWS = 256
GROUP = 16
HALF = 128
QUARTER = 1408
ROW_AT = 3
LINE_AT = 12


ANY = pl.BlockSpec(memory_space=pl.ANY)
VMEM = pl.BlockSpec(memory_space=pltpu.VMEM)
SMEM = pl.BlockSpec(memory_space=pltpu.SMEM)
SMALL = pl.CostEstimate(flops=0, bytes_accessed=0, transcendentals=0)


def rotary_table():
    half = HEAD // 2
    exponent = np.arange(half, dtype=np.float32) * np.float32(-2.0 / HEAD)
    frequency = np.power(np.float64(10000.0), exponent.astype(np.float64)).astype(np.float32)
    position = (WINDOW_SPAN + np.arange(BLOCK_TOKENS)).astype(np.float32)
    angle = (position[:, None] * frequency[None, :]).astype(np.float64)
    return np.concatenate([np.cos(angle), np.sin(angle)], axis=1).astype(np.float32)


def places():
    rows = []
    for device in range(128):
        seq, x, z = device // 16, device // 4 % 4, device % 4
        far, up, down = ((x ^ by) * 256 for by in (2, 1, 3))
        rows.append(
            [seq, z, seq % 2, far, far + 128, up, up + 128, down, down + 128, x * 256,
             x * 256 + 128, x, z ^ 1, z ^ 3, z ^ 2]
        )
    return np.array(rows, np.int32)


def rotate(u, gain, table):
    swapped = pltpu.roll(table, 64, 1)
    low = lax.broadcasted_iota(jnp.int32, table.shape, 1) < 64
    cosine = jnp.where(low, table, swapped)
    sine = jnp.where(low, -swapped, table)
    mean = jnp.sum(u * u, axis=-1, keepdims=True) * (1.0 / HEAD)
    u = u * lax.rsqrt(mean + EPSILON) * gain
    return (u * cosine + pltpu.roll(u, 64, 1) * sine).astype(BF16)


def key_value_kernel(
    pos_ref, tok_ref, g_ref, wk_ref, wv_ref, gain_ref, tab_ref,
    normed, kv_ref, own_ref, w_all, g_all, sems,
):
    step = pl.program_id(0)
    copies = [
        pltpu.make_async_copy(wk_ref, w_all.at[:, 0:128], sems.at[0]),
        pltpu.make_async_copy(wv_ref, w_all.at[:, 128:256], sems.at[1]),
    ]
    blocks = MODEL_WIDTH // 128

    def norm_group(i, carry):
        at = i * GROUP if isinstance(i, int) else pl.multiple_of(i * GROUP, GROUP)
        rows = pl.ds(at, GROUP)
        parts = [jnp.zeros((GROUP, 128), F32) for _ in range(2)]
        for b in range(blocks):
            v = tok_ref[rows, b * 128 : (b + 1) * 128].astype(F32)
            parts[b % 2] = parts[b % 2] + v * v
        mean = jnp.sum(parts[0] + parts[1], axis=-1, keepdims=True) * (1.0 / MODEL_WIDTH)
        r = jnp.broadcast_to(lax.rsqrt(mean + EPSILON), (GROUP, 128))
        for b in range(blocks):
            cols = slice(b * 128, (b + 1) * 128)
            v = tok_ref[rows, cols].astype(F32)
            normed[rows, cols] = (v * r * g_all[:, cols]).astype(BF16)
        return carry

    def multiply_and_rotate():
        raw = jnp.dot(normed[...], w_all[...], preferred_element_type=F32)
        kv_ref[:, 0:128] = rotate(raw[:, 0:128], gain_ref[...], tab_ref[...])
        kv_ref[:, 128:256] = raw[:, 128:256].astype(BF16)

    @pl.when(step == 0)
    def _():
        for copy in copies:
            copy.start()
        g_all[...] = jnp.broadcast_to(g_ref[...], g_all.shape)
        lax.fori_loop(0, ROWS // GROUP, norm_group, 0, unroll=4)
        for copy in copies:
            copy.wait()
        multiply_and_rotate()

    @pl.when(step != 0)
    def _():
        for i in range(ROWS // GROUP):
            norm_group(i, 0)
        multiply_and_rotate()

    @pl.when(step == pos_ref[ROW_AT + 8])
    def _():
        own_ref[...] = tok_ref[pl.ds(pl.multiple_of(pos_ref[1] * 64, 64), 64), :]


def in_hbm(*arrays):
    return [pltpu.with_memory_space_constraint(array, pltpu.HBM) for array in arrays]


def whole(shape):
    return pl.BlockSpec(shape, lambda i, s: (0, 0))


def row_tile(width):
    return pl.BlockSpec((ROWS, width), lambda i, s: (i, 0))


TABLE_TILE = pl.BlockSpec((ROWS, 128), lambda i, s: (s[0] * (SHARD // ROWS) + i, 0))


def key_value(pos, tokens, pre_gain, wk, wv, gain, table):
    tokens, wk, wv, table = in_hbm(tokens, wk, wv, table)
    return pl.pallas_call(
        key_value_kernel,
        grid_spec=pltpu.PrefetchScalarGridSpec(
            num_scalar_prefetch=1,
            grid=(SHARD // ROWS,),
            in_specs=[
                row_tile(MODEL_WIDTH), whole((1, MODEL_WIDTH)), ANY, ANY,
                whole((1, 128)), TABLE_TILE,
            ],
            out_specs=[row_tile(MODEL_WIDTH), row_tile(256), whole((64, MODEL_WIDTH))],
            scratch_shapes=[
                pltpu.VMEM((MODEL_WIDTH, 256), BF16),
                pltpu.VMEM((GROUP, MODEL_WIDTH), F32),
                pltpu.SemaphoreType.DMA((2,)),
            ],
        ),
        out_shape=[
            jax.ShapeDtypeStruct((SHARD, MODEL_WIDTH), BF16),
            jax.ShapeDtypeStruct((SHARD, 256), BF16),
            jax.ShapeDtypeStruct((64, MODEL_WIDTH), BF16),
        ],
        compiler_params=pltpu.CompilerParams(vmem_limit_bytes=28 << 20),
        cost_estimate=pl.CostEstimate(
            flops=8 * SHARD * MODEL_WIDTH * 256, bytes_accessed=26 << 20, transcendentals=0
        ),
        name="key_value",
    )(pos, tokens, pre_gain.reshape(1, -1), wk, wv, gain.reshape(1, -1), table)


def query_kernel(pos_ref, normed_ref, w_ref, gain_ref, tab_ref, q_ref):
    raw = jnp.dot(normed_ref[...], w_ref[...], preferred_element_type=F32)
    q_ref[:, 0:128] = rotate(raw[:, 0:128], gain_ref[...], tab_ref[...])
    q_ref[:, 128:256] = rotate(raw[:, 128:256], gain_ref[...], tab_ref[...])


def query(pos, normed, wq, gain, table):
    (table,) = in_hbm(table)
    return pl.pallas_call(
        query_kernel,
        grid_spec=pltpu.PrefetchScalarGridSpec(
            num_scalar_prefetch=1,
            grid=(SHARD // ROWS,),
            in_specs=[
                row_tile(MODEL_WIDTH), whole((MODEL_WIDTH, 256)), whole((1, 128)), TABLE_TILE
            ],
            out_specs=row_tile(256),
        ),
        out_shape=jax.ShapeDtypeStruct((SHARD, 256), BF16),
        compiler_params=pltpu.CompilerParams(vmem_limit_bytes=24 << 20),
        cost_estimate=SMALL,
        name="query",
    )(pos, normed, wq, gain.reshape(1, -1), table)


def attend_kernel(first_part, pos_ref, q_ref, kv_ref, got_ref, pk_ref, pv_ref, out_ref, keys, values):
    @pl.when(pos_ref[0] == 0)
    def _():
        keys[0:SHARD] = pk_ref[...]
        values[0:SHARD, 0:128] = pv_ref[...]

    @pl.when(pos_ref[0] != 0)
    def _():
        keys[0:SHARD] = got_ref[:, 0:128]
        values[0:SHARD, 0:128] = got_ref[:, 128:256]

    keys[SHARD:] = kv_ref[:, 0:128]
    values[SHARD:, 0:128] = kv_ref[:, 128:256]
    values[:, 128:256] = jnp.ones((2 * SHARD, 128), BF16)

    span = HALF + WINDOW_SPAN
    row = lax.broadcasted_iota(jnp.int32, (2 * HALF, HALF), 0) % HALF
    col = lax.broadcasted_iota(jnp.int32, (2 * HALF, HALF), 1)
    lowest = jnp.float32(-jnp.inf)
    for part in range(out_ref.shape[0] // HALF):
        first = pl.multiple_of(pos_ref[ROW_AT + first_part + part], HALF)
        q = q_ref[pl.ds(first, HALF), :]
        q = jnp.concatenate([q[:, 0:128], q[:, 128:256]], axis=0)
        k = keys[pl.ds(first, span), :]
        scores = lax.dot_general(q, k, (((1,), (1,)), ((), ())), preferred_element_type=F32)
        scores = jnp.concatenate(
            [
                jnp.where(col > row, scores[:, 0:HALF], lowest),
                scores[:, HALF:WINDOW_SPAN],
                jnp.where(col <= row, scores[:, WINDOW_SPAN:], lowest),
            ],
            axis=1,
        )
        top = jnp.max(scores, axis=-1, keepdims=True)
        weights = jnp.exp2((scores - top) * (SCORE_SCALE * LOG2E)).astype(BF16)
        mixed = jnp.dot(weights, values[pl.ds(first, span), :], preferred_element_type=F32)
        mixed = (mixed[:, 0:128] / mixed[:, 128:256]).astype(BF16)
        out_ref[part * HALF : (part + 1) * HALF, 0:128] = mixed[0:HALF]
        out_ref[part * HALF : (part + 1) * HALF, 128:256] = mixed[HALF:]


def attend(first_part, parts, pos, q, kv, got, prior_k, prior_v):
    vmem = pl.BlockSpec(memory_space=pltpu.VMEM)
    return pl.pallas_call(
        functools.partial(attend_kernel, first_part),
        in_specs=[pl.BlockSpec(memory_space=pltpu.SMEM)] + [vmem] * 5,
        out_specs=vmem,
        out_shape=jax.ShapeDtypeStruct((parts * HALF, 256), BF16),
        scratch_shapes=[
            pltpu.VMEM((2 * SHARD, 128), BF16),
            pltpu.VMEM((2 * SHARD, 256), BF16),
        ],
        compiler_params=pltpu.CompilerParams(vmem_limit_bytes=32 << 20),
        cost_estimate=SMALL,
        name="attend",
    )(pos, q, kv, got, prior_k, prior_v)


def quarter_start(number):
    return pl.multiple_of((number * 21 // 2) * 128, 128)


def pick_kernel(pos_ref, w_ref, own_ref, next_ref, last_ref, far_ref, sems):
    z = pos_ref[1]
    rows = pl.ds(pl.multiple_of(pos_ref[2] * 128, 128), 128)
    copies = []
    for i, ref in enumerate((next_ref, last_ref, far_ref)):
        cols = pl.ds(quarter_start(pos_ref[LINE_AT + i]), QUARTER)
        copies.append(pltpu.make_async_copy(w_ref.at[rows, cols], ref, sems.at[i]))
    cols = pl.ds(quarter_start(z), QUARTER)
    copies.append(pltpu.make_async_copy(w_ref.at[:, cols], own_ref, sems.at[3]))
    for copy in copies:
        copy.start()
    for copy in copies:
        copy.wait()


def pick(pos, w_out):
    part = jax.ShapeDtypeStruct((128, QUARTER), BF16)
    return pl.pallas_call(
        pick_kernel,
        in_specs=[SMEM, ANY],
        out_specs=[VMEM] * 4,
        out_shape=[jax.ShapeDtypeStruct((256, QUARTER), BF16), part, part, part],
        scratch_shapes=[pltpu.SemaphoreType.DMA((4,))],
        compiler_params=pltpu.CompilerParams(vmem_limit_bytes=16 << 20),
        cost_estimate=SMALL,
        name="pick",
    )(pos, *in_hbm(w_out))


def join_kernel(pos_ref, *refs):
    c, out_ref = pos_ref[2], refs[6]
    for i in range(3):
        out_ref[i, pl.ds(pl.multiple_of(c * 128, 128), 128)] = refs[i][...]
        out_ref[i, pl.ds(pl.multiple_of((1 - c) * 128, 128), 128)] = refs[3 + i][...]


def join(pos, lines, swapped):
    return pl.pallas_call(
        join_kernel,
        in_specs=[SMEM] + [VMEM] * 6,
        out_specs=VMEM,
        out_shape=jax.ShapeDtypeStruct((3, 256, QUARTER), BF16),
        compiler_params=pltpu.CompilerParams(vmem_limit_bytes=16 << 20),
        cost_estimate=SMALL,
        name="join",
    )(pos, *lines, *swapped)


def product(a_refs, w_refs, rows=slice(None)):
    out = jnp.dot(a_refs[0][rows, :], w_refs[0][...], preferred_element_type=F32)
    for i in range(3):
        out = out + jnp.dot(a_refs[1 + i][rows, :], w_refs[1][i], preferred_element_type=F32)
    return out


def far_kernel(*refs):
    out = product(refs[0:4], refs[4:6])
    refs[6][...] = out[0:HALF].astype(BF16)
    refs[7][...] = out[HALF:].astype(BF16)


def near_kernel(*refs):
    for_down, for_up, up_ref, down_ref = refs[6:]
    up = product(refs[0:4], refs[4:6], slice(0, 256))
    up_ref[0:HALF] = up[0:HALF].astype(BF16)
    up_ref[HALF:] = (up[HALF:] + for_up[...].astype(F32)).astype(BF16)
    down = product(refs[0:4], refs[4:6], slice(256, 512))
    down_ref[0:HALF] = (down[0:HALF] + for_down[...].astype(F32)).astype(BF16)
    down_ref[HALF:] = down[HALF:].astype(BF16)


def keep_kernel(*refs):
    refs[6][...] = product(refs[0:4], refs[4:6])


def multiply(kernel, pieces, weights, relays, out_shape, name):
    return pl.pallas_call(
        kernel,
        in_specs=[VMEM] * (6 + len(relays)),
        out_specs=jax.tree.map(lambda _: VMEM, out_shape),
        out_shape=out_shape,
        compiler_params=pltpu.CompilerParams(vmem_limit_bytes=24 << 20),
        cost_estimate=SMALL,
        name=name,
    )(*pieces, *weights, *relays)


def total_kernel(pos_ref, kept_ref, up_ref, down_ref, own_ref, next_ref, last_ref, far_ref, total):
    z = pos_ref[1]
    total[...] = kept_ref[...] + up_ref[...].astype(F32) + down_ref[...].astype(F32)

    def rows(number):
        return total[pl.ds(pl.multiple_of(number * 64, 64), 64), :]

    for i, ref in enumerate((next_ref, last_ref, far_ref)):
        ref[...] = rows(pos_ref[LINE_AT + i]).astype(BF16)
    own_ref[...] = rows(z)


def total_step(pos, kept, up, down):
    part = jax.ShapeDtypeStruct((64, QUARTER), BF16)
    return pl.pallas_call(
        total_kernel,
        in_specs=[SMEM] + [VMEM] * 3,
        out_specs=[VMEM] * 4,
        out_shape=[jax.ShapeDtypeStruct((64, QUARTER), F32), part, part, part],
        scratch_shapes=[pltpu.VMEM((256, QUARTER), F32)],
        compiler_params=pltpu.CompilerParams(vmem_limit_bytes=32 << 20),
        cost_estimate=SMALL,
        name="total_step",
    )(pos, kept, up, down)


def finish_kernel(pos_ref, own_ref, next_ref, last_ref, far_ref, tok_ref, g_ref, out_ref, line):
    for at, ref in ((1, own_ref), (LINE_AT, next_ref), (LINE_AT + 1, last_ref), (LINE_AT + 2, far_ref)):
        line[:, pl.ds(quarter_start(pos_ref[at]), QUARTER)] = ref[...].astype(F32)
    for i in range(4):
        rows = slice(i * 16, (i + 1) * 16)
        total = jnp.zeros((16, 128), F32)
        for b in range(MODEL_WIDTH // 128):
            part = line[rows, b * 128 : (b + 1) * 128]
            total = total + part * part
        mean = jnp.sum(total, axis=-1, keepdims=True) * (1.0 / MODEL_WIDTH)
        r = jnp.broadcast_to(lax.rsqrt(mean + EPSILON), (16, 128))
        for b in range(MODEL_WIDTH // 128):
            cols = slice(b * 128, (b + 1) * 128)
            normed = line[rows, cols] * r * g_ref[:, cols]
            out_ref[rows, cols] = (tok_ref[rows, cols].astype(F32) + normed).astype(BF16)


def finish(pos, own, nxt, last, far, own_tokens, gain):
    return pl.pallas_call(
        finish_kernel,
        in_specs=[SMEM] + [VMEM] * 6,
        out_specs=VMEM,
        out_shape=jax.ShapeDtypeStruct((64, MODEL_WIDTH), BF16),
        scratch_shapes=[pltpu.VMEM((64, MODEL_WIDTH), F32)],
        compiler_params=pltpu.CompilerParams(vmem_limit_bytes=16 << 20),
        cost_estimate=SMALL,
        name="finish",
    )(pos, own, nxt, last, far, own_tokens, gain.reshape(1, -1))


def exchange(array, axis, by):
    return lax.ppermute(array, axis, [(i, i ^ by) for i in range(4)])


def from_line(pieces):
    return [exchange(piece, "z", by) for piece, by in zip(pieces, (1, 3, 2), strict=True)]


def per_device(
    tokens, pre_gain, w_query, key_weight, value_weight, query_gain, key_gain,
    prior_key, prior_value, w_out, post_gain, table,
):
    device = lax.axis_index(("y", "c", "x", "z"))
    pos = lax.dynamic_slice_in_dim(jnp.asarray(places()), device, 1, 0).reshape(-1)
    own_w, *parts = pick(pos, w_out)
    pos, *parts = lax.optimization_barrier((pos, *parts))
    lines = from_line(parts)
    normed, kv, own_tokens = key_value(
        pos, tokens, pre_gain, key_weight, value_weight, key_gain, table
    )
    got = lax.ppermute(kv, ("y", "c"), [(i, i + 1) for i in range(7)])
    q = query(pos, normed, w_query, query_gain, table)
    q, *lines = lax.optimization_barrier((q, *lines))
    swapped = [lax.ppermute(part, "c", [(0, 1), (1, 0)]) for part in lines]
    pos, *swapped = lax.optimization_barrier((pos, *swapped))

    far = attend(0, 2, pos, q, kv, got, prior_key, prior_value)
    far_heads = [far, *from_line([far] * 3)]
    pos, _ = lax.optimization_barrier((pos, far))
    near = attend(2, 4, pos, q, kv, got, prior_key, prior_value)
    near_heads = [near, *from_line([near] * 3)]
    *far_heads, _ = lax.optimization_barrier((*far_heads, near))
    last_pos, _ = lax.optimization_barrier((pos, near))
    weights = [own_w, join(last_pos, lines, swapped)]

    half = jax.ShapeDtypeStruct((HALF, QUARTER), BF16)
    full = jax.ShapeDtypeStruct((256, QUARTER), BF16)
    kept_shape = jax.ShapeDtypeStruct((256, QUARTER), F32)
    up, down = multiply(far_kernel, far_heads, weights, (), [half, half], "far")
    relays = (exchange(up, "x", 1), exchange(down, "x", 3))
    pos, _ = lax.optimization_barrier((pos, near))
    kept = attend(6, 2, pos, q, kv, got, prior_key, prior_value)
    kept_heads = [kept, *from_line([kept] * 3)]
    kept, *relays = lax.optimization_barrier((kept, *relays))
    up, down = multiply(near_kernel, near_heads, weights, relays, [full, full], "near")
    up, down = exchange(up, "x", 1), exchange(down, "x", 3)
    kept = multiply(keep_kernel, kept_heads, weights, (), kept_shape, "keep")
    own, *others = total_step(pos, kept, up, down)
    return finish(pos, own, *from_line(others), own_tokens, post_gain)


def solution(mesh):
    fine = Mesh(mesh.devices.reshape(4, 2, 4, 4), ("y", "c", "x", "z"))
    seq, tp = ("y", "c"), ("x", "z")
    inner = jax.shard_map(
        per_device,
        mesh=fine,
        in_specs=(
            P(seq, None), P(), P(None, tp), P(None, tp), P(None, tp), P(), P(),
            P(None, tp), P(None, tp), P(tp, None), P(), P(),
        ),
        out_specs=P(seq + tp, None),
        check_vma=False,
    )

    def run(*args):
        return inner(*args, jnp.asarray(rotary_table()))

    return run
```

```python
import functools

import jax
import jax.numpy as jnp
import numpy as np
from jax import lax
from jax.experimental import pallas as pl
from jax.experimental.pallas import tpu as pltpu
from jax.sharding import Mesh
from jax.sharding import PartitionSpec as P

MODEL_WIDTH = 5376
HQ = 32
HEAD = 128
WINDOW_SPAN = 1024
BLOCK_TOKENS = 8192
SHARD = 1024
EPSILON = 1e-06
LOG2E = 1.4426950408889634
SCORE_SCALE = float(MODEL_WIDTH // HQ) ** (-0.5)

F32 = jnp.float32
BF16 = jnp.bfloat16

ROWS = 256
GROUP = 16
HALF = 128
QUARTER = 1408
ROW_AT = 3


ANY = pl.BlockSpec(memory_space=pl.ANY)
VMEM = pl.BlockSpec(memory_space=pltpu.VMEM)
SMEM = pl.BlockSpec(memory_space=pltpu.SMEM)
SMALL = pl.CostEstimate(flops=0, bytes_accessed=0, transcendentals=0)
MEDIUM = pl.CostEstimate(flops=4_000_000_000, bytes_accessed=0, transcendentals=0)
LARGE = pl.CostEstimate(flops=30_000_000_000, bytes_accessed=0, transcendentals=0)


def rotary_table():
    half = HEAD // 2
    exponent = np.arange(half, dtype=np.float32) * np.float32(-2.0 / HEAD)
    frequency = np.power(np.float64(10000.0), exponent.astype(np.float64)).astype(np.float32)
    position = (WINDOW_SPAN + np.arange(BLOCK_TOKENS)).astype(np.float32)
    angle = (position[:, None] * frequency[None, :]).astype(np.float64)
    return np.concatenate([np.cos(angle), np.sin(angle)], axis=1).astype(np.float32)


def places():
    rows = []
    for device in range(128):
        seq, x, z = device // 16, device // 4 % 4, device % 4
        far, up, down = ((x + by) % 4 * 256 for by in (2, 1, 3))
        rows.append(
            [seq, z, seq % 2, far, far + 128, up, up + 128, down, down + 128, x * 256,
             x * 256 + 128, x]
        )
    return np.array(rows, np.int32)


def rotate(u, gain, table):
    swapped = pltpu.roll(table, 64, 1)
    low = lax.broadcasted_iota(jnp.int32, table.shape, 1) < 64
    cosine = jnp.where(low, table, swapped)
    sine = jnp.where(low, -swapped, table)
    mean = jnp.sum(u * u, axis=-1, keepdims=True) * (1.0 / HEAD)
    u = u * lax.rsqrt(mean + EPSILON) * gain
    return (u * cosine + pltpu.roll(u, 64, 1) * sine).astype(BF16)


def key_value_kernel(
    pos_ref, tok_ref, g_ref, wk_ref, wv_ref, gain_ref, tab_ref,
    normed, kv_ref, own_ref, w_all, g_all, sems,
):
    step = pl.program_id(0)
    copies = [
        pltpu.make_async_copy(wk_ref, w_all.at[:, 0:128], sems.at[0]),
        pltpu.make_async_copy(wv_ref, w_all.at[:, 128:256], sems.at[1]),
    ]
    blocks = MODEL_WIDTH // 128

    def norm_group(i, carry):
        at = i * GROUP if isinstance(i, int) else pl.multiple_of(i * GROUP, GROUP)
        rows = pl.ds(at, GROUP)
        parts = [jnp.zeros((GROUP, 128), F32) for _ in range(2)]
        for b in range(blocks):
            v = tok_ref[rows, b * 128 : (b + 1) * 128].astype(F32)
            parts[b % 2] = parts[b % 2] + v * v
        mean = jnp.sum(parts[0] + parts[1], axis=-1, keepdims=True) * (1.0 / MODEL_WIDTH)
        r = jnp.broadcast_to(lax.rsqrt(mean + EPSILON), (GROUP, 128))
        for b in range(blocks):
            cols = slice(b * 128, (b + 1) * 128)
            v = tok_ref[rows, cols].astype(F32)
            normed[rows, cols] = (v * r * g_all[:, cols]).astype(BF16)
        return carry

    def multiply_and_rotate():
        raw = jnp.dot(normed[...], w_all[...], preferred_element_type=F32)
        kv_ref[:, 0:128] = rotate(raw[:, 0:128], gain_ref[...], tab_ref[...])
        kv_ref[:, 128:256] = raw[:, 128:256].astype(BF16)

    @pl.when(step == 0)
    def _():
        for copy in copies:
            copy.start()
        g_all[...] = jnp.broadcast_to(g_ref[...], g_all.shape)
        lax.fori_loop(0, ROWS // GROUP, norm_group, 0, unroll=4)
        for copy in copies:
            copy.wait()
        multiply_and_rotate()

    @pl.when(step != 0)
    def _():
        for i in range(ROWS // GROUP):
            norm_group(i, 0)
        multiply_and_rotate()

    @pl.when(step == pos_ref[ROW_AT + 8])
    def _():
        own_ref[...] = tok_ref[pl.ds(pl.multiple_of(pos_ref[1] * 64, 64), 64), :]


def in_hbm(*arrays):
    return [pltpu.with_memory_space_constraint(array, pltpu.HBM) for array in arrays]


def whole(shape):
    return pl.BlockSpec(shape, lambda i, s: (0, 0))


def row_tile(width):
    return pl.BlockSpec((ROWS, width), lambda i, s: (i, 0))


TABLE_TILE = pl.BlockSpec((ROWS, 128), lambda i, s: (s[0] * (SHARD // ROWS) + i, 0))


def key_value(pos, tokens, pre_gain, wk, wv, gain, table):
    tokens, wk, wv, table = in_hbm(tokens, wk, wv, table)
    return pl.pallas_call(
        key_value_kernel,
        grid_spec=pltpu.PrefetchScalarGridSpec(
            num_scalar_prefetch=1,
            grid=(SHARD // ROWS,),
            in_specs=[
                row_tile(MODEL_WIDTH), whole((1, MODEL_WIDTH)), ANY, ANY,
                whole((1, 128)), TABLE_TILE,
            ],
            out_specs=[row_tile(MODEL_WIDTH), row_tile(256), whole((64, MODEL_WIDTH))],
            scratch_shapes=[
                pltpu.VMEM((MODEL_WIDTH, 256), BF16),
                pltpu.VMEM((GROUP, MODEL_WIDTH), F32),
                pltpu.SemaphoreType.DMA((2,)),
            ],
        ),
        out_shape=[
            jax.ShapeDtypeStruct((SHARD, MODEL_WIDTH), BF16),
            jax.ShapeDtypeStruct((SHARD, 256), BF16),
            jax.ShapeDtypeStruct((64, MODEL_WIDTH), BF16),
        ],
        compiler_params=pltpu.CompilerParams(vmem_limit_bytes=28 << 20),
        cost_estimate=pl.CostEstimate(
            flops=8 * SHARD * MODEL_WIDTH * 256, bytes_accessed=26 << 20, transcendentals=0
        ),
        name="key_value",
    )(pos, tokens, pre_gain.reshape(1, -1), wk, wv, gain.reshape(1, -1), table)


def query_kernel(pos_ref, normed_ref, w_ref, gain_ref, tab_ref, q_ref):
    raw = jnp.dot(normed_ref[...], w_ref[...], preferred_element_type=F32)
    q_ref[:, 0:128] = rotate(raw[:, 0:128], gain_ref[...], tab_ref[...])
    q_ref[:, 128:256] = rotate(raw[:, 128:256], gain_ref[...], tab_ref[...])


def query(pos, normed, wq, gain, table):
    (table,) = in_hbm(table)
    return pl.pallas_call(
        query_kernel,
        grid_spec=pltpu.PrefetchScalarGridSpec(
            num_scalar_prefetch=1,
            grid=(SHARD // ROWS,),
            in_specs=[
                row_tile(MODEL_WIDTH), whole((MODEL_WIDTH, 256)), whole((1, 128)), TABLE_TILE
            ],
            out_specs=row_tile(256),
        ),
        out_shape=jax.ShapeDtypeStruct((SHARD, 256), BF16),
        compiler_params=pltpu.CompilerParams(vmem_limit_bytes=24 << 20),
        cost_estimate=SMALL,
        name="query",
    )(pos, normed, wq, gain.reshape(1, -1), table)


def attend_kernel(first_part, pos_ref, q_ref, kv_ref, got_ref, pk_ref, pv_ref, out_ref, keys, values):
    @pl.when(pos_ref[0] == 0)
    def _():
        keys[0:SHARD] = pk_ref[...]
        values[0:SHARD, 0:128] = pv_ref[...]

    @pl.when(pos_ref[0] != 0)
    def _():
        keys[0:SHARD] = got_ref[:, 0:128]
        values[0:SHARD, 0:128] = got_ref[:, 128:256]

    keys[SHARD:] = kv_ref[:, 0:128]
    values[SHARD:, 0:128] = kv_ref[:, 128:256]
    values[:, 128:256] = jnp.ones((2 * SHARD, 128), BF16)

    span = HALF + WINDOW_SPAN
    row = lax.broadcasted_iota(jnp.int32, (2 * HALF, HALF), 0) % HALF
    col = lax.broadcasted_iota(jnp.int32, (2 * HALF, HALF), 1)
    lowest = jnp.float32(-jnp.inf)
    for part in range(out_ref.shape[0] // HALF):
        first = pl.multiple_of(pos_ref[ROW_AT + first_part + part], HALF)
        q = q_ref[pl.ds(first, HALF), :]
        q = jnp.concatenate([q[:, 0:128], q[:, 128:256]], axis=0)
        k = keys[pl.ds(first, span), :]
        scores = lax.dot_general(q, k, (((1,), (1,)), ((), ())), preferred_element_type=F32)
        scores = jnp.concatenate(
            [
                jnp.where(col > row, scores[:, 0:HALF], lowest),
                scores[:, HALF:WINDOW_SPAN],
                jnp.where(col <= row, scores[:, WINDOW_SPAN:], lowest),
            ],
            axis=1,
        )
        top = jnp.max(scores, axis=-1, keepdims=True)
        weights = jnp.exp2((scores - top) * (SCORE_SCALE * LOG2E)).astype(BF16)
        mixed = jnp.dot(weights, values[pl.ds(first, span), :], preferred_element_type=F32)
        mixed = (mixed[:, 0:128] / mixed[:, 128:256]).astype(BF16)
        out_ref[part * HALF : (part + 1) * HALF, 0:128] = mixed[0:HALF]
        out_ref[part * HALF : (part + 1) * HALF, 128:256] = mixed[HALF:]


def attend(first_part, parts, pos, q, kv, got, prior_k, prior_v, cost=SMALL):
    vmem = pl.BlockSpec(memory_space=pltpu.VMEM)
    return pl.pallas_call(
        functools.partial(attend_kernel, first_part),
        in_specs=[pl.BlockSpec(memory_space=pltpu.SMEM)] + [vmem] * 5,
        out_specs=vmem,
        out_shape=jax.ShapeDtypeStruct((parts * HALF, 256), BF16),
        scratch_shapes=[
            pltpu.VMEM((2 * SHARD, 128), BF16),
            pltpu.VMEM((2 * SHARD, 256), BF16),
        ],
        compiler_params=pltpu.CompilerParams(vmem_limit_bytes=32 << 20),
        cost_estimate=cost,
        name="attend",
    )(pos, q, kv, got, prior_k, prior_v)


def quarter_start(number):
    return pl.multiple_of((number * 21 // 2) * 128, 128)


def pick_kernel(pos_ref, w_ref, own_ref, next_ref, last_ref, far_ref, sems):
    z = pos_ref[1]
    rows = pl.ds(pl.multiple_of(pos_ref[2] * 128, 128), 128)
    copies = []
    for i, (shift, ref) in enumerate(((1, next_ref), (3, last_ref), (2, far_ref))):
        cols = pl.ds(quarter_start((z + shift) % 4), QUARTER)
        copies.append(pltpu.make_async_copy(w_ref.at[rows, cols], ref, sems.at[i]))
    cols = pl.ds(quarter_start(z), QUARTER)
    copies.append(pltpu.make_async_copy(w_ref.at[:, cols], own_ref, sems.at[3]))
    for copy in copies:
        copy.start()
    for copy in copies:
        copy.wait()


def pick(pos, w_out):
    part = jax.ShapeDtypeStruct((128, QUARTER), BF16)
    return pl.pallas_call(
        pick_kernel,
        in_specs=[SMEM, ANY],
        out_specs=[VMEM] * 4,
        out_shape=[jax.ShapeDtypeStruct((256, QUARTER), BF16), part, part, part],
        scratch_shapes=[pltpu.SemaphoreType.DMA((4,))],
        compiler_params=pltpu.CompilerParams(vmem_limit_bytes=16 << 20),
        cost_estimate=SMALL,
        name="pick",
    )(pos, *in_hbm(w_out))


def join_kernel(pos_ref, *refs):
    c, out_ref = pos_ref[2], refs[6]
    for i in range(3):
        out_ref[i, pl.ds(pl.multiple_of(c * 128, 128), 128)] = refs[i][...]
        out_ref[i, pl.ds(pl.multiple_of((1 - c) * 128, 128), 128)] = refs[3 + i][...]


def join(pos, lines, swapped):
    return pl.pallas_call(
        join_kernel,
        in_specs=[SMEM] + [VMEM] * 6,
        out_specs=VMEM,
        out_shape=jax.ShapeDtypeStruct((3, 256, QUARTER), BF16),
        compiler_params=pltpu.CompilerParams(vmem_limit_bytes=16 << 20),
        cost_estimate=SMALL,
        name="join",
    )(pos, *lines, *swapped)


def product(a_refs, w_refs, rows=slice(None)):
    out = jnp.dot(a_refs[0][rows, :], w_refs[0][...], preferred_element_type=F32)
    for i in range(3):
        out = out + jnp.dot(a_refs[1 + i][rows, :], w_refs[1][i], preferred_element_type=F32)
    return out


def far_kernel(*refs):
    out = product(refs[0:4], refs[4:6])
    refs[6][...] = out[0:HALF].astype(BF16)
    refs[7][...] = out[HALF:].astype(BF16)


def near_kernel(*refs):
    refs[6][...] = product(refs[0:4], refs[4:6], slice(0, 256)).astype(BF16)
    refs[7][...] = product(refs[0:4], refs[4:6], slice(256, 512)).astype(BF16)


def relay_kernel(relay_up, relay_down, up_in, down_in, up_ref, down_ref):
    up_ref[0:HALF] = (up_in[0:HALF].astype(F32) + relay_up[...].astype(F32)).astype(BF16)
    up_ref[HALF:] = up_in[HALF:]
    down_ref[0:HALF] = down_in[0:HALF]
    down_ref[HALF:] = (down_in[HALF:].astype(F32) + relay_down[...].astype(F32)).astype(BF16)


def relay(relays, up, down):
    return pl.pallas_call(
        relay_kernel,
        in_specs=[VMEM] * 4,
        out_specs=[VMEM] * 2,
        out_shape=[jax.ShapeDtypeStruct((256, QUARTER), BF16)] * 2,
        input_output_aliases={2: 0, 3: 1},
        compiler_params=pltpu.CompilerParams(vmem_limit_bytes=16 << 20),
        cost_estimate=SMALL,
        name="relay",
    )(*relays, up, down)


def keep_kernel(*refs):
    refs[6][...] = product(refs[0:4], refs[4:6])


def multiply(kernel, pieces, weights, out_shape, name, cost=SMALL):
    return pl.pallas_call(
        kernel,
        in_specs=[VMEM] * 6,
        out_specs=jax.tree.map(lambda _: VMEM, out_shape),
        out_shape=out_shape,
        compiler_params=pltpu.CompilerParams(vmem_limit_bytes=24 << 20),
        cost_estimate=cost,
        name=name,
    )(*pieces, *weights)


def total_kernel(pos_ref, kept_ref, up_ref, down_ref, own_ref, next_ref, last_ref, far_ref, total):
    z = pos_ref[1]
    total[...] = kept_ref[...] + up_ref[...].astype(F32) + down_ref[...].astype(F32)

    def rows(shift):
        return total[pl.ds(pl.multiple_of(((z + shift) % 4) * 64, 64), 64), :]

    next_ref[...] = rows(1).astype(BF16)
    last_ref[...] = rows(3).astype(BF16)
    far_ref[...] = rows(2).astype(BF16)
    own_ref[...] = rows(0)


def total_step(pos, kept, up, down):
    part = jax.ShapeDtypeStruct((64, QUARTER), BF16)
    return pl.pallas_call(
        total_kernel,
        in_specs=[SMEM] + [VMEM] * 3,
        out_specs=[VMEM] * 4,
        out_shape=[jax.ShapeDtypeStruct((64, QUARTER), F32), part, part, part],
        scratch_shapes=[pltpu.VMEM((256, QUARTER), F32)],
        compiler_params=pltpu.CompilerParams(vmem_limit_bytes=32 << 20),
        cost_estimate=SMALL,
        name="total_step",
    )(pos, kept, up, down)


def finish_kernel(pos_ref, own_ref, next_ref, last_ref, far_ref, tok_ref, g_ref, out_ref, line):
    z = pos_ref[1]
    for shift, ref in ((0, own_ref), (3, next_ref), (1, last_ref), (2, far_ref)):
        line[:, pl.ds(quarter_start((z + shift) % 4), QUARTER)] = ref[...].astype(F32)
    for i in range(4):
        rows = slice(i * 16, (i + 1) * 16)
        total = jnp.zeros((16, 128), F32)
        for b in range(MODEL_WIDTH // 128):
            part = line[rows, b * 128 : (b + 1) * 128]
            total = total + part * part
        mean = jnp.sum(total, axis=-1, keepdims=True) * (1.0 / MODEL_WIDTH)
        r = jnp.broadcast_to(lax.rsqrt(mean + EPSILON), (16, 128))
        for b in range(MODEL_WIDTH // 128):
            cols = slice(b * 128, (b + 1) * 128)
            normed = line[rows, cols] * r * g_ref[:, cols]
            out_ref[rows, cols] = (tok_ref[rows, cols].astype(F32) + normed).astype(BF16)


def finish(pos, own, nxt, last, far, own_tokens, gain):
    return pl.pallas_call(
        finish_kernel,
        in_specs=[SMEM] + [VMEM] * 6,
        out_specs=VMEM,
        out_shape=jax.ShapeDtypeStruct((64, MODEL_WIDTH), BF16),
        scratch_shapes=[pltpu.VMEM((64, MODEL_WIDTH), F32)],
        compiler_params=pltpu.CompilerParams(vmem_limit_bytes=16 << 20),
        cost_estimate=SMALL,
        name="finish",
    )(pos, own, nxt, last, far, own_tokens, gain.reshape(1, -1))


def shift_by(array, axis, steps):
    return lax.ppermute(array, axis, [(i, (i + steps) % 4) for i in range(4)])


def from_line(pieces):
    return [shift_by(piece, "z", by) for piece, by in zip(pieces, (1, 3, 2), strict=True)]


def per_device(
    tokens, pre_gain, w_query, key_weight, value_weight, query_gain, key_gain,
    prior_key, prior_value, w_out, post_gain, table,
):
    device = lax.axis_index(("y", "c", "x", "z"))
    pos = lax.dynamic_slice_in_dim(jnp.asarray(places()), device, 1, 0).reshape(-1)
    own_w, *parts = pick(pos, w_out)
    pos, *parts = lax.optimization_barrier((pos, *parts))
    lines = from_line(parts)
    normed, kv, own_tokens = key_value(
        pos, tokens, pre_gain, key_weight, value_weight, key_gain, table
    )
    got = lax.ppermute(kv, ("y", "c"), [(i, i + 1) for i in range(7)])
    q = query(pos, normed, w_query, query_gain, table)
    q, *lines = lax.optimization_barrier((q, *lines))
    swapped = [lax.ppermute(part, "c", [(0, 1), (1, 0)]) for part in lines]
    pos, *swapped = lax.optimization_barrier((pos, *swapped))

    far = attend(0, 2, pos, q, kv, got, prior_key, prior_value)
    far_heads = [far, *from_line([far] * 3)]
    pos, _ = lax.optimization_barrier((pos, far))
    near = attend(2, 4, pos, q, kv, got, prior_key, prior_value)
    near_heads = [near, *from_line([near] * 3)]
    *far_heads, _ = lax.optimization_barrier((*far_heads, near))
    last_pos, _ = lax.optimization_barrier((pos, near))
    weights = [own_w, join(last_pos, lines, swapped)]

    half = jax.ShapeDtypeStruct((HALF, QUARTER), BF16)
    full = jax.ShapeDtypeStruct((256, QUARTER), BF16)
    kept_shape = jax.ShapeDtypeStruct((256, QUARTER), F32)
    up, down = multiply(far_kernel, far_heads, weights, [half, half], "far")
    relays = (shift_by(up, "x", 1), shift_by(down, "x", 3))
    pos, *_ = lax.optimization_barrier((pos, near, up))
    kept = attend(6, 2, pos, q, kv, got, prior_key, prior_value, MEDIUM)
    kept_heads = [kept, *from_line([kept] * 3)]
    *near_heads, _ = lax.optimization_barrier((*near_heads, kept))
    up, down = multiply(near_kernel, near_heads, weights, [full, full], "near", LARGE)
    up, down = relay(relays, up, down)
    up, down = shift_by(up, "x", 1), shift_by(down, "x", 3)
    kept = multiply(keep_kernel, kept_heads, weights, kept_shape, "keep")
    own, *others = total_step(pos, kept, up, down)
    return finish(pos, own, *from_line(others), own_tokens, post_gain)


def solution(mesh):
    fine = Mesh(mesh.devices.reshape(4, 2, 4, 4), ("y", "c", "x", "z"))
    seq, tp = ("y", "c"), ("x", "z")
    inner = jax.shard_map(
        per_device,
        mesh=fine,
        in_specs=(
            P(seq, None), P(), P(None, tp), P(None, tp), P(None, tp), P(), P(),
            P(None, tp), P(None, tp), P(tp, None), P(), P(),
        ),
        out_specs=P(seq + tp, None),
        check_vma=False,
    )

    def run(*args):
        return inner(*args, jnp.asarray(rotary_table()))

    return run
```

```python
import functools

import jax
import jax.numpy as jnp
import numpy as np
from jax import lax
from jax.experimental import pallas as pl
from jax.experimental.pallas import tpu as pltpu
from jax.sharding import Mesh
from jax.sharding import PartitionSpec as P

MODEL_WIDTH = 5376
HQ = 32
HEAD = 128
WINDOW_SPAN = 1024
BLOCK_TOKENS = 8192
SHARD = 1024
EPSILON = 1e-06
LOG2E = 1.4426950408889634
SCORE_SCALE = float(MODEL_WIDTH // HQ) ** (-0.5)

F32 = jnp.float32
BF16 = jnp.bfloat16

ROWS = 256
GROUP = 16
HALF = 128
QUARTER = 1408
ROW_AT = 3


ANY = pl.BlockSpec(memory_space=pl.ANY)
VMEM = pl.BlockSpec(memory_space=pltpu.VMEM)
SMEM = pl.BlockSpec(memory_space=pltpu.SMEM)
SMALL = pl.CostEstimate(flops=0, bytes_accessed=0, transcendentals=0)
MEDIUM = pl.CostEstimate(flops=4_000_000_000, bytes_accessed=0, transcendentals=0)
LARGE = pl.CostEstimate(flops=30_000_000_000, bytes_accessed=0, transcendentals=0)


def rotary_table():
    half = HEAD // 2
    exponent = np.arange(half, dtype=np.float32) * np.float32(-2.0 / HEAD)
    frequency = np.power(np.float64(10000.0), exponent.astype(np.float64)).astype(np.float32)
    position = (WINDOW_SPAN + np.arange(BLOCK_TOKENS)).astype(np.float32)
    angle = (position[:, None] * frequency[None, :]).astype(np.float64)
    return np.concatenate([np.cos(angle), np.sin(angle)], axis=1).astype(np.float32)


def places():
    rows = []
    for device in range(128):
        seq, x, z = device // 16, device // 4 % 4, device % 4
        far, up, down = ((x + by) % 4 * 256 for by in (2, 1, 3))
        rows.append(
            [seq, z, seq % 2, far, far + 128, up, up + 128, down, down + 128, x * 256,
             x * 256 + 128, x]
        )
    return np.array(rows, np.int32)


def rotate(u, gain, table):
    swapped = pltpu.roll(table, 64, 1)
    low = lax.broadcasted_iota(jnp.int32, table.shape, 1) < 64
    cosine = jnp.where(low, table, swapped)
    sine = jnp.where(low, -swapped, table)
    mean = jnp.sum(u * u, axis=-1, keepdims=True) * (1.0 / HEAD)
    u = u * lax.rsqrt(mean + EPSILON) * gain
    return (u * cosine + pltpu.roll(u, 64, 1) * sine).astype(BF16)


def table_copy(pos_ref, tab_ref, table, sem):
    rows = pl.ds(pl.multiple_of(pos_ref[0] * SHARD, SHARD), SHARD)
    return pltpu.make_async_copy(tab_ref.at[rows], table, sem)


def key_value_kernel(
    pos_ref, tok_ref, g_ref, wk_ref, wv_ref, gain_ref, tab_ref,
    normed, kv_ref, own_ref, tok, w_all, g_all, table, sems, tok_sems,
):
    copies = [
        pltpu.make_async_copy(wk_ref, w_all.at[:, 0:128], sems.at[0]),
        pltpu.make_async_copy(wv_ref, w_all.at[:, 128:256], sems.at[1]),
        table_copy(pos_ref, tab_ref, table, sems.at[2]),
    ]

    def tile_copy(i):
        rows = pl.ds(pl.multiple_of(i * ROWS, ROWS), ROWS)
        return pltpu.make_async_copy(tok_ref.at[rows], tok.at[rows], tok_sems.at[i])

    tile_copy(0).start()
    for copy in copies:
        copy.start()
    for i in range(1, SHARD // ROWS):
        tile_copy(i).start()
    g_all[...] = jnp.broadcast_to(g_ref[...], g_all.shape)
    blocks = MODEL_WIDTH // 128

    def norm_group(first):
        rows = pl.ds(pl.multiple_of(first, GROUP), GROUP)
        parts = [jnp.zeros((GROUP, 128), F32) for _ in range(2)]
        for b in range(blocks):
            v = tok[rows, b * 128 : (b + 1) * 128].astype(F32)
            parts[b % 2] = parts[b % 2] + v * v
        mean = jnp.sum(parts[0] + parts[1], axis=-1, keepdims=True) * (1.0 / MODEL_WIDTH)
        r = jnp.broadcast_to(lax.rsqrt(mean + EPSILON), (GROUP, 128))
        for b in range(blocks):
            cols = slice(b * 128, (b + 1) * 128)
            v = tok[rows, cols].astype(F32)
            normed[rows, cols] = (v * r * g_all[:, cols]).astype(BF16)

    def tile(i, carry):
        tile_copy(i).wait()
        for j in range(ROWS // GROUP):
            norm_group(i * ROWS + j * GROUP)

        @pl.when(i == 0)
        def _():
            for copy in copies:
                copy.wait()

        rows = pl.ds(pl.multiple_of(i * ROWS, ROWS), ROWS)
        raw = jnp.dot(normed[rows, :], w_all[...], preferred_element_type=F32)
        kv_ref[rows, 0:128] = rotate(raw[:, 0:128], gain_ref[...], table[rows, :])
        kv_ref[rows, 128:256] = raw[:, 128:256].astype(BF16)
        return carry

    lax.fori_loop(0, SHARD // ROWS, tile, 0)
    first = pos_ref[ROW_AT + 8] * ROWS + pos_ref[1] * 64
    own_ref[...] = tok[pl.ds(pl.multiple_of(first, 64), 64), :]


def in_hbm(*arrays):
    return [pltpu.with_memory_space_constraint(array, pltpu.HBM) for array in arrays]


def key_value(pos, tokens, pre_gain, wk, wv, gain, table):
    tokens, wk, wv, table = in_hbm(tokens, wk, wv, table)
    return pl.pallas_call(
        key_value_kernel,
        in_specs=[SMEM, ANY, VMEM, ANY, ANY, VMEM, ANY],
        out_specs=[VMEM] * 3,
        out_shape=[
            jax.ShapeDtypeStruct((SHARD, MODEL_WIDTH), BF16),
            jax.ShapeDtypeStruct((SHARD, 256), BF16),
            jax.ShapeDtypeStruct((64, MODEL_WIDTH), BF16),
        ],
        scratch_shapes=[
            pltpu.VMEM((SHARD, MODEL_WIDTH), BF16),
            pltpu.VMEM((MODEL_WIDTH, 256), BF16),
            pltpu.VMEM((GROUP, MODEL_WIDTH), F32),
            pltpu.VMEM((SHARD, 128), F32),
            pltpu.SemaphoreType.DMA((3,)),
            pltpu.SemaphoreType.DMA((SHARD // ROWS,)),
        ],
        compiler_params=pltpu.CompilerParams(vmem_limit_bytes=34 << 20),
        cost_estimate=pl.CostEstimate(
            flops=8 * SHARD * MODEL_WIDTH * 256, bytes_accessed=26 << 20, transcendentals=0
        ),
        name="key_value",
    )(pos, tokens, pre_gain.reshape(1, -1), wk, wv, gain.reshape(1, -1), table)


def query_kernel(pos_ref, normed_ref, w_ref, gain_ref, tab_ref, q_ref, table, sem):
    copy = table_copy(pos_ref, tab_ref, table, sem)
    copy.start()
    copy.wait()
    for i in range(SHARD // ROWS):
        rows = slice(i * ROWS, (i + 1) * ROWS)
        raw = jnp.dot(normed_ref[rows, :], w_ref[...], preferred_element_type=F32)
        q_ref[rows, 0:128] = rotate(raw[:, 0:128], gain_ref[...], table[rows, :])
        q_ref[rows, 128:256] = rotate(raw[:, 128:256], gain_ref[...], table[rows, :])


def query(pos, normed, wq, gain, table):
    (table,) = in_hbm(table)
    return pl.pallas_call(
        query_kernel,
        in_specs=[SMEM, VMEM, VMEM, VMEM, ANY],
        out_specs=VMEM,
        out_shape=jax.ShapeDtypeStruct((SHARD, 256), BF16),
        scratch_shapes=[pltpu.VMEM((SHARD, 128), F32), pltpu.SemaphoreType.DMA(())],
        compiler_params=pltpu.CompilerParams(vmem_limit_bytes=24 << 20),
        cost_estimate=SMALL,
        name="query",
    )(pos, normed, wq, gain.reshape(1, -1), table)


def attend_kernel(first_part, pos_ref, q_ref, kv_ref, got_ref, pk_ref, pv_ref, out_ref, keys, values):
    @pl.when(pos_ref[0] == 0)
    def _():
        keys[0:SHARD] = pk_ref[...]
        values[0:SHARD, 0:128] = pv_ref[...]

    @pl.when(pos_ref[0] != 0)
    def _():
        keys[0:SHARD] = got_ref[:, 0:128]
        values[0:SHARD, 0:128] = got_ref[:, 128:256]

    keys[SHARD:] = kv_ref[:, 0:128]
    values[SHARD:, 0:128] = kv_ref[:, 128:256]
    values[:, 128:256] = jnp.ones((2 * SHARD, 128), BF16)

    span = HALF + WINDOW_SPAN
    row = lax.broadcasted_iota(jnp.int32, (2 * HALF, HALF), 0) % HALF
    col = lax.broadcasted_iota(jnp.int32, (2 * HALF, HALF), 1)
    lowest = jnp.float32(-jnp.inf)
    for part in range(out_ref.shape[0] // HALF):
        first = pl.multiple_of(pos_ref[ROW_AT + first_part + part], HALF)
        q = q_ref[pl.ds(first, HALF), :]
        q = jnp.concatenate([q[:, 0:128], q[:, 128:256]], axis=0)
        k = keys[pl.ds(first, span), :]
        scores = lax.dot_general(q, k, (((1,), (1,)), ((), ())), preferred_element_type=F32)
        scores = jnp.concatenate(
            [
                jnp.where(col > row, scores[:, 0:HALF], lowest),
                scores[:, HALF:WINDOW_SPAN],
                jnp.where(col <= row, scores[:, WINDOW_SPAN:], lowest),
            ],
            axis=1,
        )
        top = jnp.max(scores, axis=-1, keepdims=True)
        weights = jnp.exp2((scores - top) * (SCORE_SCALE * LOG2E)).astype(BF16)
        mixed = jnp.dot(weights, values[pl.ds(first, span), :], preferred_element_type=F32)
        mixed = (mixed[:, 0:128] / mixed[:, 128:256]).astype(BF16)
        out_ref[part * HALF : (part + 1) * HALF, 0:128] = mixed[0:HALF]
        out_ref[part * HALF : (part + 1) * HALF, 128:256] = mixed[HALF:]


def attend(first_part, parts, pos, q, kv, got, prior_k, prior_v, cost=SMALL):
    vmem = pl.BlockSpec(memory_space=pltpu.VMEM)
    return pl.pallas_call(
        functools.partial(attend_kernel, first_part),
        in_specs=[pl.BlockSpec(memory_space=pltpu.SMEM)] + [vmem] * 5,
        out_specs=vmem,
        out_shape=jax.ShapeDtypeStruct((parts * HALF, 256), BF16),
        scratch_shapes=[
            pltpu.VMEM((2 * SHARD, 128), BF16),
            pltpu.VMEM((2 * SHARD, 256), BF16),
        ],
        compiler_params=pltpu.CompilerParams(vmem_limit_bytes=32 << 20),
        cost_estimate=cost,
        name="attend",
    )(pos, q, kv, got, prior_k, prior_v)


def quarter_start(number):
    return pl.multiple_of((number * 21 // 2) * 128, 128)


def pick_kernel(pos_ref, w_ref, own_ref, next_ref, last_ref, far_ref, sems):
    z = pos_ref[1]
    rows = pl.ds(pl.multiple_of(pos_ref[2] * 128, 128), 128)
    copies = []
    for i, (shift, ref) in enumerate(((1, next_ref), (3, last_ref), (2, far_ref))):
        cols = pl.ds(quarter_start((z + shift) % 4), QUARTER)
        copies.append(pltpu.make_async_copy(w_ref.at[rows, cols], ref, sems.at[i]))
    cols = pl.ds(quarter_start(z), QUARTER)
    copies.append(pltpu.make_async_copy(w_ref.at[:, cols], own_ref, sems.at[3]))
    for copy in copies:
        copy.start()
    for copy in copies:
        copy.wait()


def pick(pos, w_out):
    part = jax.ShapeDtypeStruct((128, QUARTER), BF16)
    return pl.pallas_call(
        pick_kernel,
        in_specs=[SMEM, ANY],
        out_specs=[VMEM] * 4,
        out_shape=[jax.ShapeDtypeStruct((256, QUARTER), BF16), part, part, part],
        scratch_shapes=[pltpu.SemaphoreType.DMA((4,))],
        compiler_params=pltpu.CompilerParams(vmem_limit_bytes=16 << 20),
        cost_estimate=SMALL,
        name="pick",
    )(pos, *in_hbm(w_out))


def join_kernel(pos_ref, *refs):
    c, out_ref = pos_ref[2], refs[6]
    for i in range(3):
        out_ref[i, pl.ds(pl.multiple_of(c * 128, 128), 128)] = refs[i][...]
        out_ref[i, pl.ds(pl.multiple_of((1 - c) * 128, 128), 128)] = refs[3 + i][...]


def join(pos, lines, swapped):
    return pl.pallas_call(
        join_kernel,
        in_specs=[SMEM] + [VMEM] * 6,
        out_specs=VMEM,
        out_shape=jax.ShapeDtypeStruct((3, 256, QUARTER), BF16),
        compiler_params=pltpu.CompilerParams(vmem_limit_bytes=16 << 20),
        cost_estimate=SMALL,
        name="join",
    )(pos, *lines, *swapped)


def product(a_refs, w_refs, rows=slice(None)):
    out = jnp.dot(a_refs[0][rows, :], w_refs[0][...], preferred_element_type=F32)
    for i in range(3):
        out = out + jnp.dot(a_refs[1 + i][rows, :], w_refs[1][i], preferred_element_type=F32)
    return out


def far_kernel(*refs):
    out = product(refs[0:4], refs[4:6])
    refs[6][...] = out[0:HALF].astype(BF16)
    refs[7][...] = out[HALF:].astype(BF16)


def near_kernel(*refs):
    refs[6][...] = product(refs[0:4], refs[4:6], slice(0, 256)).astype(BF16)
    refs[7][...] = product(refs[0:4], refs[4:6], slice(256, 512)).astype(BF16)


def relay_kernel(relay_up, relay_down, up_in, down_in, up_ref, down_ref):
    up_ref[0:HALF] = (up_in[0:HALF].astype(F32) + relay_up[...].astype(F32)).astype(BF16)
    up_ref[HALF:] = up_in[HALF:]
    down_ref[0:HALF] = down_in[0:HALF]
    down_ref[HALF:] = (down_in[HALF:].astype(F32) + relay_down[...].astype(F32)).astype(BF16)


def relay(relays, up, down):
    return pl.pallas_call(
        relay_kernel,
        in_specs=[VMEM] * 4,
        out_specs=[VMEM] * 2,
        out_shape=[jax.ShapeDtypeStruct((256, QUARTER), BF16)] * 2,
        input_output_aliases={2: 0, 3: 1},
        compiler_params=pltpu.CompilerParams(vmem_limit_bytes=16 << 20),
        cost_estimate=SMALL,
        name="relay",
    )(*relays, up, down)


def keep_kernel(*refs):
    refs[6][...] = product(refs[0:4], refs[4:6])


def multiply(kernel, pieces, weights, out_shape, name, cost=SMALL):
    return pl.pallas_call(
        kernel,
        in_specs=[VMEM] * 6,
        out_specs=jax.tree.map(lambda _: VMEM, out_shape),
        out_shape=out_shape,
        compiler_params=pltpu.CompilerParams(vmem_limit_bytes=24 << 20),
        cost_estimate=cost,
        name=name,
    )(*pieces, *weights)


def total_kernel(pos_ref, kept_ref, up_ref, down_ref, own_ref, next_ref, last_ref, far_ref, total):
    z = pos_ref[1]
    total[...] = kept_ref[...] + up_ref[...].astype(F32) + down_ref[...].astype(F32)

    def rows(shift):
        return total[pl.ds(pl.multiple_of(((z + shift) % 4) * 64, 64), 64), :]

    next_ref[...] = rows(1).astype(BF16)
    last_ref[...] = rows(3).astype(BF16)
    far_ref[...] = rows(2).astype(BF16)
    own_ref[...] = rows(0)


def total_step(pos, kept, up, down):
    part = jax.ShapeDtypeStruct((64, QUARTER), BF16)
    return pl.pallas_call(
        total_kernel,
        in_specs=[SMEM] + [VMEM] * 3,
        out_specs=[VMEM] * 4,
        out_shape=[jax.ShapeDtypeStruct((64, QUARTER), F32), part, part, part],
        scratch_shapes=[pltpu.VMEM((256, QUARTER), F32)],
        compiler_params=pltpu.CompilerParams(vmem_limit_bytes=32 << 20),
        cost_estimate=SMALL,
        name="total_step",
    )(pos, kept, up, down)


def finish_kernel(pos_ref, own_ref, far_ref, last_ref, next_ref, tok_ref, g_ref, out_ref, line):
    z = pos_ref[1]
    for shift, ref in ((0, own_ref), (2, far_ref), (3, last_ref), (1, next_ref)):
        line[:, pl.ds(quarter_start((z + shift) % 4), QUARTER)] = ref[...].astype(F32)
    for i in range(4):
        rows = slice(i * 16, (i + 1) * 16)
        total = jnp.zeros((16, 128), F32)
        for b in range(MODEL_WIDTH // 128):
            part = line[rows, b * 128 : (b + 1) * 128]
            total = total + part * part
        mean = jnp.sum(total, axis=-1, keepdims=True) * (1.0 / MODEL_WIDTH)
        r = jnp.broadcast_to(lax.rsqrt(mean + EPSILON), (16, 128))
        for b in range(MODEL_WIDTH // 128):
            cols = slice(b * 128, (b + 1) * 128)
            normed = line[rows, cols] * r * g_ref[:, cols]
            out_ref[rows, cols] = (tok_ref[rows, cols].astype(F32) + normed).astype(BF16)


def finish(pos, own, far, last, nxt, own_tokens, gain):
    return pl.pallas_call(
        finish_kernel,
        in_specs=[SMEM] + [VMEM] * 6,
        out_specs=VMEM,
        out_shape=jax.ShapeDtypeStruct((64, MODEL_WIDTH), BF16),
        scratch_shapes=[pltpu.VMEM((64, MODEL_WIDTH), F32)],
        compiler_params=pltpu.CompilerParams(vmem_limit_bytes=16 << 20),
        cost_estimate=SMALL,
        name="finish",
    )(pos, own, far, last, nxt, own_tokens, gain.reshape(1, -1))


def shift_by(array, axis, steps):
    return lax.ppermute(array, axis, [(i, (i + steps) % 4) for i in range(4)])


def from_line(pieces):
    after, before, across = pieces
    return [shift_by(across, "z", 2), shift_by(after, "z", 1), shift_by(before, "z", 3)]


def per_device(
    tokens, pre_gain, w_query, key_weight, value_weight, query_gain, key_gain,
    prior_key, prior_value, w_out, post_gain, table,
):
    device = lax.axis_index(("y", "c", "x", "z"))
    pos = lax.dynamic_slice_in_dim(jnp.asarray(places()), device, 1, 0).reshape(-1)
    own_w, *parts = pick(pos, w_out)
    pos, *parts = lax.optimization_barrier((pos, *parts))
    lines = from_line(parts)
    normed, kv, own_tokens = key_value(
        pos, tokens, pre_gain, key_weight, value_weight, key_gain, table
    )
    got = lax.ppermute(kv, ("y", "c"), [(i, i + 1) for i in range(7)])
    q = query(pos, normed, w_query, query_gain, table)
    q, *lines = lax.optimization_barrier((q, *lines))
    swapped = [lax.ppermute(part, "c", [(0, 1), (1, 0)]) for part in lines]
    pos, *swapped = lax.optimization_barrier((pos, *swapped))

    far = attend(0, 2, pos, q, kv, got, prior_key, prior_value)
    far_heads = [far, *from_line([far] * 3)]
    pos, _ = lax.optimization_barrier((pos, far))
    near = attend(2, 4, pos, q, kv, got, prior_key, prior_value)
    near_heads = [near, *from_line([near] * 3)]
    *far_heads, _ = lax.optimization_barrier((*far_heads, near))
    last_pos, _ = lax.optimization_barrier((pos, near))
    weights = [own_w, join(last_pos, lines, swapped)]

    half = jax.ShapeDtypeStruct((HALF, QUARTER), BF16)
    full = jax.ShapeDtypeStruct((256, QUARTER), BF16)
    kept_shape = jax.ShapeDtypeStruct((256, QUARTER), F32)
    up, down = multiply(far_kernel, far_heads, weights, [half, half], "far")
    relays = (shift_by(up, "x", 1), shift_by(down, "x", 3))
    pos, *_ = lax.optimization_barrier((pos, near, up))
    kept = attend(6, 2, pos, q, kv, got, prior_key, prior_value, MEDIUM)
    kept_heads = [kept, *from_line([kept] * 3)]
    *near_heads, _ = lax.optimization_barrier((*near_heads, kept))
    up, down = multiply(near_kernel, near_heads, weights, [full, full], "near", LARGE)
    up, down = relay(relays, up, down)
    up, down = shift_by(up, "x", 1), shift_by(down, "x", 3)
    kept = multiply(keep_kernel, kept_heads, weights, kept_shape, "keep")
    own, *others = total_step(pos, kept, up, down)
    return finish(pos, own, *from_line(others), own_tokens, post_gain)


def solution(mesh):
    fine = Mesh(mesh.devices.reshape(4, 2, 4, 4), ("y", "c", "x", "z"))
    seq, tp = ("y", "c"), ("x", "z")
    inner = jax.shard_map(
        per_device,
        mesh=fine,
        in_specs=(
            P(seq, None), P(), P(None, tp), P(None, tp), P(None, tp), P(), P(),
            P(None, tp), P(None, tp), P(tp, None), P(), P(),
        ),
        out_specs=P(seq + tp, None),
        check_vma=False,
    )

    def run(*args):
        return inner(*args, jnp.asarray(rotary_table()))

    return run
```

```python
import functools

import jax
import jax.numpy as jnp
import numpy as np
from jax import lax
from jax.experimental import pallas as pl
from jax.experimental.pallas import tpu as pltpu
from jax.sharding import Mesh
from jax.sharding import PartitionSpec as P

MODEL_WIDTH = 5376
HQ = 32
HEAD = 128
WINDOW_SPAN = 1024
BLOCK_TOKENS = 8192
SHARD = 1024
EPSILON = 1e-06
LOG2E = 1.4426950408889634
SCORE_SCALE = float(MODEL_WIDTH // HQ) ** (-0.5)

F32 = jnp.float32
BF16 = jnp.bfloat16

ROWS = 256
GROUP = 16
HALF = 128
QUARTER = 1408
ROW_AT = 3


ANY = pl.BlockSpec(memory_space=pl.ANY)
VMEM = pl.BlockSpec(memory_space=pltpu.VMEM)
SMEM = pl.BlockSpec(memory_space=pltpu.SMEM)
SMALL = pl.CostEstimate(flops=0, bytes_accessed=0, transcendentals=0)
MEDIUM = pl.CostEstimate(flops=4_000_000_000, bytes_accessed=0, transcendentals=0)
LARGE = pl.CostEstimate(flops=30_000_000_000, bytes_accessed=0, transcendentals=0)


def rotary_table():
    half = HEAD // 2
    exponent = np.arange(half, dtype=np.float32) * np.float32(-2.0 / HEAD)
    frequency = np.power(np.float64(10000.0), exponent.astype(np.float64)).astype(np.float32)
    position = (WINDOW_SPAN + np.arange(BLOCK_TOKENS)).astype(np.float32)
    angle = (position[:, None] * frequency[None, :]).astype(np.float64)
    return np.concatenate([np.cos(angle), np.sin(angle)], axis=1).astype(np.float32)


def places():
    rows = []
    for device in range(128):
        seq, x, z = device // 16, device // 4 % 4, device % 4
        far, up, down = ((x + by) % 4 * 256 for by in (2, 1, 3))
        rows.append(
            [seq, z, seq % 2, far, far + 128, up, up + 128, down, down + 128, x * 256,
             x * 256 + 128, x]
        )
    return np.array(rows, np.int32)


def rotate(u, gain, table):
    swapped = pltpu.roll(table, 64, 1)
    low = lax.broadcasted_iota(jnp.int32, table.shape, 1) < 64
    cosine = jnp.where(low, table, swapped)
    sine = jnp.where(low, -swapped, table)
    mean = jnp.sum(u * u, axis=-1, keepdims=True) * (1.0 / HEAD)
    u = u * lax.rsqrt(mean + EPSILON) * gain
    return (u * cosine + pltpu.roll(u, 64, 1) * sine).astype(BF16)


def key_value_kernel(
    pos_ref, tok_ref, g_ref, wk_ref, wv_ref, gain_ref, tab_ref,
    normed, kv_ref, own_ref, w_all, g_all, sems,
):
    step = pl.program_id(0)
    copies = [
        pltpu.make_async_copy(wk_ref, w_all.at[:, 0:128], sems.at[0]),
        pltpu.make_async_copy(wv_ref, w_all.at[:, 128:256], sems.at[1]),
    ]
    blocks = MODEL_WIDTH // 128

    def norm_group(i, carry):
        at = i * GROUP if isinstance(i, int) else pl.multiple_of(i * GROUP, GROUP)
        rows = pl.ds(at, GROUP)
        parts = [jnp.zeros((GROUP, 128), F32) for _ in range(2)]
        for b in range(blocks):
            v = tok_ref[rows, b * 128 : (b + 1) * 128].astype(F32)
            parts[b % 2] = parts[b % 2] + v * v
        mean = jnp.sum(parts[0] + parts[1], axis=-1, keepdims=True) * (1.0 / MODEL_WIDTH)
        r = jnp.broadcast_to(lax.rsqrt(mean + EPSILON), (GROUP, 128))
        for b in range(blocks):
            cols = slice(b * 128, (b + 1) * 128)
            v = tok_ref[rows, cols].astype(F32)
            normed[rows, cols] = (v * r * g_all[:, cols]).astype(BF16)
        return carry

    def multiply_and_rotate():
        raw = jnp.dot(normed[...], w_all[...], preferred_element_type=F32)
        kv_ref[:, 0:128] = rotate(raw[:, 0:128], gain_ref[...], tab_ref[...])
        kv_ref[:, 128:256] = raw[:, 128:256].astype(BF16)

    @pl.when(step == 0)
    def _():
        for copy in copies:
            copy.start()
        g_all[...] = jnp.broadcast_to(g_ref[...], g_all.shape)
        lax.fori_loop(0, ROWS // GROUP, norm_group, 0, unroll=4)
        for copy in copies:
            copy.wait()
        multiply_and_rotate()

    @pl.when(step != 0)
    def _():
        for i in range(ROWS // GROUP):
            norm_group(i, 0)
        multiply_and_rotate()

    @pl.when(step == pos_ref[ROW_AT + 8])
    def _():
        own_ref[...] = tok_ref[pl.ds(pl.multiple_of(pos_ref[1] * 64, 64), 64), :]


def in_hbm(*arrays):
    return [pltpu.with_memory_space_constraint(array, pltpu.HBM) for array in arrays]


def whole(shape):
    return pl.BlockSpec(shape, lambda i, s: (0, 0))


def row_tile(width):
    return pl.BlockSpec((ROWS, width), lambda i, s: (i, 0))


TABLE_TILE = pl.BlockSpec((ROWS, 128), lambda i, s: (s[0] * (SHARD // ROWS) + i, 0))


def key_value(pos, tokens, pre_gain, wk, wv, gain, table):
    tokens, wk, wv, table = in_hbm(tokens, wk, wv, table)
    return pl.pallas_call(
        key_value_kernel,
        grid_spec=pltpu.PrefetchScalarGridSpec(
            num_scalar_prefetch=1,
            grid=(SHARD // ROWS,),
            in_specs=[
                row_tile(MODEL_WIDTH), whole((1, MODEL_WIDTH)), ANY, ANY,
                whole((1, 128)), TABLE_TILE,
            ],
            out_specs=[row_tile(MODEL_WIDTH), row_tile(256), whole((64, MODEL_WIDTH))],
            scratch_shapes=[
                pltpu.VMEM((MODEL_WIDTH, 256), BF16),
                pltpu.VMEM((GROUP, MODEL_WIDTH), F32),
                pltpu.SemaphoreType.DMA((2,)),
            ],
        ),
        out_shape=[
            jax.ShapeDtypeStruct((SHARD, MODEL_WIDTH), BF16),
            jax.ShapeDtypeStruct((SHARD, 256), BF16),
            jax.ShapeDtypeStruct((64, MODEL_WIDTH), BF16),
        ],
        compiler_params=pltpu.CompilerParams(vmem_limit_bytes=28 << 20),
        cost_estimate=pl.CostEstimate(
            flops=8 * SHARD * MODEL_WIDTH * 256, bytes_accessed=26 << 20, transcendentals=0
        ),
        name="key_value",
    )(pos, tokens, pre_gain.reshape(1, -1), wk, wv, gain.reshape(1, -1), table)


def table_copy(pos_ref, tab_ref, table, sem):
    rows = pl.ds(pl.multiple_of(pos_ref[0] * SHARD, SHARD), SHARD)
    return pltpu.make_async_copy(tab_ref.at[rows], table, sem)


def query_kernel(pos_ref, normed_ref, w_ref, gain_ref, tab_ref, q_ref, table, sem):
    copy = table_copy(pos_ref, tab_ref, table, sem)
    copy.start()
    copy.wait()
    for i in range(SHARD // ROWS):
        rows = slice(i * ROWS, (i + 1) * ROWS)
        raw = jnp.dot(normed_ref[rows, :], w_ref[...], preferred_element_type=F32)
        q_ref[rows, 0:128] = rotate(raw[:, 0:128], gain_ref[...], table[rows, :])
        q_ref[rows, 128:256] = rotate(raw[:, 128:256], gain_ref[...], table[rows, :])


def query(pos, normed, wq, gain, table):
    (table,) = in_hbm(table)
    return pl.pallas_call(
        query_kernel,
        in_specs=[SMEM, VMEM, VMEM, VMEM, ANY],
        out_specs=VMEM,
        out_shape=jax.ShapeDtypeStruct((SHARD, 256), BF16),
        scratch_shapes=[pltpu.VMEM((SHARD, 128), F32), pltpu.SemaphoreType.DMA(())],
        compiler_params=pltpu.CompilerParams(vmem_limit_bytes=24 << 20),
        cost_estimate=SMALL,
        name="query",
    )(pos, normed, wq, gain.reshape(1, -1), table)


def attend_kernel(first_part, pos_ref, q_ref, kv_ref, got_ref, pk_ref, pv_ref, out_ref, keys, values):
    @pl.when(pos_ref[0] == 0)
    def _():
        keys[0:SHARD] = pk_ref[...]
        values[0:SHARD, 0:128] = pv_ref[...]

    @pl.when(pos_ref[0] != 0)
    def _():
        keys[0:SHARD] = got_ref[:, 0:128]
        values[0:SHARD, 0:128] = got_ref[:, 128:256]

    keys[SHARD:] = kv_ref[:, 0:128]
    values[SHARD:, 0:128] = kv_ref[:, 128:256]
    values[:, 128:256] = jnp.ones((2 * SHARD, 128), BF16)

    span = HALF + WINDOW_SPAN
    row = lax.broadcasted_iota(jnp.int32, (2 * HALF, HALF), 0) % HALF
    col = lax.broadcasted_iota(jnp.int32, (2 * HALF, HALF), 1)
    lowest = jnp.float32(-jnp.inf)
    for part in range(out_ref.shape[0] // HALF):
        first = pl.multiple_of(pos_ref[ROW_AT + first_part + part], HALF)
        q = q_ref[pl.ds(first, HALF), :]
        q = jnp.concatenate([q[:, 0:128], q[:, 128:256]], axis=0)
        k = keys[pl.ds(first, span), :]
        scores = lax.dot_general(q, k, (((1,), (1,)), ((), ())), preferred_element_type=F32)
        scores = jnp.concatenate(
            [
                jnp.where(col > row, scores[:, 0:HALF], lowest),
                scores[:, HALF:WINDOW_SPAN],
                jnp.where(col <= row, scores[:, WINDOW_SPAN:], lowest),
            ],
            axis=1,
        )
        top = jnp.max(scores, axis=-1, keepdims=True)
        weights = jnp.exp2((scores - top) * (SCORE_SCALE * LOG2E)).astype(BF16)
        mixed = jnp.dot(weights, values[pl.ds(first, span), :], preferred_element_type=F32)
        mixed = (mixed[:, 0:128] / mixed[:, 128:256]).astype(BF16)
        out_ref[part * HALF : (part + 1) * HALF, 0:128] = mixed[0:HALF]
        out_ref[part * HALF : (part + 1) * HALF, 128:256] = mixed[HALF:]


def attend(first_part, parts, pos, q, kv, got, prior_k, prior_v, cost=SMALL):
    vmem = pl.BlockSpec(memory_space=pltpu.VMEM)
    return pl.pallas_call(
        functools.partial(attend_kernel, first_part),
        in_specs=[pl.BlockSpec(memory_space=pltpu.SMEM)] + [vmem] * 5,
        out_specs=vmem,
        out_shape=jax.ShapeDtypeStruct((parts * HALF, 256), BF16),
        scratch_shapes=[
            pltpu.VMEM((2 * SHARD, 128), BF16),
            pltpu.VMEM((2 * SHARD, 256), BF16),
        ],
        compiler_params=pltpu.CompilerParams(vmem_limit_bytes=32 << 20),
        cost_estimate=cost,
        name="attend",
    )(pos, q, kv, got, prior_k, prior_v)


def quarter_start(number):
    return pl.multiple_of((number * 21 // 2) * 128, 128)


def pick_kernel(pos_ref, w_ref, next_ref, last_ref, far_ref, sems):
    z = pos_ref[1]
    rows = pl.ds(pl.multiple_of(pos_ref[2] * 128, 128), 128)
    copies = []
    for i, (shift, ref) in enumerate(((1, next_ref), (3, last_ref), (2, far_ref))):
        cols = pl.ds(quarter_start((z + shift) % 4), QUARTER)
        copies.append(pltpu.make_async_copy(w_ref.at[rows, cols], ref, sems.at[i]))
    for copy in copies:
        copy.start()
    for copy in copies:
        copy.wait()


def pick(pos, w_out):
    part = jax.ShapeDtypeStruct((128, QUARTER), BF16)
    return pl.pallas_call(
        pick_kernel,
        in_specs=[SMEM, ANY],
        out_specs=[VMEM] * 3,
        out_shape=[part, part, part],
        scratch_shapes=[pltpu.SemaphoreType.DMA((3,))],
        compiler_params=pltpu.CompilerParams(vmem_limit_bytes=16 << 20),
        cost_estimate=SMALL,
        name="pick",
    )(pos, *in_hbm(w_out))


def join_kernel(pos_ref, w_ref, *refs):
    c, out_ref, sem = pos_ref[2], refs[6], refs[7]
    cols = pl.ds(quarter_start(pos_ref[1]), QUARTER)
    copy = pltpu.make_async_copy(w_ref.at[:, cols], out_ref.at[0], sem)
    copy.start()
    for i in range(3):
        out_ref[1 + i, pl.ds(pl.multiple_of(c * 128, 128), 128)] = refs[i][...]
        out_ref[1 + i, pl.ds(pl.multiple_of((1 - c) * 128, 128), 128)] = refs[3 + i][...]
    copy.wait()


def join(pos, w_out, lines, swapped):
    return pl.pallas_call(
        join_kernel,
        in_specs=[SMEM, ANY] + [VMEM] * 6,
        out_specs=VMEM,
        out_shape=jax.ShapeDtypeStruct((4, 256, QUARTER), BF16),
        scratch_shapes=[pltpu.SemaphoreType.DMA(())],
        compiler_params=pltpu.CompilerParams(vmem_limit_bytes=16 << 20),
        cost_estimate=SMALL,
        name="join",
    )(pos, *in_hbm(w_out), *lines, *swapped)


def product(a_refs, w_ref, rows=slice(None)):
    out = jnp.dot(a_refs[0][rows, :], w_ref[0], preferred_element_type=F32)
    for i in range(1, 4):
        out = out + jnp.dot(a_refs[i][rows, :], w_ref[i], preferred_element_type=F32)
    return out


def far_kernel(*refs):
    out = product(refs[0:4], refs[4])
    refs[5][...] = out[0:HALF].astype(BF16)
    refs[6][...] = out[HALF:].astype(BF16)


def near_kernel(*refs):
    refs[5][...] = product(refs[0:4], refs[4], slice(0, 256)).astype(BF16)
    refs[6][...] = product(refs[0:4], refs[4], slice(256, 512)).astype(BF16)


def relay_kernel(relay_up, relay_down, up_in, down_in, up_ref, down_ref):
    up_ref[0:HALF] = (up_in[0:HALF].astype(F32) + relay_up[...].astype(F32)).astype(BF16)
    up_ref[HALF:] = up_in[HALF:]
    down_ref[0:HALF] = down_in[0:HALF]
    down_ref[HALF:] = (down_in[HALF:].astype(F32) + relay_down[...].astype(F32)).astype(BF16)


def relay(relays, up, down):
    return pl.pallas_call(
        relay_kernel,
        in_specs=[VMEM] * 4,
        out_specs=[VMEM] * 2,
        out_shape=[jax.ShapeDtypeStruct((256, QUARTER), BF16)] * 2,
        input_output_aliases={2: 0, 3: 1},
        compiler_params=pltpu.CompilerParams(vmem_limit_bytes=16 << 20),
        cost_estimate=SMALL,
        name="relay",
    )(*relays, up, down)


def keep_kernel(*refs):
    refs[5][...] = product(refs[0:4], refs[4])


def multiply(kernel, pieces, weight, out_shape, name, cost=SMALL):
    return pl.pallas_call(
        kernel,
        in_specs=[VMEM] * 5,
        out_specs=jax.tree.map(lambda _: VMEM, out_shape),
        out_shape=out_shape,
        compiler_params=pltpu.CompilerParams(vmem_limit_bytes=24 << 20),
        cost_estimate=cost,
        name=name,
    )(*pieces, weight)


def total_kernel(pos_ref, kept_ref, up_ref, down_ref, own_ref, next_ref, last_ref, far_ref, total):
    z = pos_ref[1]
    total[...] = kept_ref[...] + up_ref[...].astype(F32) + down_ref[...].astype(F32)

    def rows(shift):
        return total[pl.ds(pl.multiple_of(((z + shift) % 4) * 64, 64), 64), :]

    next_ref[...] = rows(1).astype(BF16)
    last_ref[...] = rows(3).astype(BF16)
    far_ref[...] = rows(2).astype(BF16)
    own_ref[...] = rows(0)


def total_step(pos, kept, up, down):
    part = jax.ShapeDtypeStruct((64, QUARTER), BF16)
    return pl.pallas_call(
        total_kernel,
        in_specs=[SMEM] + [VMEM] * 3,
        out_specs=[VMEM] * 4,
        out_shape=[jax.ShapeDtypeStruct((64, QUARTER), F32), part, part, part],
        scratch_shapes=[pltpu.VMEM((256, QUARTER), F32)],
        compiler_params=pltpu.CompilerParams(vmem_limit_bytes=32 << 20),
        cost_estimate=SMALL,
        name="total_step",
    )(pos, kept, up, down)


def finish_kernel(pos_ref, own_ref, next_ref, last_ref, far_ref, tok_ref, g_ref, out_ref, line):
    z = pos_ref[1]
    for shift, ref in ((0, own_ref), (3, next_ref), (1, last_ref), (2, far_ref)):
        line[:, pl.ds(quarter_start((z + shift) % 4), QUARTER)] = ref[...].astype(F32)
    for i in range(4):
        rows = slice(i * 16, (i + 1) * 16)
        total = jnp.zeros((16, 128), F32)
        for b in range(MODEL_WIDTH // 128):
            part = line[rows, b * 128 : (b + 1) * 128]
            total = total + part * part
        mean = jnp.sum(total, axis=-1, keepdims=True) * (1.0 / MODEL_WIDTH)
        r = jnp.broadcast_to(lax.rsqrt(mean + EPSILON), (16, 128))
        for b in range(MODEL_WIDTH // 128):
            cols = slice(b * 128, (b + 1) * 128)
            normed = line[rows, cols] * r * g_ref[:, cols]
            out_ref[rows, cols] = (tok_ref[rows, cols].astype(F32) + normed).astype(BF16)


def finish(pos, own, nxt, last, far, own_tokens, gain):
    return pl.pallas_call(
        finish_kernel,
        in_specs=[SMEM] + [VMEM] * 6,
        out_specs=VMEM,
        out_shape=jax.ShapeDtypeStruct((64, MODEL_WIDTH), BF16),
        scratch_shapes=[pltpu.VMEM((64, MODEL_WIDTH), F32)],
        compiler_params=pltpu.CompilerParams(vmem_limit_bytes=16 << 20),
        cost_estimate=SMALL,
        name="finish",
    )(pos, own, nxt, last, far, own_tokens, gain.reshape(1, -1))


def shift_by(array, axis, steps):
    return lax.ppermute(array, axis, [(i, (i + steps) % 4) for i in range(4)])


def from_line(pieces):
    return [shift_by(piece, "z", by) for piece, by in zip(pieces, (1, 3, 2), strict=True)]


def per_device(
    tokens, pre_gain, w_query, key_weight, value_weight, query_gain, key_gain,
    prior_key, prior_value, w_out, post_gain, table,
):
    device = lax.axis_index(("y", "c", "x", "z"))
    pos = lax.dynamic_slice_in_dim(jnp.asarray(places()), device, 1, 0).reshape(-1)
    parts = pick(pos, w_out)
    pos, *parts = lax.optimization_barrier((pos, *parts))
    lines = from_line(parts)
    normed, kv, own_tokens = key_value(
        pos, tokens, pre_gain, key_weight, value_weight, key_gain, table
    )
    got = lax.ppermute(kv, ("y", "c"), [(i, i + 1) for i in range(7)])
    q = query(pos, normed, w_query, query_gain, table)
    q, *lines = lax.optimization_barrier((q, *lines))
    swapped = [lax.ppermute(part, "c", [(0, 1), (1, 0)]) for part in lines]
    pos, *swapped = lax.optimization_barrier((pos, *swapped))

    far = attend(0, 2, pos, q, kv, got, prior_key, prior_value)
    far_heads = [far, *from_line([far] * 3)]
    pos, _ = lax.optimization_barrier((pos, far))
    near = attend(2, 4, pos, q, kv, got, prior_key, prior_value)
    near_heads = [near, *from_line([near] * 3)]
    *far_heads, _ = lax.optimization_barrier((*far_heads, near))
    last_pos, _ = lax.optimization_barrier((pos, near))
    weight = join(last_pos, w_out, lines, swapped)

    half = jax.ShapeDtypeStruct((HALF, QUARTER), BF16)
    full = jax.ShapeDtypeStruct((256, QUARTER), BF16)
    kept_shape = jax.ShapeDtypeStruct((256, QUARTER), F32)
    up, down = multiply(far_kernel, far_heads, weight, [half, half], "far")
    relays = (shift_by(up, "x", 1), shift_by(down, "x", 3))
    pos, *_ = lax.optimization_barrier((pos, near, up))
    kept = attend(6, 2, pos, q, kv, got, prior_key, prior_value, MEDIUM)
    kept_heads = [kept, *from_line([kept] * 3)]
    *near_heads, _ = lax.optimization_barrier((*near_heads, kept))
    up, down = multiply(near_kernel, near_heads, weight, [full, full], "near", LARGE)
    up, down = relay(relays, up, down)
    up, down = shift_by(up, "x", 1), shift_by(down, "x", 3)
    kept = multiply(keep_kernel, kept_heads, weight, kept_shape, "keep")
    own, *others = total_step(pos, kept, up, down)
    return finish(pos, own, *from_line(others), own_tokens, post_gain)


def solution(mesh):
    fine = Mesh(mesh.devices.reshape(4, 2, 4, 4), ("y", "c", "x", "z"))
    seq, tp = ("y", "c"), ("x", "z")
    inner = jax.shard_map(
        per_device,
        mesh=fine,
        in_specs=(
            P(seq, None), P(), P(None, tp), P(None, tp), P(None, tp), P(), P(),
            P(None, tp), P(None, tp), P(tp, None), P(), P(),
        ),
        out_specs=P(seq + tp, None),
        check_vma=False,
    )

    def run(*args):
        return inner(*args, jnp.asarray(rotary_table()))

    return run
```

```python
import functools

import jax
import jax.numpy as jnp
import numpy as np
from jax import lax
from jax.experimental import pallas as pl
from jax.experimental.pallas import tpu as pltpu
from jax.sharding import Mesh
from jax.sharding import PartitionSpec as P

MODEL_WIDTH = 5376
HQ = 32
HEAD = 128
WINDOW_SPAN = 1024
BLOCK_TOKENS = 8192
SHARD = 1024
EPSILON = 1e-06
LOG2E = 1.4426950408889634
SCORE_SCALE = float(MODEL_WIDTH // HQ) ** (-0.5)

F32 = jnp.float32
BF16 = jnp.bfloat16

ROWS = 256
GROUP = 16
HALF = 128
QUARTER = 1408
ROW_AT = 3


ANY = pl.BlockSpec(memory_space=pl.ANY)
VMEM = pl.BlockSpec(memory_space=pltpu.VMEM)
SMEM = pl.BlockSpec(memory_space=pltpu.SMEM)
SMALL = pl.CostEstimate(flops=0, bytes_accessed=0, transcendentals=0)
MEDIUM = pl.CostEstimate(flops=4_000_000_000, bytes_accessed=0, transcendentals=0)
LARGE = pl.CostEstimate(flops=30_000_000_000, bytes_accessed=0, transcendentals=0)


def rotary_table():
    half = HEAD // 2
    exponent = np.arange(half, dtype=np.float32) * np.float32(-2.0 / HEAD)
    frequency = np.power(np.float64(10000.0), exponent.astype(np.float64)).astype(np.float32)
    position = (WINDOW_SPAN + np.arange(BLOCK_TOKENS)).astype(np.float32)
    angle = (position[:, None] * frequency[None, :]).astype(np.float64)
    return np.concatenate([np.cos(angle), np.sin(angle)], axis=1).astype(np.float32)


def places():
    rows = []
    for device in range(128):
        seq, x, z = device // 16, device // 4 % 4, device % 4
        far, up, down = ((x + by) % 4 * 256 for by in (2, 1, 3))
        rows.append(
            [seq, z, seq % 2, far, far + 128, up, up + 128, down, down + 128, x * 256,
             x * 256 + 128, x]
        )
    return np.array(rows, np.int32)


def rotate(u, gain, table):
    swapped = pltpu.roll(table, 64, 1)
    low = lax.broadcasted_iota(jnp.int32, table.shape, 1) < 64
    cosine = jnp.where(low, table, swapped)
    sine = jnp.where(low, -swapped, table)
    mean = jnp.sum(u * u, axis=-1, keepdims=True) * (1.0 / HEAD)
    u = u * lax.rsqrt(mean + EPSILON) * gain
    return (u * cosine + pltpu.roll(u, 64, 1) * sine).astype(BF16)


def key_value_kernel(
    pos_ref, tok_ref, g_ref, wk_ref, wv_ref, gain_ref, tab_ref,
    normed, kv_ref, own_ref, w_all, g_all, sems,
):
    step = pl.program_id(0)
    copies = [
        pltpu.make_async_copy(wk_ref, w_all.at[:, 0:128], sems.at[0]),
        pltpu.make_async_copy(wv_ref, w_all.at[:, 128:256], sems.at[1]),
    ]
    blocks = MODEL_WIDTH // 128

    def norm_group(i, carry):
        at = i * GROUP if isinstance(i, int) else pl.multiple_of(i * GROUP, GROUP)
        rows = pl.ds(at, GROUP)
        parts = [jnp.zeros((GROUP, 128), F32) for _ in range(2)]
        for b in range(blocks):
            v = tok_ref[rows, b * 128 : (b + 1) * 128].astype(F32)
            parts[b % 2] = parts[b % 2] + v * v
        mean = jnp.sum(parts[0] + parts[1], axis=-1, keepdims=True) * (1.0 / MODEL_WIDTH)
        r = jnp.broadcast_to(lax.rsqrt(mean + EPSILON), (GROUP, 128))
        for b in range(blocks):
            cols = slice(b * 128, (b + 1) * 128)
            v = tok_ref[rows, cols].astype(F32)
            normed[rows, cols] = (v * r * g_all[:, cols]).astype(BF16)
        return carry

    def multiply_and_rotate():
        raw = jnp.dot(normed[...], w_all[...], preferred_element_type=F32)
        kv_ref[:, 0:128] = rotate(raw[:, 0:128], gain_ref[...], tab_ref[...])
        kv_ref[:, 128:256] = raw[:, 128:256].astype(BF16)

    @pl.when(step == 0)
    def _():
        for copy in copies:
            copy.start()
        g_all[...] = jnp.broadcast_to(g_ref[...], g_all.shape)
        lax.fori_loop(0, ROWS // GROUP, norm_group, 0, unroll=4)
        for copy in copies:
            copy.wait()
        multiply_and_rotate()

    @pl.when(step != 0)
    def _():
        for i in range(ROWS // GROUP):
            norm_group(i, 0)
        multiply_and_rotate()

    @pl.when(step == pos_ref[ROW_AT + 8])
    def _():
        own_ref[...] = tok_ref[pl.ds(pl.multiple_of(pos_ref[1] * 64, 64), 64), :]


def in_hbm(*arrays):
    return [pltpu.with_memory_space_constraint(array, pltpu.HBM) for array in arrays]


def whole(shape):
    return pl.BlockSpec(shape, lambda i, s: (0, 0))


def row_tile(width):
    return pl.BlockSpec((ROWS, width), lambda i, s: (i, 0))


TABLE_TILE = pl.BlockSpec((ROWS, 128), lambda i, s: (s[0] * (SHARD // ROWS) + i, 0))


def key_value(pos, tokens, pre_gain, wk, wv, gain, table):
    tokens, wk, wv, table = in_hbm(tokens, wk, wv, table)
    return pl.pallas_call(
        key_value_kernel,
        grid_spec=pltpu.PrefetchScalarGridSpec(
            num_scalar_prefetch=1,
            grid=(SHARD // ROWS,),
            in_specs=[
                row_tile(MODEL_WIDTH), whole((1, MODEL_WIDTH)), ANY, ANY,
                whole((1, 128)), TABLE_TILE,
            ],
            out_specs=[row_tile(MODEL_WIDTH), row_tile(256), whole((64, MODEL_WIDTH))],
            scratch_shapes=[
                pltpu.VMEM((MODEL_WIDTH, 256), BF16),
                pltpu.VMEM((GROUP, MODEL_WIDTH), F32),
                pltpu.SemaphoreType.DMA((2,)),
            ],
        ),
        out_shape=[
            jax.ShapeDtypeStruct((SHARD, MODEL_WIDTH), BF16),
            jax.ShapeDtypeStruct((SHARD, 256), BF16),
            jax.ShapeDtypeStruct((64, MODEL_WIDTH), BF16),
        ],
        compiler_params=pltpu.CompilerParams(vmem_limit_bytes=28 << 20),
        cost_estimate=pl.CostEstimate(
            flops=8 * SHARD * MODEL_WIDTH * 256, bytes_accessed=26 << 20, transcendentals=0
        ),
        name="key_value",
    )(pos, tokens, pre_gain.reshape(1, -1), wk, wv, gain.reshape(1, -1), table)


def table_copy(pos_ref, tab_ref, table, sem):
    rows = pl.ds(pl.multiple_of(pos_ref[0] * SHARD, SHARD), SHARD)
    return pltpu.make_async_copy(tab_ref.at[rows], table, sem)


def query_kernel(
    pos_ref, normed_ref, w_ref, gain_ref, tab_ref, w_out_ref, q_ref, own_w_ref, table, sems
):
    copy = table_copy(pos_ref, tab_ref, table, sems.at[0])
    copy.start()
    cols = pl.ds(quarter_start(pos_ref[1]), QUARTER)
    fetch = pltpu.make_async_copy(w_out_ref.at[:, cols], own_w_ref, sems.at[1])
    fetch.start()
    copy.wait()
    for i in range(SHARD // ROWS):
        rows = slice(i * ROWS, (i + 1) * ROWS)
        raw = jnp.dot(normed_ref[rows, :], w_ref[...], preferred_element_type=F32)
        q_ref[rows, 0:128] = rotate(raw[:, 0:128], gain_ref[...], table[rows, :])
        q_ref[rows, 128:256] = rotate(raw[:, 128:256], gain_ref[...], table[rows, :])
    fetch.wait()


def query(pos, normed, wq, gain, table, w_out):
    table, w_out = in_hbm(table, w_out)
    return pl.pallas_call(
        query_kernel,
        in_specs=[SMEM, VMEM, VMEM, VMEM, ANY, ANY],
        out_specs=[VMEM] * 2,
        out_shape=[
            jax.ShapeDtypeStruct((SHARD, 256), BF16),
            jax.ShapeDtypeStruct((256, QUARTER), BF16),
        ],
        scratch_shapes=[pltpu.VMEM((SHARD, 128), F32), pltpu.SemaphoreType.DMA((2,))],
        compiler_params=pltpu.CompilerParams(vmem_limit_bytes=24 << 20),
        cost_estimate=SMALL,
        name="query",
    )(pos, normed, wq, gain.reshape(1, -1), table, w_out)


def first_attend_kernel(
    first_part, pos_ref, q_ref, kv_ref, got_ref, pk_ref, pv_ref, out_ref, keys, values
):
    @pl.when(pos_ref[0] == 0)
    def _():
        keys[0:SHARD] = pk_ref[...]
        values[0:SHARD, 0:128] = pv_ref[...]

    @pl.when(pos_ref[0] != 0)
    def _():
        keys[0:SHARD] = got_ref[:, 0:128]
        values[0:SHARD, 0:128] = got_ref[:, 128:256]

    keys[SHARD:] = kv_ref[:, 0:128]
    values[SHARD:, 0:128] = kv_ref[:, 128:256]
    values[:, 128:256] = jnp.ones((2 * SHARD, 128), BF16)
    attend_kernel(first_part, pos_ref, q_ref, keys, values, out_ref)


def attend_kernel(first_part, pos_ref, q_ref, keys, values, out_ref):
    span = HALF + WINDOW_SPAN
    row = lax.broadcasted_iota(jnp.int32, (2 * HALF, HALF), 0) % HALF
    col = lax.broadcasted_iota(jnp.int32, (2 * HALF, HALF), 1)
    lowest = jnp.float32(-jnp.inf)
    for part in range(out_ref.shape[0] // HALF):
        first = pl.multiple_of(pos_ref[ROW_AT + first_part + part], HALF)
        q = q_ref[pl.ds(first, HALF), :]
        q = jnp.concatenate([q[:, 0:128], q[:, 128:256]], axis=0)
        k = keys[pl.ds(first, span), :]
        scores = lax.dot_general(q, k, (((1,), (1,)), ((), ())), preferred_element_type=F32)
        scores = jnp.concatenate(
            [
                jnp.where(col > row, scores[:, 0:HALF], lowest),
                scores[:, HALF:WINDOW_SPAN],
                jnp.where(col <= row, scores[:, WINDOW_SPAN:], lowest),
            ],
            axis=1,
        )
        top = jnp.max(scores, axis=-1, keepdims=True)
        weights = jnp.exp2((scores - top) * (SCORE_SCALE * LOG2E)).astype(BF16)
        mixed = jnp.dot(weights, values[pl.ds(first, span), :], preferred_element_type=F32)
        mixed = (mixed[:, 0:128] / mixed[:, 128:256]).astype(BF16)
        out_ref[part * HALF : (part + 1) * HALF, 0:128] = mixed[0:HALF]
        out_ref[part * HALF : (part + 1) * HALF, 128:256] = mixed[HALF:]


def attend(first_part, parts, pos, q, sources, cost=SMALL):
    out_shape = [jax.ShapeDtypeStruct((parts * HALF, 256), BF16)]
    kernel = attend_kernel
    if len(sources) > 2:
        kernel = first_attend_kernel
        out_shape += [
            jax.ShapeDtypeStruct((2 * SHARD, 128), BF16),
            jax.ShapeDtypeStruct((2 * SHARD, 256), BF16),
        ]
    return pl.pallas_call(
        functools.partial(kernel, first_part),
        in_specs=[SMEM] + [VMEM] * (1 + len(sources)),
        out_specs=[VMEM] * len(out_shape),
        out_shape=out_shape,
        compiler_params=pltpu.CompilerParams(vmem_limit_bytes=32 << 20),
        cost_estimate=cost,
        name="attend",
    )(pos, q, *sources)


def quarter_start(number):
    return pl.multiple_of((number * 21 // 2) * 128, 128)


def pick_kernel(pos_ref, w_ref, next_ref, last_ref, far_ref, sems):
    z = pos_ref[1]
    rows = pl.ds(pl.multiple_of(pos_ref[2] * 128, 128), 128)
    copies = []
    for i, (shift, ref) in enumerate(((1, next_ref), (3, last_ref), (2, far_ref))):
        cols = pl.ds(quarter_start((z + shift) % 4), QUARTER)
        copies.append(pltpu.make_async_copy(w_ref.at[rows, cols], ref, sems.at[i]))
    for copy in copies:
        copy.start()
    for copy in copies:
        copy.wait()


def pick(pos, w_out):
    part = jax.ShapeDtypeStruct((128, QUARTER), BF16)
    return pl.pallas_call(
        pick_kernel,
        in_specs=[SMEM, ANY],
        out_specs=[VMEM] * 3,
        out_shape=[part, part, part],
        scratch_shapes=[pltpu.SemaphoreType.DMA((3,))],
        compiler_params=pltpu.CompilerParams(vmem_limit_bytes=16 << 20),
        cost_estimate=SMALL,
        name="pick",
    )(pos, *in_hbm(w_out))


def join_kernel(pos_ref, *refs):
    c, out_ref = pos_ref[2], refs[6]
    for i in range(3):
        out_ref[i, pl.ds(pl.multiple_of(c * 128, 128), 128)] = refs[i][...]
        out_ref[i, pl.ds(pl.multiple_of((1 - c) * 128, 128), 128)] = refs[3 + i][...]


def join(pos, lines, swapped):
    return pl.pallas_call(
        join_kernel,
        in_specs=[SMEM] + [VMEM] * 6,
        out_specs=VMEM,
        out_shape=jax.ShapeDtypeStruct((3, 256, QUARTER), BF16),
        compiler_params=pltpu.CompilerParams(vmem_limit_bytes=16 << 20),
        cost_estimate=SMALL,
        name="join",
    )(pos, *lines, *swapped)


def product(a_refs, own_ref, line_ref, rows=slice(None)):
    out = jnp.dot(a_refs[0][rows, :], own_ref[...], preferred_element_type=F32)
    for i in range(3):
        out = out + jnp.dot(a_refs[1 + i][rows, :], line_ref[i], preferred_element_type=F32)
    return out


def far_kernel(*refs):
    out = product(refs[0:4], refs[4], refs[5])
    refs[6][...] = out[0:HALF].astype(BF16)
    refs[7][...] = out[HALF:].astype(BF16)


def near_kernel(*refs):
    refs[6][...] = product(refs[0:4], refs[4], refs[5], slice(0, 256)).astype(BF16)
    refs[7][...] = product(refs[0:4], refs[4], refs[5], slice(256, 512)).astype(BF16)


def relay_kernel(relay_up, relay_down, up_in, down_in, up_ref, down_ref):
    up_ref[0:HALF] = (up_in[0:HALF].astype(F32) + relay_up[...].astype(F32)).astype(BF16)
    up_ref[HALF:] = up_in[HALF:]
    down_ref[0:HALF] = down_in[0:HALF]
    down_ref[HALF:] = (down_in[HALF:].astype(F32) + relay_down[...].astype(F32)).astype(BF16)


def relay(relays, up, down):
    return pl.pallas_call(
        relay_kernel,
        in_specs=[VMEM] * 4,
        out_specs=[VMEM] * 2,
        out_shape=[jax.ShapeDtypeStruct((256, QUARTER), BF16)] * 2,
        input_output_aliases={2: 0, 3: 1},
        compiler_params=pltpu.CompilerParams(vmem_limit_bytes=16 << 20),
        cost_estimate=SMALL,
        name="relay",
    )(*relays, up, down)


def keep_kernel(*refs):
    refs[6][...] = product(refs[0:4], refs[4], refs[5])


def multiply(kernel, pieces, weights, out_shape, name, cost=SMALL):
    return pl.pallas_call(
        kernel,
        in_specs=[VMEM] * 6,
        out_specs=jax.tree.map(lambda _: VMEM, out_shape),
        out_shape=out_shape,
        compiler_params=pltpu.CompilerParams(vmem_limit_bytes=24 << 20),
        cost_estimate=cost,
        name=name,
    )(*pieces, *weights)


def total_kernel(pos_ref, kept_ref, up_ref, down_ref, own_ref, next_ref, last_ref, far_ref, total):
    z = pos_ref[1]
    total[...] = kept_ref[...] + up_ref[...].astype(F32) + down_ref[...].astype(F32)

    def rows(shift):
        return total[pl.ds(pl.multiple_of(((z + shift) % 4) * 64, 64), 64), :]

    next_ref[...] = rows(1).astype(BF16)
    last_ref[...] = rows(3).astype(BF16)
    far_ref[...] = rows(2).astype(BF16)
    own_ref[...] = rows(0)


def total_step(pos, kept, up, down):
    part = jax.ShapeDtypeStruct((64, QUARTER), BF16)
    return pl.pallas_call(
        total_kernel,
        in_specs=[SMEM] + [VMEM] * 3,
        out_specs=[VMEM] * 4,
        out_shape=[jax.ShapeDtypeStruct((64, QUARTER), F32), part, part, part],
        scratch_shapes=[pltpu.VMEM((256, QUARTER), F32)],
        compiler_params=pltpu.CompilerParams(vmem_limit_bytes=32 << 20),
        cost_estimate=SMALL,
        name="total_step",
    )(pos, kept, up, down)


def finish_kernel(pos_ref, own_ref, next_ref, last_ref, far_ref, tok_ref, g_ref, out_ref, line):
    z = pos_ref[1]
    for shift, ref in ((0, own_ref), (3, next_ref), (1, last_ref), (2, far_ref)):
        line[:, pl.ds(quarter_start((z + shift) % 4), QUARTER)] = ref[...].astype(F32)
    for i in range(4):
        rows = slice(i * 16, (i + 1) * 16)
        total = jnp.zeros((16, 128), F32)
        for b in range(MODEL_WIDTH // 128):
            part = line[rows, b * 128 : (b + 1) * 128]
            total = total + part * part
        mean = jnp.sum(total, axis=-1, keepdims=True) * (1.0 / MODEL_WIDTH)
        r = jnp.broadcast_to(lax.rsqrt(mean + EPSILON), (16, 128))
        for b in range(MODEL_WIDTH // 128):
            cols = slice(b * 128, (b + 1) * 128)
            normed = line[rows, cols] * r * g_ref[:, cols]
            out_ref[rows, cols] = (tok_ref[rows, cols].astype(F32) + normed).astype(BF16)


def finish(pos, own, nxt, last, far, own_tokens, gain):
    return pl.pallas_call(
        finish_kernel,
        in_specs=[SMEM] + [VMEM] * 6,
        out_specs=VMEM,
        out_shape=jax.ShapeDtypeStruct((64, MODEL_WIDTH), BF16),
        scratch_shapes=[pltpu.VMEM((64, MODEL_WIDTH), F32)],
        compiler_params=pltpu.CompilerParams(vmem_limit_bytes=16 << 20),
        cost_estimate=SMALL,
        name="finish",
    )(pos, own, nxt, last, far, own_tokens, gain.reshape(1, -1))


def shift_by(array, axis, steps):
    return lax.ppermute(array, axis, [(i, (i + steps) % 4) for i in range(4)])


def from_line(pieces):
    return [shift_by(piece, "z", by) for piece, by in zip(pieces, (1, 3, 2), strict=True)]


def per_device(
    tokens, pre_gain, w_query, key_weight, value_weight, query_gain, key_gain,
    prior_key, prior_value, w_out, post_gain, table,
):
    device = lax.axis_index(("y", "c", "x", "z"))
    pos = lax.dynamic_slice_in_dim(jnp.asarray(places()), device, 1, 0).reshape(-1)
    parts = pick(pos, w_out)
    pos, *parts = lax.optimization_barrier((pos, *parts))
    lines = from_line(parts)
    normed, kv, own_tokens = key_value(
        pos, tokens, pre_gain, key_weight, value_weight, key_gain, table
    )
    got = lax.ppermute(kv, ("y", "c"), [(i, i + 1) for i in range(7)])
    q, own_w = query(pos, normed, w_query, query_gain, table, w_out)
    q, *lines = lax.optimization_barrier((q, *lines))
    swapped = [lax.ppermute(part, "c", [(0, 1), (1, 0)]) for part in lines]
    pos, *swapped = lax.optimization_barrier((pos, *swapped))

    far, *extended = attend(0, 2, pos, q, (kv, got, prior_key, prior_value))
    far_heads = [far, *from_line([far] * 3)]
    pos, _ = lax.optimization_barrier((pos, far))
    (near,) = attend(2, 4, pos, q, extended)
    near_heads = [near, *from_line([near] * 3)]
    *far_heads, _ = lax.optimization_barrier((*far_heads, near))
    last_pos, _ = lax.optimization_barrier((pos, near))
    weights = [own_w, join(last_pos, lines, swapped)]

    half = jax.ShapeDtypeStruct((HALF, QUARTER), BF16)
    full = jax.ShapeDtypeStruct((256, QUARTER), BF16)
    kept_shape = jax.ShapeDtypeStruct((256, QUARTER), F32)
    up, down = multiply(far_kernel, far_heads, weights, [half, half], "far")
    relays = (shift_by(up, "x", 1), shift_by(down, "x", 3))
    pos, *_ = lax.optimization_barrier((pos, near, up))
    (kept,) = attend(6, 2, pos, q, extended, MEDIUM)
    kept_heads = [kept, *from_line([kept] * 3)]
    *near_heads, _ = lax.optimization_barrier((*near_heads, kept))
    up, down = multiply(near_kernel, near_heads, weights, [full, full], "near", LARGE)
    up, down = relay(relays, up, down)
    up, down = shift_by(up, "x", 1), shift_by(down, "x", 3)
    kept = multiply(keep_kernel, kept_heads, weights, kept_shape, "keep")
    own, *others = total_step(pos, kept, up, down)
    return finish(pos, own, *from_line(others), own_tokens, post_gain)


def solution(mesh):
    fine = Mesh(mesh.devices.reshape(4, 2, 4, 4), ("y", "c", "x", "z"))
    seq, tp = ("y", "c"), ("x", "z")
    inner = jax.shard_map(
        per_device,
        mesh=fine,
        in_specs=(
            P(seq, None), P(), P(None, tp), P(None, tp), P(None, tp), P(), P(),
            P(None, tp), P(None, tp), P(tp, None), P(), P(),
        ),
        out_specs=P(seq + tp, None),
        check_vma=False,
    )

    def run(*args):
        return inner(*args, jnp.asarray(rotary_table()))

    return run
```

```python
import functools

import jax
import jax.numpy as jnp
import numpy as np
from jax import lax
from jax.experimental import pallas as pl
from jax.experimental.pallas import tpu as pltpu
from jax.sharding import Mesh
from jax.sharding import PartitionSpec as P

MODEL_WIDTH = 5376
HQ = 32
HEAD = 128
WINDOW_SPAN = 1024
BLOCK_TOKENS = 8192
SHARD = 1024
EPSILON = 1e-06
LOG2E = 1.4426950408889634
SCORE_SCALE = float(MODEL_WIDTH // HQ) ** (-0.5)

F32 = jnp.float32
BF16 = jnp.bfloat16

ROWS = 256
GROUP = 16
HALF = 128
QUARTER = 1408
ROW_AT = 3


ANY = pl.BlockSpec(memory_space=pl.ANY)
VMEM = pl.BlockSpec(memory_space=pltpu.VMEM)
SMEM = pl.BlockSpec(memory_space=pltpu.SMEM)
SMALL = pl.CostEstimate(flops=0, bytes_accessed=0, transcendentals=0)
MEDIUM = pl.CostEstimate(flops=4_000_000_000, bytes_accessed=0, transcendentals=0)
LARGE = pl.CostEstimate(flops=30_000_000_000, bytes_accessed=0, transcendentals=0)


def rotary_table():
    half = HEAD // 2
    exponent = np.arange(half, dtype=np.float32) * np.float32(-2.0 / HEAD)
    frequency = np.power(np.float64(10000.0), exponent.astype(np.float64)).astype(np.float32)
    position = (WINDOW_SPAN + np.arange(BLOCK_TOKENS)).astype(np.float32)
    angle = (position[:, None] * frequency[None, :]).astype(np.float64)
    return np.concatenate([np.cos(angle), np.sin(angle)], axis=1).astype(np.float32)


def places():
    rows = []
    for device in range(128):
        seq, x, z = device // 16, device // 4 % 4, device % 4
        far, up, down = ((x + by) % 4 * 256 for by in (2, 1, 3))
        rows.append(
            [seq, z, seq % 2, far, far + 128, up, up + 128, down, down + 128, x * 256,
             x * 256 + 128, x]
        )
    return np.array(rows, np.int32)


def rotate(u, gain, table):
    swapped = pltpu.roll(table, 64, 1)
    low = lax.broadcasted_iota(jnp.int32, table.shape, 1) < 64
    cosine = jnp.where(low, table, swapped)
    sine = jnp.where(low, -swapped, table)
    mean = jnp.sum(u * u, axis=-1, keepdims=True) * (1.0 / HEAD)
    u = u * lax.rsqrt(mean + EPSILON) * gain
    return (u * cosine + pltpu.roll(u, 64, 1) * sine).astype(BF16)


def key_value_kernel(
    pos_ref, tok_ref, g_ref, wk_ref, wv_ref, gain_ref, tab_ref,
    normed, kv_ref, own_ref, w_all, g_all, sems,
):
    step = pl.program_id(0)
    copies = [
        pltpu.make_async_copy(wk_ref, w_all.at[:, 0:128], sems.at[0]),
        pltpu.make_async_copy(wv_ref, w_all.at[:, 128:256], sems.at[1]),
    ]
    blocks = MODEL_WIDTH // 128

    def norm_group(i):
        rows = slice(i * GROUP, (i + 1) * GROUP)
        parts = [jnp.zeros((GROUP, 128), F32) for _ in range(2)]
        for b in range(blocks):
            v = tok_ref[rows, b * 128 : (b + 1) * 128].astype(F32)
            parts[b % 2] = parts[b % 2] + v * v
        mean = jnp.sum(parts[0] + parts[1], axis=-1, keepdims=True) * (1.0 / MODEL_WIDTH)
        r = jnp.broadcast_to(lax.rsqrt(mean + EPSILON), (GROUP, 128))
        for b in range(blocks):
            cols = slice(b * 128, (b + 1) * 128)
            v = tok_ref[rows, cols].astype(F32)
            normed[rows, cols] = (v * r * g_all[:, cols]).astype(BF16)

    def multiply_and_rotate():
        raw = jnp.dot(normed[...], w_all[...], preferred_element_type=F32)
        kv_ref[:, 0:128] = rotate(raw[:, 0:128], gain_ref[...], tab_ref[...])
        kv_ref[:, 128:256] = raw[:, 128:256].astype(BF16)

    @pl.when(step == 0)
    def _():
        for copy in copies:
            copy.start()
        g_all[...] = jnp.broadcast_to(g_ref[...], g_all.shape)
        for i in range(ROWS // GROUP):
            norm_group(i)
        for copy in copies:
            copy.wait()
        multiply_and_rotate()

    @pl.when(step != 0)
    def _():
        for i in range(ROWS // GROUP):
            norm_group(i)
        multiply_and_rotate()

    @pl.when(step == pos_ref[ROW_AT + 8])
    def _():
        own_ref[...] = tok_ref[pl.ds(pl.multiple_of(pos_ref[1] * 64, 64), 64), :]


def in_hbm(*arrays):
    return [pltpu.with_memory_space_constraint(array, pltpu.HBM) for array in arrays]


def whole(shape):
    return pl.BlockSpec(shape, lambda i, s: (0, 0))


def row_tile(width):
    return pl.BlockSpec((ROWS, width), lambda i, s: (i, 0))


TABLE_TILE = pl.BlockSpec((ROWS, 128), lambda i, s: (s[0] * (SHARD // ROWS) + i, 0))


def key_value(pos, tokens, pre_gain, wk, wv, gain, table):
    tokens, wk, wv, table = in_hbm(tokens, wk, wv, table)
    return pl.pallas_call(
        key_value_kernel,
        grid_spec=pltpu.PrefetchScalarGridSpec(
            num_scalar_prefetch=1,
            grid=(SHARD // ROWS,),
            in_specs=[
                row_tile(MODEL_WIDTH), whole((1, MODEL_WIDTH)), ANY, ANY,
                whole((1, 128)), TABLE_TILE,
            ],
            out_specs=[row_tile(MODEL_WIDTH), row_tile(256), whole((64, MODEL_WIDTH))],
            scratch_shapes=[
                pltpu.VMEM((MODEL_WIDTH, 256), BF16),
                pltpu.VMEM((GROUP, MODEL_WIDTH), F32),
                pltpu.SemaphoreType.DMA((2,)),
            ],
        ),
        out_shape=[
            jax.ShapeDtypeStruct((SHARD, MODEL_WIDTH), BF16),
            jax.ShapeDtypeStruct((SHARD, 256), BF16),
            jax.ShapeDtypeStruct((64, MODEL_WIDTH), BF16),
        ],
        compiler_params=pltpu.CompilerParams(vmem_limit_bytes=28 << 20),
        cost_estimate=pl.CostEstimate(
            flops=8 * SHARD * MODEL_WIDTH * 256, bytes_accessed=26 << 20, transcendentals=0
        ),
        name="key_value",
    )(pos, tokens, pre_gain.reshape(1, -1), wk, wv, gain.reshape(1, -1), table)


def table_copy(pos_ref, tab_ref, table, sem):
    rows = pl.ds(pl.multiple_of(pos_ref[0] * SHARD, SHARD), SHARD)
    return pltpu.make_async_copy(tab_ref.at[rows], table, sem)


def query_kernel(
    pos_ref, normed_ref, w_ref, gain_ref, tab_ref, w_out_ref, q_ref, own_w_ref, table, sems
):
    copy = table_copy(pos_ref, tab_ref, table, sems.at[0])
    copy.start()
    cols = pl.ds(quarter_start(pos_ref[1]), QUARTER)
    fetch = pltpu.make_async_copy(w_out_ref.at[:, cols], own_w_ref, sems.at[1])
    fetch.start()
    copy.wait()
    for i in range(SHARD // ROWS):
        rows = slice(i * ROWS, (i + 1) * ROWS)
        raw = jnp.dot(normed_ref[rows, :], w_ref[...], preferred_element_type=F32)
        q_ref[rows, 0:128] = rotate(raw[:, 0:128], gain_ref[...], table[rows, :])
        q_ref[rows, 128:256] = rotate(raw[:, 128:256], gain_ref[...], table[rows, :])
    fetch.wait()


def query(pos, normed, wq, gain, table, w_out):
    table, w_out = in_hbm(table, w_out)
    return pl.pallas_call(
        query_kernel,
        in_specs=[SMEM, VMEM, VMEM, VMEM, ANY, ANY],
        out_specs=[VMEM] * 2,
        out_shape=[
            jax.ShapeDtypeStruct((SHARD, 256), BF16),
            jax.ShapeDtypeStruct((256, QUARTER), BF16),
        ],
        scratch_shapes=[pltpu.VMEM((SHARD, 128), F32), pltpu.SemaphoreType.DMA((2,))],
        compiler_params=pltpu.CompilerParams(vmem_limit_bytes=24 << 20),
        cost_estimate=SMALL,
        name="query",
    )(pos, normed, wq, gain.reshape(1, -1), table, w_out)


def first_attend_kernel(
    first_part, pos_ref, q_ref, kv_ref, got_ref, pk_ref, pv_ref, out_ref, keys, values
):
    @pl.when(pos_ref[0] == 0)
    def _():
        keys[0:SHARD] = pk_ref[...]
        values[0:SHARD, 0:128] = pv_ref[...]

    @pl.when(pos_ref[0] != 0)
    def _():
        keys[0:SHARD] = got_ref[:, 0:128]
        values[0:SHARD, 0:128] = got_ref[:, 128:256]

    keys[SHARD:] = kv_ref[:, 0:128]
    values[SHARD:, 0:128] = kv_ref[:, 128:256]
    values[:, 128:256] = jnp.ones((2 * SHARD, 128), BF16)
    attend_kernel(first_part, pos_ref, q_ref, keys, values, out_ref)


def attend_kernel(first_part, pos_ref, q_ref, keys, values, out_ref):
    span = HALF + WINDOW_SPAN
    row = lax.broadcasted_iota(jnp.int32, (2 * HALF, HALF), 0) % HALF
    col = lax.broadcasted_iota(jnp.int32, (2 * HALF, HALF), 1)
    lowest = jnp.float32(-jnp.inf)
    for part in range(out_ref.shape[0] // HALF):
        first = pl.multiple_of(pos_ref[ROW_AT + first_part + part], HALF)
        q = q_ref[pl.ds(first, HALF), :]
        q = jnp.concatenate([q[:, 0:128], q[:, 128:256]], axis=0)
        k = keys[pl.ds(first, span), :]
        scores = lax.dot_general(q, k, (((1,), (1,)), ((), ())), preferred_element_type=F32)
        scores = jnp.concatenate(
            [
                jnp.where(col > row, scores[:, 0:HALF], lowest),
                scores[:, HALF:WINDOW_SPAN],
                jnp.where(col <= row, scores[:, WINDOW_SPAN:], lowest),
            ],
            axis=1,
        )
        top = jnp.max(scores, axis=-1, keepdims=True)
        weights = jnp.exp2((scores - top) * (SCORE_SCALE * LOG2E)).astype(BF16)
        mixed = jnp.dot(weights, values[pl.ds(first, span), :], preferred_element_type=F32)
        mixed = (mixed[:, 0:128] / mixed[:, 128:256]).astype(BF16)
        out_ref[part * HALF : (part + 1) * HALF, 0:128] = mixed[0:HALF]
        out_ref[part * HALF : (part + 1) * HALF, 128:256] = mixed[HALF:]


def attend(first_part, parts, pos, q, sources, cost=SMALL):
    out_shape = [jax.ShapeDtypeStruct((parts * HALF, 256), BF16)]
    kernel = attend_kernel
    if len(sources) > 2:
        kernel = first_attend_kernel
        out_shape += [
            jax.ShapeDtypeStruct((2 * SHARD, 128), BF16),
            jax.ShapeDtypeStruct((2 * SHARD, 256), BF16),
        ]
    return pl.pallas_call(
        functools.partial(kernel, first_part),
        in_specs=[SMEM] + [VMEM] * (1 + len(sources)),
        out_specs=[VMEM] * len(out_shape),
        out_shape=out_shape,
        compiler_params=pltpu.CompilerParams(vmem_limit_bytes=32 << 20),
        cost_estimate=cost,
        name="attend",
    )(pos, q, *sources)


def quarter_start(number):
    return pl.multiple_of((number * 21 // 2) * 128, 128)


def pick_kernel(pos_ref, w_ref, next_ref, last_ref, far_ref, sems):
    z = pos_ref[1]
    rows = pl.ds(pl.multiple_of(pos_ref[2] * 128, 128), 128)
    copies = []
    for i, (shift, ref) in enumerate(((1, next_ref), (3, last_ref), (2, far_ref))):
        cols = pl.ds(quarter_start((z + shift) % 4), QUARTER)
        copies.append(pltpu.make_async_copy(w_ref.at[rows, cols], ref, sems.at[i]))
    for copy in copies:
        copy.start()
    for copy in copies:
        copy.wait()


def pick(pos, w_out):
    part = jax.ShapeDtypeStruct((128, QUARTER), BF16)
    return pl.pallas_call(
        pick_kernel,
        in_specs=[SMEM, ANY],
        out_specs=[VMEM] * 3,
        out_shape=[part, part, part],
        scratch_shapes=[pltpu.SemaphoreType.DMA((3,))],
        compiler_params=pltpu.CompilerParams(vmem_limit_bytes=16 << 20),
        cost_estimate=SMALL,
        name="pick",
    )(pos, *in_hbm(w_out))


def join_kernel(pos_ref, *refs):
    c, out_ref = pos_ref[2], refs[6]
    for i in range(3):
        out_ref[i, pl.ds(pl.multiple_of(c * 128, 128), 128)] = refs[i][...]
        out_ref[i, pl.ds(pl.multiple_of((1 - c) * 128, 128), 128)] = refs[3 + i][...]


def join(pos, lines, swapped):
    return pl.pallas_call(
        join_kernel,
        in_specs=[SMEM] + [VMEM] * 6,
        out_specs=VMEM,
        out_shape=jax.ShapeDtypeStruct((3, 256, QUARTER), BF16),
        compiler_params=pltpu.CompilerParams(vmem_limit_bytes=16 << 20),
        cost_estimate=SMALL,
        name="join",
    )(pos, *lines, *swapped)


def product(a_refs, own_ref, line_ref, rows=slice(None)):
    out = jnp.dot(a_refs[0][rows, :], own_ref[...], preferred_element_type=F32)
    for i in range(3):
        out = out + jnp.dot(a_refs[1 + i][rows, :], line_ref[i], preferred_element_type=F32)
    return out


def far_kernel(*refs):
    out = product(refs[0:4], refs[4], refs[5])
    refs[6][...] = out[0:HALF].astype(BF16)
    refs[7][...] = out[HALF:].astype(BF16)


def near_kernel(*refs):
    refs[6][...] = product(refs[0:4], refs[4], refs[5], slice(0, 256)).astype(BF16)
    refs[7][...] = product(refs[0:4], refs[4], refs[5], slice(256, 512)).astype(BF16)


def relay_kernel(relay_up, relay_down, up_in, down_in, up_ref, down_ref):
    up_ref[0:HALF] = (up_in[0:HALF].astype(F32) + relay_up[...].astype(F32)).astype(BF16)
    up_ref[HALF:] = up_in[HALF:]
    down_ref[0:HALF] = down_in[0:HALF]
    down_ref[HALF:] = (down_in[HALF:].astype(F32) + relay_down[...].astype(F32)).astype(BF16)


def relay(relays, up, down):
    return pl.pallas_call(
        relay_kernel,
        in_specs=[VMEM] * 4,
        out_specs=[VMEM] * 2,
        out_shape=[jax.ShapeDtypeStruct((256, QUARTER), BF16)] * 2,
        input_output_aliases={2: 0, 3: 1},
        compiler_params=pltpu.CompilerParams(vmem_limit_bytes=16 << 20),
        cost_estimate=SMALL,
        name="relay",
    )(*relays, up, down)


def keep_kernel(*refs):
    refs[6][...] = product(refs[0:4], refs[4], refs[5])


def multiply(kernel, pieces, weights, out_shape, name, cost=SMALL):
    return pl.pallas_call(
        kernel,
        in_specs=[VMEM] * 6,
        out_specs=jax.tree.map(lambda _: VMEM, out_shape),
        out_shape=out_shape,
        compiler_params=pltpu.CompilerParams(vmem_limit_bytes=24 << 20),
        cost_estimate=cost,
        name=name,
    )(*pieces, *weights)


def total_kernel(pos_ref, kept_ref, up_ref, down_ref, own_ref, next_ref, last_ref, far_ref, total):
    z = pos_ref[1]
    total[...] = kept_ref[...] + up_ref[...].astype(F32) + down_ref[...].astype(F32)

    def rows(shift):
        return total[pl.ds(pl.multiple_of(((z + shift) % 4) * 64, 64), 64), :]

    next_ref[...] = rows(1).astype(BF16)
    last_ref[...] = rows(3).astype(BF16)
    far_ref[...] = rows(2).astype(BF16)
    own_ref[...] = rows(0)


def total_step(pos, kept, up, down):
    part = jax.ShapeDtypeStruct((64, QUARTER), BF16)
    return pl.pallas_call(
        total_kernel,
        in_specs=[SMEM] + [VMEM] * 3,
        out_specs=[VMEM] * 4,
        out_shape=[jax.ShapeDtypeStruct((64, QUARTER), F32), part, part, part],
        scratch_shapes=[pltpu.VMEM((256, QUARTER), F32)],
        compiler_params=pltpu.CompilerParams(vmem_limit_bytes=32 << 20),
        cost_estimate=SMALL,
        name="total_step",
    )(pos, kept, up, down)


def finish_kernel(pos_ref, own_ref, next_ref, last_ref, far_ref, tok_ref, g_ref, out_ref, line):
    z = pos_ref[1]
    for shift, ref in ((0, own_ref), (3, next_ref), (1, last_ref), (2, far_ref)):
        line[:, pl.ds(quarter_start((z + shift) % 4), QUARTER)] = ref[...].astype(F32)
    for i in range(4):
        rows = slice(i * 16, (i + 1) * 16)
        total = jnp.zeros((16, 128), F32)
        for b in range(MODEL_WIDTH // 128):
            part = line[rows, b * 128 : (b + 1) * 128]
            total = total + part * part
        mean = jnp.sum(total, axis=-1, keepdims=True) * (1.0 / MODEL_WIDTH)
        r = jnp.broadcast_to(lax.rsqrt(mean + EPSILON), (16, 128))
        for b in range(MODEL_WIDTH // 128):
            cols = slice(b * 128, (b + 1) * 128)
            normed = line[rows, cols] * r * g_ref[:, cols]
            out_ref[rows, cols] = (tok_ref[rows, cols].astype(F32) + normed).astype(BF16)


def finish(pos, own, nxt, last, far, own_tokens, gain):
    return pl.pallas_call(
        finish_kernel,
        in_specs=[SMEM] + [VMEM] * 6,
        out_specs=VMEM,
        out_shape=jax.ShapeDtypeStruct((64, MODEL_WIDTH), BF16),
        scratch_shapes=[pltpu.VMEM((64, MODEL_WIDTH), F32)],
        compiler_params=pltpu.CompilerParams(vmem_limit_bytes=16 << 20),
        cost_estimate=SMALL,
        name="finish",
    )(pos, own, nxt, last, far, own_tokens, gain.reshape(1, -1))


def shift_by(array, axis, steps):
    return lax.ppermute(array, axis, [(i, (i + steps) % 4) for i in range(4)])


def from_line(pieces):
    return [shift_by(piece, "z", by) for piece, by in zip(pieces, (1, 3, 2), strict=True)]


def per_device(
    tokens, pre_gain, w_query, key_weight, value_weight, query_gain, key_gain,
    prior_key, prior_value, w_out, post_gain, table,
):
    device = lax.axis_index(("y", "c", "x", "z"))
    pos = lax.dynamic_slice_in_dim(jnp.asarray(places()), device, 1, 0).reshape(-1)
    parts = pick(pos, w_out)
    pos, *parts = lax.optimization_barrier((pos, *parts))
    lines = from_line(parts)
    normed, kv, own_tokens = key_value(
        pos, tokens, pre_gain, key_weight, value_weight, key_gain, table
    )
    got = lax.ppermute(kv, ("y", "c"), [(i, i + 1) for i in range(7)])
    q, own_w = query(pos, normed, w_query, query_gain, table, w_out)
    q, *lines = lax.optimization_barrier((q, *lines))
    swapped = [lax.ppermute(part, "c", [(0, 1), (1, 0)]) for part in lines]
    pos, *swapped = lax.optimization_barrier((pos, *swapped))

    far, *extended = attend(0, 2, pos, q, (kv, got, prior_key, prior_value))
    far_heads = [far, *from_line([far] * 3)]
    pos, _ = lax.optimization_barrier((pos, far))
    (near,) = attend(2, 4, pos, q, extended)
    near_heads = [near, *from_line([near] * 3)]
    *far_heads, _ = lax.optimization_barrier((*far_heads, near))
    last_pos, _ = lax.optimization_barrier((pos, near))
    weights = [own_w, join(last_pos, lines, swapped)]

    half = jax.ShapeDtypeStruct((HALF, QUARTER), BF16)
    full = jax.ShapeDtypeStruct((256, QUARTER), BF16)
    kept_shape = jax.ShapeDtypeStruct((256, QUARTER), F32)
    up, down = multiply(far_kernel, far_heads, weights, [half, half], "far")
    relays = (shift_by(up, "x", 1), shift_by(down, "x", 3))
    pos, *_ = lax.optimization_barrier((pos, near, up))
    (kept,) = attend(6, 2, pos, q, extended, MEDIUM)
    kept_heads = [kept, *from_line([kept] * 3)]
    *near_heads, _ = lax.optimization_barrier((*near_heads, kept))
    up, down = multiply(near_kernel, near_heads, weights, [full, full], "near", LARGE)
    up, down = relay(relays, up, down)
    up, down = shift_by(up, "x", 1), shift_by(down, "x", 3)
    kept = multiply(keep_kernel, kept_heads, weights, kept_shape, "keep")
    own, *others = total_step(pos, kept, up, down)
    return finish(pos, own, *from_line(others), own_tokens, post_gain)


def solution(mesh):
    fine = Mesh(mesh.devices.reshape(4, 2, 4, 4), ("y", "c", "x", "z"))
    seq, tp = ("y", "c"), ("x", "z")
    inner = jax.shard_map(
        per_device,
        mesh=fine,
        in_specs=(
            P(seq, None), P(), P(None, tp), P(None, tp), P(None, tp), P(), P(),
            P(None, tp), P(None, tp), P(tp, None), P(), P(),
        ),
        out_specs=P(seq + tp, None),
        check_vma=False,
    )

    def run(*args):
        return inner(*args, jnp.asarray(rotary_table()))

    return run
```

```python
import functools

import jax
import jax.numpy as jnp
import numpy as np
from jax import lax
from jax.experimental import pallas as pl
from jax.experimental.pallas import tpu as pltpu
from jax.sharding import Mesh
from jax.sharding import PartitionSpec as P

MODEL_WIDTH = 5376
HQ = 32
HEAD = 128
WINDOW_SPAN = 1024
BLOCK_TOKENS = 8192
SHARD = 1024
EPSILON = 1e-06
LOG2E = 1.4426950408889634
SCORE_SCALE = float(MODEL_WIDTH // HQ) ** (-0.5)

F32 = jnp.float32
BF16 = jnp.bfloat16

ROWS = 256
GROUP = 16
HALF = 128
QUARTER = 1408
ROW_AT = 3


ANY = pl.BlockSpec(memory_space=pl.ANY)
VMEM = pl.BlockSpec(memory_space=pltpu.VMEM)
SMEM = pl.BlockSpec(memory_space=pltpu.SMEM)
SMALL = pl.CostEstimate(flops=0, bytes_accessed=0, transcendentals=0)
MEDIUM = pl.CostEstimate(flops=4_000_000_000, bytes_accessed=0, transcendentals=0)
LARGE = pl.CostEstimate(flops=30_000_000_000, bytes_accessed=0, transcendentals=0)


def rotary_table():
    half = HEAD // 2
    exponent = np.arange(half, dtype=np.float32) * np.float32(-2.0 / HEAD)
    frequency = np.power(np.float64(10000.0), exponent.astype(np.float64)).astype(np.float32)
    position = (WINDOW_SPAN + np.arange(BLOCK_TOKENS)).astype(np.float32)
    angle = (position[:, None] * frequency[None, :]).astype(np.float64)
    return np.concatenate([np.cos(angle), np.sin(angle)], axis=1).astype(np.float32)


def places():
    rows = []
    for device in range(128):
        seq, x, z = device // 16, device // 4 % 4, device % 4
        far, up, down = ((x + by) % 4 * 256 for by in (2, 1, 3))
        rows.append(
            [seq, z, seq % 2, far, far + 128, up, up + 128, down, down + 128, x * 256,
             x * 256 + 128, x]
        )
    return np.array(rows, np.int32)


def rotate(u, gain, table):
    swapped = pltpu.roll(table, 64, 1)
    low = lax.broadcasted_iota(jnp.int32, table.shape, 1) < 64
    cosine = jnp.where(low, table, swapped)
    sine = jnp.where(low, -swapped, table)
    mean = jnp.sum(u * u, axis=-1, keepdims=True) * (1.0 / HEAD)
    u = u * lax.rsqrt(mean + EPSILON) * gain
    return (u * cosine + pltpu.roll(u, 64, 1) * sine).astype(BF16)


def key_value_kernel(
    pos_ref, tok_ref, g_ref, wk_ref, wv_ref, gain_ref, tab_ref,
    normed, kv_ref, own_ref, w_all, g_all, sems,
):
    step = pl.program_id(0)
    copies = [
        pltpu.make_async_copy(wk_ref, w_all.at[:, 0:128], sems.at[0]),
        pltpu.make_async_copy(wv_ref, w_all.at[:, 128:256], sems.at[1]),
    ]
    blocks = MODEL_WIDTH // 128

    def norm_group(i, carry):
        at = i * GROUP if isinstance(i, int) else pl.multiple_of(i * GROUP, GROUP)
        rows = pl.ds(at, GROUP)
        parts = [jnp.zeros((GROUP, 128), F32) for _ in range(2)]
        for b in range(blocks):
            v = tok_ref[rows, b * 128 : (b + 1) * 128].astype(F32)
            parts[b % 2] = parts[b % 2] + v * v
        mean = jnp.sum(parts[0] + parts[1], axis=-1, keepdims=True) * (1.0 / MODEL_WIDTH)
        r = jnp.broadcast_to(lax.rsqrt(mean + EPSILON), (GROUP, 128))
        for b in range(blocks):
            cols = slice(b * 128, (b + 1) * 128)
            v = tok_ref[rows, cols].astype(F32)
            normed[rows, cols] = (v * r * g_all[:, cols]).astype(BF16)
        return carry

    def multiply_and_rotate():
        raw = jnp.dot(normed[...], w_all[...], preferred_element_type=F32)
        kv_ref[:, 0:128] = rotate(raw[:, 0:128], gain_ref[...], tab_ref[...])
        kv_ref[:, 128:256] = raw[:, 128:256].astype(BF16)

    @pl.when(step == 0)
    def _():
        for copy in copies:
            copy.start()
        g_all[...] = jnp.broadcast_to(g_ref[...], g_all.shape)
        lax.fori_loop(0, ROWS // GROUP, norm_group, 0, unroll=4)
        for copy in copies:
            copy.wait()
        multiply_and_rotate()

    @pl.when(step != 0)
    def _():
        for i in range(ROWS // GROUP):
            norm_group(i, 0)
        multiply_and_rotate()

    @pl.when(step == pos_ref[ROW_AT + 8])
    def _():
        own_ref[...] = tok_ref[pl.ds(pl.multiple_of(pos_ref[1] * 64, 64), 64), :]


def in_hbm(*arrays):
    return [pltpu.with_memory_space_constraint(array, pltpu.HBM) for array in arrays]


def whole(shape):
    return pl.BlockSpec(shape, lambda i, s: (0, 0))


def row_tile(width):
    return pl.BlockSpec((ROWS, width), lambda i, s: (i, 0))


TABLE_TILE = pl.BlockSpec((ROWS, 128), lambda i, s: (s[0] * (SHARD // ROWS) + i, 0))


def key_value(pos, tokens, pre_gain, wk, wv, gain, table):
    tokens, wk, wv, table = in_hbm(tokens, wk, wv, table)
    return pl.pallas_call(
        key_value_kernel,
        grid_spec=pltpu.PrefetchScalarGridSpec(
            num_scalar_prefetch=1,
            grid=(SHARD // ROWS,),
            in_specs=[
                row_tile(MODEL_WIDTH), whole((1, MODEL_WIDTH)), ANY, ANY,
                whole((1, 128)), TABLE_TILE,
            ],
            out_specs=[row_tile(MODEL_WIDTH), row_tile(256), whole((64, MODEL_WIDTH))],
            scratch_shapes=[
                pltpu.VMEM((MODEL_WIDTH, 256), BF16),
                pltpu.VMEM((GROUP, MODEL_WIDTH), F32),
                pltpu.SemaphoreType.DMA((2,)),
            ],
        ),
        out_shape=[
            jax.ShapeDtypeStruct((SHARD, MODEL_WIDTH), BF16),
            jax.ShapeDtypeStruct((SHARD, 256), BF16),
            jax.ShapeDtypeStruct((64, MODEL_WIDTH), BF16),
        ],
        compiler_params=pltpu.CompilerParams(vmem_limit_bytes=28 << 20),
        cost_estimate=pl.CostEstimate(
            flops=8 * SHARD * MODEL_WIDTH * 256, bytes_accessed=26 << 20, transcendentals=0
        ),
        name="key_value",
    )(pos, tokens, pre_gain.reshape(1, -1), wk, wv, gain.reshape(1, -1), table)


def table_copy(pos_ref, tab_ref, table, sem):
    rows = pl.ds(pl.multiple_of(pos_ref[0] * SHARD, SHARD), SHARD)
    return pltpu.make_async_copy(tab_ref.at[rows], table, sem)


def query_kernel(
    pos_ref, normed_ref, w_ref, gain_ref, tab_ref, w_out_ref, q_ref, own_w_ref, table, sems
):
    copy = table_copy(pos_ref, tab_ref, table, sems.at[0])
    copy.start()
    cols = pl.ds(quarter_start(pos_ref[1]), QUARTER)
    fetch = pltpu.make_async_copy(w_out_ref.at[:, cols], own_w_ref, sems.at[1])
    fetch.start()
    copy.wait()
    for i in range(SHARD // ROWS):
        rows = slice(i * ROWS, (i + 1) * ROWS)
        raw = jnp.dot(normed_ref[rows, :], w_ref[...], preferred_element_type=F32)
        q_ref[rows, 0:128] = rotate(raw[:, 0:128], gain_ref[...], table[rows, :])
        q_ref[rows, 128:256] = rotate(raw[:, 128:256], gain_ref[...], table[rows, :])
    fetch.wait()


def query(pos, normed, wq, gain, table, w_out):
    table, w_out = in_hbm(table, w_out)
    return pl.pallas_call(
        query_kernel,
        in_specs=[SMEM, VMEM, VMEM, VMEM, ANY, ANY],
        out_specs=[VMEM] * 2,
        out_shape=[
            jax.ShapeDtypeStruct((SHARD, 256), BF16),
            jax.ShapeDtypeStruct((256, QUARTER), BF16),
        ],
        scratch_shapes=[pltpu.VMEM((SHARD, 128), F32), pltpu.SemaphoreType.DMA((2,))],
        compiler_params=pltpu.CompilerParams(vmem_limit_bytes=24 << 20),
        cost_estimate=SMALL,
        name="query",
    )(pos, normed, wq, gain.reshape(1, -1), table, w_out)


def first_attend_kernel(
    first_part, pos_ref, q_ref, kv_ref, got_ref, pk_ref, pv_ref, out_ref, keys, values
):
    @pl.when(pos_ref[0] == 0)
    def _():
        keys[0:SHARD] = pk_ref[...]
        values[0:SHARD, 0:128] = pv_ref[...]

    @pl.when(pos_ref[0] != 0)
    def _():
        keys[0:SHARD] = got_ref[:, 0:128]
        values[0:SHARD, 0:128] = got_ref[:, 128:256]

    keys[SHARD:] = kv_ref[:, 0:128]
    values[SHARD:, 0:128] = kv_ref[:, 128:256]
    values[:, 128:256] = jnp.ones((2 * SHARD, 128), BF16)
    attend_kernel(first_part, pos_ref, q_ref, keys, values, out_ref)


def attend_kernel(first_part, pos_ref, q_ref, keys, values, out_ref):
    span = HALF + WINDOW_SPAN
    row = lax.broadcasted_iota(jnp.int32, (2 * HALF, HALF), 0) % HALF
    col = lax.broadcasted_iota(jnp.int32, (2 * HALF, HALF), 1)
    lowest = jnp.float32(-jnp.inf)
    for part in range(out_ref.shape[0] // HALF):
        first = pl.multiple_of(pos_ref[ROW_AT + first_part + part], HALF)
        q = q_ref[pl.ds(first, HALF), :]
        q = jnp.concatenate([q[:, 0:128], q[:, 128:256]], axis=0)
        k = keys[pl.ds(first, span), :]
        scores = lax.dot_general(q, k, (((1,), (1,)), ((), ())), preferred_element_type=F32)
        scores = jnp.concatenate(
            [
                jnp.where(col > row, scores[:, 0:HALF], lowest),
                scores[:, HALF:WINDOW_SPAN],
                jnp.where(col <= row, scores[:, WINDOW_SPAN:], lowest),
            ],
            axis=1,
        )
        top = jnp.max(scores, axis=-1, keepdims=True)
        weights = jnp.exp2((scores - top) * (SCORE_SCALE * LOG2E)).astype(BF16)
        mixed = jnp.dot(weights, values[pl.ds(first, span), :], preferred_element_type=F32)
        mixed = (mixed[:, 0:128] / mixed[:, 128:256]).astype(BF16)
        out_ref[part * HALF : (part + 1) * HALF, 0:128] = mixed[0:HALF]
        out_ref[part * HALF : (part + 1) * HALF, 128:256] = mixed[HALF:]


def attend(first_part, parts, pos, q, sources, cost=SMALL):
    out_shape = [jax.ShapeDtypeStruct((parts * HALF, 256), BF16)]
    kernel = attend_kernel
    if len(sources) > 2:
        kernel = first_attend_kernel
        out_shape += [
            jax.ShapeDtypeStruct((2 * SHARD, 128), BF16),
            jax.ShapeDtypeStruct((2 * SHARD, 256), BF16),
        ]
    return pl.pallas_call(
        functools.partial(kernel, first_part),
        in_specs=[SMEM] + [VMEM] * (1 + len(sources)),
        out_specs=[VMEM] * len(out_shape),
        out_shape=out_shape,
        compiler_params=pltpu.CompilerParams(vmem_limit_bytes=32 << 20),
        cost_estimate=cost,
        name="attend",
    )(pos, q, *sources)


def quarter_start(number):
    return pl.multiple_of((number * 21 // 2) * 128, 128)


def pick_kernel(pos_ref, w_ref, next_ref, last_ref, far_ref, sems):
    z = pos_ref[1]
    rows = pl.ds(pl.multiple_of(pos_ref[2] * 128, 128), 128)
    copies = []
    for i, (shift, ref) in enumerate(((1, next_ref), (3, last_ref), (2, far_ref))):
        cols = pl.ds(quarter_start((z + shift) % 4), QUARTER)
        copies.append(pltpu.make_async_copy(w_ref.at[rows, cols], ref, sems.at[i]))
    for copy in copies:
        copy.start()
    for copy in copies:
        copy.wait()


def pick(pos, w_out):
    part = jax.ShapeDtypeStruct((128, QUARTER), BF16)
    return pl.pallas_call(
        pick_kernel,
        in_specs=[SMEM, ANY],
        out_specs=[VMEM] * 3,
        out_shape=[part, part, part],
        scratch_shapes=[pltpu.SemaphoreType.DMA((3,))],
        compiler_params=pltpu.CompilerParams(vmem_limit_bytes=16 << 20),
        cost_estimate=SMALL,
        name="pick",
    )(pos, *in_hbm(w_out))


def join_kernel(pos_ref, *refs):
    c, out_ref = pos_ref[2], refs[6]
    for i in range(3):
        out_ref[i, pl.ds(pl.multiple_of(c * 128, 128), 128)] = refs[i][...]
        out_ref[i, pl.ds(pl.multiple_of((1 - c) * 128, 128), 128)] = refs[3 + i][...]


def join(pos, lines, swapped):
    return pl.pallas_call(
        join_kernel,
        in_specs=[SMEM] + [VMEM] * 6,
        out_specs=VMEM,
        out_shape=jax.ShapeDtypeStruct((3, 256, QUARTER), BF16),
        compiler_params=pltpu.CompilerParams(vmem_limit_bytes=16 << 20),
        cost_estimate=SMALL,
        name="join",
    )(pos, *lines, *swapped)


def product(a_refs, own_ref, line_ref, rows=slice(None)):
    out = jnp.dot(a_refs[0][rows, :], own_ref[...], preferred_element_type=F32)
    for i in range(3):
        out = out + jnp.dot(a_refs[1 + i][rows, :], line_ref[i], preferred_element_type=F32)
    return out


def far_kernel(*refs):
    out = product(refs[0:4], refs[4], refs[5])
    refs[6][...] = out[0:HALF].astype(BF16)
    refs[7][...] = out[HALF:].astype(BF16)


def near_kernel(*refs):
    refs[6][...] = product(refs[0:4], refs[4], refs[5], slice(0, 256)).astype(BF16)
    refs[7][...] = product(refs[0:4], refs[4], refs[5], slice(256, 512)).astype(BF16)


def relay_kernel(relay_up, relay_down, up_in, down_in, up_ref, down_ref):
    up_ref[0:HALF] = (up_in[0:HALF].astype(F32) + relay_up[...].astype(F32)).astype(BF16)
    up_ref[HALF:] = up_in[HALF:]
    down_ref[0:HALF] = down_in[0:HALF]
    down_ref[HALF:] = (down_in[HALF:].astype(F32) + relay_down[...].astype(F32)).astype(BF16)


def relay(relays, up, down):
    return pl.pallas_call(
        relay_kernel,
        in_specs=[VMEM] * 4,
        out_specs=[VMEM] * 2,
        out_shape=[jax.ShapeDtypeStruct((256, QUARTER), BF16)] * 2,
        input_output_aliases={2: 0, 3: 1},
        compiler_params=pltpu.CompilerParams(vmem_limit_bytes=16 << 20),
        cost_estimate=SMALL,
        name="relay",
    )(*relays, up, down)


def keep_kernel(*refs):
    refs[6][...] = product(refs[0:4], refs[4], refs[5])


def multiply(kernel, pieces, weights, out_shape, name, cost=SMALL):
    return pl.pallas_call(
        kernel,
        in_specs=[VMEM] * 6,
        out_specs=jax.tree.map(lambda _: VMEM, out_shape),
        out_shape=out_shape,
        compiler_params=pltpu.CompilerParams(vmem_limit_bytes=24 << 20),
        cost_estimate=cost,
        name=name,
    )(*pieces, *weights)


def total_kernel(pos_ref, kept_ref, up_ref, down_ref, own_ref, next_ref, last_ref, far_ref):
    z = pos_ref[1]

    def rows(shift):
        at = pl.ds(pl.multiple_of(((z + shift) % 4) * 64, 64), 64)
        return kept_ref[at, :] + up_ref[at, :].astype(F32) + down_ref[at, :].astype(F32)

    next_ref[...] = rows(1).astype(BF16)
    last_ref[...] = rows(3).astype(BF16)
    far_ref[...] = rows(2).astype(BF16)
    own_ref[...] = rows(0)


def total_step(pos, kept, up, down):
    part = jax.ShapeDtypeStruct((64, QUARTER), BF16)
    return pl.pallas_call(
        total_kernel,
        in_specs=[SMEM] + [VMEM] * 3,
        out_specs=[VMEM] * 4,
        out_shape=[jax.ShapeDtypeStruct((64, QUARTER), F32), part, part, part],
        compiler_params=pltpu.CompilerParams(vmem_limit_bytes=32 << 20),
        cost_estimate=SMALL,
        name="total_step",
    )(pos, kept, up, down)


def finish_kernel(pos_ref, own_ref, next_ref, last_ref, far_ref, tok_ref, g_ref, out_ref, line):
    z = pos_ref[1]
    for shift, ref in ((0, own_ref), (3, next_ref), (1, last_ref), (2, far_ref)):
        line[:, pl.ds(quarter_start((z + shift) % 4), QUARTER)] = ref[...].astype(F32)
    for i in range(4):
        rows = slice(i * 16, (i + 1) * 16)
        total = jnp.zeros((16, 128), F32)
        for b in range(MODEL_WIDTH // 128):
            part = line[rows, b * 128 : (b + 1) * 128]
            total = total + part * part
        mean = jnp.sum(total, axis=-1, keepdims=True) * (1.0 / MODEL_WIDTH)
        r = jnp.broadcast_to(lax.rsqrt(mean + EPSILON), (16, 128))
        for b in range(MODEL_WIDTH // 128):
            cols = slice(b * 128, (b + 1) * 128)
            normed = line[rows, cols] * r * g_ref[:, cols]
            out_ref[rows, cols] = (tok_ref[rows, cols].astype(F32) + normed).astype(BF16)


def finish(pos, own, nxt, last, far, own_tokens, gain):
    return pl.pallas_call(
        finish_kernel,
        in_specs=[SMEM] + [VMEM] * 6,
        out_specs=VMEM,
        out_shape=jax.ShapeDtypeStruct((64, MODEL_WIDTH), BF16),
        scratch_shapes=[pltpu.VMEM((64, MODEL_WIDTH), F32)],
        compiler_params=pltpu.CompilerParams(vmem_limit_bytes=16 << 20),
        cost_estimate=SMALL,
        name="finish",
    )(pos, own, nxt, last, far, own_tokens, gain.reshape(1, -1))


def shift_by(array, axis, steps):
    return lax.ppermute(array, axis, [(i, (i + steps) % 4) for i in range(4)])


def from_line(pieces):
    return [shift_by(piece, "z", by) for piece, by in zip(pieces, (1, 3, 2), strict=True)]


def per_device(
    tokens, pre_gain, w_query, key_weight, value_weight, query_gain, key_gain,
    prior_key, prior_value, w_out, post_gain, table,
):
    device = lax.axis_index(("y", "c", "x", "z"))
    pos = lax.dynamic_slice_in_dim(jnp.asarray(places()), device, 1, 0).reshape(-1)
    parts = pick(pos, w_out)
    pos, *parts = lax.optimization_barrier((pos, *parts))
    lines = from_line(parts)
    normed, kv, own_tokens = key_value(
        pos, tokens, pre_gain, key_weight, value_weight, key_gain, table
    )
    got = lax.ppermute(kv, ("y", "c"), [(i, i + 1) for i in range(7)])
    q, own_w = query(pos, normed, w_query, query_gain, table, w_out)
    q, *lines = lax.optimization_barrier((q, *lines))
    swapped = [lax.ppermute(part, "c", [(0, 1), (1, 0)]) for part in lines]
    pos, *swapped = lax.optimization_barrier((pos, *swapped))

    far, *extended = attend(0, 2, pos, q, (kv, got, prior_key, prior_value))
    far_heads = [far, *from_line([far] * 3)]
    pos, _ = lax.optimization_barrier((pos, far))
    (near,) = attend(2, 4, pos, q, extended)
    near_heads = [near, *from_line([near] * 3)]
    *far_heads, _ = lax.optimization_barrier((*far_heads, near))
    last_pos, _ = lax.optimization_barrier((pos, near))
    weights = [own_w, join(last_pos, lines, swapped)]

    half = jax.ShapeDtypeStruct((HALF, QUARTER), BF16)
    full = jax.ShapeDtypeStruct((256, QUARTER), BF16)
    kept_shape = jax.ShapeDtypeStruct((256, QUARTER), F32)
    up, down = multiply(far_kernel, far_heads, weights, [half, half], "far")
    relays = (shift_by(up, "x", 1), shift_by(down, "x", 3))
    pos, *_ = lax.optimization_barrier((pos, near, up))
    (kept,) = attend(6, 2, pos, q, extended, MEDIUM)
    kept_heads = [kept, *from_line([kept] * 3)]
    *near_heads, _ = lax.optimization_barrier((*near_heads, kept))
    up, down = multiply(near_kernel, near_heads, weights, [full, full], "near", LARGE)
    up, down = relay(relays, up, down)
    up, down = shift_by(up, "x", 1), shift_by(down, "x", 3)
    kept = multiply(keep_kernel, kept_heads, weights, kept_shape, "keep")
    own, *others = total_step(pos, kept, up, down)
    return finish(pos, own, *from_line(others), own_tokens, post_gain)


def solution(mesh):
    fine = Mesh(mesh.devices.reshape(4, 2, 4, 4), ("y", "c", "x", "z"))
    seq, tp = ("y", "c"), ("x", "z")
    inner = jax.shard_map(
        per_device,
        mesh=fine,
        in_specs=(
            P(seq, None), P(), P(None, tp), P(None, tp), P(None, tp), P(), P(),
            P(None, tp), P(None, tp), P(tp, None), P(), P(),
        ),
        out_specs=P(seq + tp, None),
        check_vma=False,
    )

    def run(*args):
        return inner(*args, jnp.asarray(rotary_table()))

    return run
```
